32 devices in a mesh: dp: 8 (over z, y), mp: 4 (over x, core).
Axes of the slice: x: 2, y: 2, z: 4, core: 2. Of those that a mesh axis runs over, the one named last changes fastest.
Arguments:
- tokens: bfloat16 [4096, 2560], P(('dp', 'mp')), may hold values from -6 to 6
- upstream: bfloat16 [4096, 2560], P(('dp', 'mp')), may hold values from -6 to 6
- offsets: int32 [4096], P('dp'), may hold values from 0 to 799, as said below
- query_weight: float32 [2560, 2560], P('dp', 'mp'), may hold values from -0.125 to 0.125
- keyval_weight: float32 [2, 2560, 640], P(None, 'dp', 'mp'), may hold values from -0.125 to 0.125
- output_weight: float32 [2560, 2560], P('dp', 'mp'), may hold values from -0.625 to 0.625
- gateup_weight: float32 [2, 2560, 7168], P(None, 'dp', 'mp'), may hold values from -0.125 to 0.125
- down_weight: float32 [2560, 7168], P('dp', 'mp'), may hold values from -0.0625 to 0.0625
- norm_gains: float32 [2, 2560], P(None, 'dp')
- first_query: float32 [2560, 2560], P('dp', 'mp'), may hold values from -0.6 to 0.6
- first_keyval: float32 [2, 2560, 640], P(None, 'dp', 'mp'), may hold values from -0.6 to 0.6
- first_output: float32 [2560, 2560], P('dp', 'mp'), may hold values from -0.6 to 0.6
- first_gateup: float32 [2, 2560, 7168], P(None, 'dp', 'mp'), may hold values from -0.6 to 0.6
- first_down: float32 [2560, 7168], P('dp', 'mp'), may hold values from -0.6 to 0.6
- first_gains: float32 [2, 2560], P(None, 'dp'), may hold values from -0.6 to 0.6
- second_query: float32 [2560, 2560], P('dp', 'mp'), may hold values from 0.02 to 0.2
- second_keyval: float32 [2, 2560, 640], P(None, 'dp', 'mp'), may hold values from 0.02 to 0.2
- second_output: float32 [2560, 2560], P('dp', 'mp'), may hold values from 0.02 to 0.2
- second_gateup: float32 [2, 2560, 7168], P(None, 'dp', 'mp'), may hold values from 0.02 to 0.2
- second_down: float32 [2560, 7168], P('dp', 'mp'), may hold values from 0.02 to 0.2
- second_gains: float32 [2, 2560], P(None, 'dp'), may hold values from 0.02 to 0.2
Outputs:
- block_out: bfloat16 [4096, 2560], P(('dp', 'mp'))
- grad_tokens: float32 [4096, 2560], P(('dp', 'mp'))
- grad_norm: float32 [], replicated
- grad_query: float32 [2560, 2560], P('dp', 'mp')
- grad_keyval: float32 [2, 2560, 640], P(None, 'dp', 'mp')
- grad_output: float32 [2560, 2560], P('dp', 'mp')
- grad_gateup: float32 [2, 2560, 7168], P(None, 'dp', 'mp')
- grad_down: float32 [2560, 7168], P('dp', 'mp')
- grad_gains: float32 [2, 2560], P(None, 'dp')
- next_first_query: float32 [2560, 2560], P('dp', 'mp')
- next_first_keyval: float32 [2, 2560, 640], P(None, 'dp', 'mp')
- next_first_output: float32 [2560, 2560], P('dp', 'mp')
- next_first_gateup: float32 [2, 2560, 7168], P(None, 'dp', 'mp')
- next_first_down: float32 [2560, 7168], P('dp', 'mp')
- next_first_gains: float32 [2, 2560], P(None, 'dp')
- next_second_query: float32 [2560, 2560], P('dp', 'mp')
- next_second_keyval: float32 [2, 2560, 640], P(None, 'dp', 'mp')
- next_second_output: float32 [2560, 2560], P('dp', 'mp')
- next_second_gateup: float32 [2, 2560, 7168], P(None, 'dp', 'mp')
- next_second_down: float32 [2560, 7168], P('dp', 'mp')
- next_second_gains: float32 [2, 2560], P(None, 'dp')
- step_query: float32 [2560, 2560], P('dp', 'mp')
- step_keyval: float32 [2, 2560, 640], P(None, 'dp', 'mp')
- step_output: float32 [2560, 2560], P('dp', 'mp')
- step_gateup: float32 [2, 2560, 7168], P(None, 'dp', 'mp')
- step_down: float32 [2560, 7168], P('dp', 'mp')
- step_gains: float32 [2, 2560], P(None, 'dp')
The draws below stay inside these ranges and needn't reach their ends.
Inputs may be any that keep to these rules, and one draw needn't show every extreme that they name: `offsets`: the distance of each token from the first token of its document; documents are runs of consecutive tokens of the stream, so each offset is 0 or one more than the previous token's, and the first token's is 0; a document has 1 to 800 tokens, and some document has exactly 800.
All inputs are finite; a program needn't handle non-finite values.
Results may differ from the reference program's by a relative error of at most 0.025.
Values may be sent and summed in bfloat16 or wider, within the bound.
No kernel may reach another device: no remote copies, remote signals or barrier semaphores. Data moves between devices by JAX's collectives and lax.ppermute only.
A program may use at most 512 MiB of HBM per device.

```python
import math
import jax
import jax.numpy as jnp
from jax import lax

MODEL_WIDTH = 2560
QUERY_HEAD_COUNT = 32
KEY_VALUE_HEADS = 8
HEAD_SIZE = 80
HIDDEN_UNITS = 7168
TOK_DEV = 512
DOC_MAX = 800
DOC_MIN = 60
STEP = 10
QW = 2560
KW = 640
TOKENS = 4096


def draw_offsets(key, part):
    devices = TOKENS // TOK_DEV
    reach = min((DOC_MAX + TOK_DEV - 2) // TOK_DEV, devices - 1)
    inner = (reach - 1) * TOK_DEV
    rest = DOC_MAX - inner
    before = rest - rest // 2
    picks = []
    for device in [0, devices // 2 - reach, devices // 2, devices - 1 - reach]:
        if device >= 0 and device + reach <= devices - 1:
            if len(picks) == 0 or device >= picks[-1] + reach:
                picks.append(device)
    anchors = [(device + 1) * TOK_DEV - before for device in picks]
    count = TOKENS // DOC_MIN + 1
    lengths = jax.random.randint(jax.random.fold_in(key, 11), (count,), DOC_MIN, DOC_MAX + 1).astype(jnp.int32)
    random_starts = jnp.cumsum(lengths) - lengths
    places = jnp.arange(TOKENS).astype(jnp.int32)
    marks = jnp.zeros((TOKENS,), jnp.int32).at[random_starts].set(1, mode='drop')
    for anchor in anchors:
        inside = (places > anchor) & (places < anchor + DOC_MAX)
        marks = jnp.where(inside, 0, marks)
        marks = jnp.where((places == anchor) | (places == anchor + DOC_MAX), 1, marks)
    marks = jnp.where(places == 0, 1, marks)
    latest = lax.cummax(jnp.where(marks == 1, places, 0), axis=0)
    return (places - latest).astype(jnp.int32)


def draw_norm_gains(key, part):
    columns = jnp.arange(MODEL_WIDTH).astype(jnp.float32) / MODEL_WIDTH
    ramp = 0.3 + 1.2 * columns
    noise = jnp.clip(0.05 * jax.random.normal(key, (2, MODEL_WIDTH), jnp.float32), -0.15, 0.15)
    return ramp[None, :] * (1.0 + noise)


def spiked(values, key, source, target, shards_of, factor):
    def block_of(position):
        return (jnp.arange(values.shape[position]) // (values.shape[position] // shards_of)).reshape((-1,) + (1,) * (values.ndim - 1 - position))

    one_side = jax.random.permutation(key, shards_of)[block_of(target)]
    second = (block_of(target) + shards_of // 2) % shards_of
    return jnp.where((block_of(source) == one_side) | (block_of(source) == second), factor * values, values)


def block_levels(rng, shape, shards, least, largest):
    loudness, own = 1.0, jax.random.fold_in(rng, 6)
    for position, shards_of in shards:
        heights = jnp.exp(jax.random.uniform(jax.random.fold_in(own, position), (shards_of,), jnp.float32, least / len(shards), largest / len(shards)))
        loudness = loudness * jnp.repeat(heights, shape[position] // shards_of).reshape([-1 if axis == position else 1 for axis in range(len(shape))])
    return loudness


def centred(own_key, dims, deviation, most, split=(), held_as=jnp.bfloat16):
    array = jax.random.normal(own_key, dims, jnp.float32) * deviation
    if len(split) > 0:
        array = block_levels(own_key, dims, split, -0.22, 0.18) * array
    return jnp.clip(array, min=-most, max=most).astype(held_as)


def heavy_noise(key, dims, spread, most, cuts, heavy, kind=jnp.bfloat16):
    entries = spread * jax.random.normal(key, dims, jnp.float32)
    if cuts:
        entries = entries * block_levels(key, dims, cuts, -0.22, 0.18)
    return jnp.clip(spiked(entries, jax.random.fold_in(key, 3), *heavy), -most, most).astype(kind)


def setup_inputs(seed: int = 0) -> dict:
    keys = jax.random.split(jax.random.key(seed), 22)
    return {
        "tokens": centred(keys[0], (TOKENS, MODEL_WIDTH), 1.0, 6.0, ((0, 32),)),
        "upstream": heavy_noise(keys[1], (TOKENS, MODEL_WIDTH), 1.0, 6.0, ((0, 32),), (0, 1, 32, 2.75)),
        "offsets": draw_offsets(jax.random.fold_in(keys[21], 71), 0),
        "query_weight": centred(keys[3], (MODEL_WIDTH, QW), MODEL_WIDTH ** -0.5, 0.125, ((0, 8), (1, 4)), jnp.float32),
        "keyval_weight": centred(keys[4], (2, MODEL_WIDTH, KW), MODEL_WIDTH ** -0.5, 0.125, ((1, 8), (2, 4)), jnp.float32),
        "output_weight": centred(keys[5], (MODEL_WIDTH, QW), (QW // 32) ** -0.5, 0.625, ((0, 8), (1, 4)), jnp.float32),
        "gateup_weight": centred(keys[6], (2, MODEL_WIDTH, HIDDEN_UNITS), MODEL_WIDTH ** -0.5, 0.125, ((1, 8), (2, 4)), jnp.float32),
        "down_weight": centred(keys[7], (MODEL_WIDTH, HIDDEN_UNITS), HIDDEN_UNITS ** -0.5, 0.0625, ((0, 8), (1, 4)), jnp.float32),
        "norm_gains": draw_norm_gains(jax.random.fold_in(keys[21], 71), 0),
        "first_query": centred(keys[9], (MODEL_WIDTH, QW), 0.1, 0.6, ((0, 8), (1, 4)), jnp.float32),
        "first_keyval": centred(keys[10], (2, MODEL_WIDTH, KW), 0.1, 0.6, ((1, 8), (2, 4)), jnp.float32),
        "first_output": centred(keys[11], (MODEL_WIDTH, QW), 0.1, 0.6, ((0, 8), (1, 4)), jnp.float32),
        "first_gateup": centred(keys[12], (2, MODEL_WIDTH, HIDDEN_UNITS), 0.1, 0.6, ((1, 8), (2, 4)), jnp.float32),
        "first_down": centred(keys[13], (MODEL_WIDTH, HIDDEN_UNITS), 0.1, 0.6, ((0, 8), (1, 4)), jnp.float32),
        "first_gains": centred(keys[14], (2, MODEL_WIDTH), 0.1, 0.6, ((1, 8),), jnp.float32),
        "second_query": jnp.clip(jnp.exp(math.log(0.2) - 2.3025851 * jax.random.uniform(keys[15], (MODEL_WIDTH, QW), jnp.float32) ** block_levels(keys[15], (MODEL_WIDTH, QW), ((0, 8), (1, 4)), -0.2, 0.2)), 0.02, 0.2),
        "second_keyval": jnp.clip(jnp.exp(math.log(0.2) - 2.3025851 * jax.random.uniform(keys[16], (2, MODEL_WIDTH, KW), jnp.float32) ** block_levels(keys[16], (2, MODEL_WIDTH, KW), ((1, 8), (2, 4)), -0.2, 0.2)), 0.02, 0.2),
        "second_output": jnp.clip(jnp.exp(math.log(0.2) - 2.3025851 * jax.random.uniform(keys[17], (MODEL_WIDTH, QW), jnp.float32) ** block_levels(keys[17], (MODEL_WIDTH, QW), ((0, 8), (1, 4)), -0.2, 0.2)), 0.02, 0.2),
        "second_gateup": jnp.clip(jnp.exp(math.log(0.2) - 2.3025851 * jax.random.uniform(keys[18], (2, MODEL_WIDTH, HIDDEN_UNITS), jnp.float32) ** block_levels(keys[18], (2, MODEL_WIDTH, HIDDEN_UNITS), ((1, 8), (2, 4)), -0.2, 0.2)), 0.02, 0.2),
        "second_down": jnp.clip(jnp.exp(math.log(0.2) - 2.3025851 * jax.random.uniform(keys[19], (MODEL_WIDTH, HIDDEN_UNITS), jnp.float32) ** block_levels(keys[19], (MODEL_WIDTH, HIDDEN_UNITS), ((0, 8), (1, 4)), -0.2, 0.2)), 0.02, 0.2),
        "second_gains": jnp.clip(jnp.exp(math.log(0.2) - 2.3025851 * jax.random.uniform(keys[20], (2, MODEL_WIDTH), jnp.float32) ** block_levels(keys[20], (2, MODEL_WIDTH), ((1, 8),), -0.2, 0.2)), 0.02, 0.2),
    }


eps_norm = 1e-05
rope_base = 1000000.0
beta_first = 0.9
beta_second = 0.95
learn_rate = 0.02
weight_decay = 0.1
adam_eps = 1e-08
masked_score = -1e+30

@jax.custom_vjp
def low(v):
    return lax.optimization_barrier(v.astype(jnp.bfloat16)).astype(jnp.float32)

@jax.custom_vjp
def low_back(v):
    return v

def low_keep(v):
    return (low(v), None)

def low_pass(kept, grad):
    return (grad,)

def back_keep(v):
    return (v, None)

def back_low(kept, grad):
    return (low(grad),)
low.defvjp(low_keep, low_pass)
low_back.defvjp(back_keep, back_low)

def matrix_product(left_side, right_side):
    return jnp.dot(left_side, right_side, precision=lax.Precision.HIGHEST)

def rope_tables(positions):
    half = HEAD_SIZE // 2
    freqs = rope_base ** (-(jnp.arange(half).astype(jnp.float32) * 2.0 / HEAD_SIZE))
    angle = positions.astype(jnp.float32)[:, None] * freqs[None, :]
    return (jnp.cos(angle), jnp.sin(angle))

def apply_rotation(value_rows, cosine_table, sine_table):
    half = value_rows.shape[-1] // 2
    first_half = value_rows[..., :half]
    second_half = value_rows[..., half:]
    cos_wide = cosine_table[:, None, :]
    sin_wide = sine_table[:, None, :]
    return jnp.concatenate([first_half * cos_wide - second_half * sin_wide, second_half * cos_wide + first_half * sin_wide], axis=-1)

def rms_norm(value_rows, gain):
    return value_rows * lax.rsqrt(lax.optimization_barrier(jnp.mean(value_rows * value_rows, axis=-1, keepdims=True)) + eps_norm) * gain

def layer(params, inputs, positions):
    query_w, key_value_weight, output_w, gateup_w, down_w, gains = [low(weight) for weight in params]
    total_rows = inputs.shape[0]
    head_group = QUERY_HEAD_COUNT // KEY_VALUE_HEADS
    normalized_rows = low(rms_norm(inputs, gains[0]))
    cosine_table, sine_table = rope_tables(positions)
    query_rows = low(apply_rotation(low_back(matrix_product(normalized_rows, query_w)).reshape(total_rows, QUERY_HEAD_COUNT, HEAD_SIZE), cosine_table, sine_table))
    key_rows = low(apply_rotation(low_back(matrix_product(normalized_rows, key_value_weight[0])).reshape(total_rows, KEY_VALUE_HEADS, HEAD_SIZE), cosine_table, sine_table))
    value_rows = low(low_back(matrix_product(normalized_rows, key_value_weight[1]))).reshape(total_rows, KEY_VALUE_HEADS, HEAD_SIZE)
    token_rows = min(512, total_rows)
    block_list = total_rows // token_rows
    span = (DOC_MAX - 1 + token_rows - 1) // token_rows * token_rows
    reach_rows = span + token_rows
    padding = jnp.zeros((span, KEY_VALUE_HEADS, HEAD_SIZE), key_rows.dtype)
    padded_keys = jnp.concatenate([padding, key_rows], axis=0)
    padded_values = jnp.concatenate([padding, value_rows], axis=0)
    grouped_heads = query_rows.reshape(block_list, token_rows, KEY_VALUE_HEADS, head_group, HEAD_SIZE)
    block_offsets = positions.reshape(block_list, token_rows).astype(jnp.int32)
    starts = (jnp.arange(block_list) * token_rows).astype(jnp.int32)
    scale = HEAD_SIZE ** (-0.5)

    def attend(item):
        block_q, start, block_off = item
        near_keys = lax.dynamic_slice_in_dim(padded_keys, start, reach_rows, 0)
        near_values = lax.dynamic_slice_in_dim(padded_values, start, reach_rows, 0)
        raw = jnp.einsum('tgrd,ngd->tgrn', block_q, near_keys, precision=lax.Precision.HIGHEST)
        scores = low_back(raw * scale)
        key_pos = (start - span + jnp.arange(reach_rows)).astype(jnp.int32)
        query_pos = (start + jnp.arange(token_rows)).astype(jnp.int32)
        allowed = (key_pos[None, :] <= query_pos[:, None]) & (key_pos[None, :] >= (query_pos - block_off)[:, None])
        scores = jnp.where(allowed[:, None, None, :], scores, masked_score)
        weights = low(jax.nn.softmax(scores, axis=-1))
        return jnp.einsum('tgrn,ngd->tgrd', weights, near_values, precision=lax.Precision.HIGHEST)
    attended = lax.map(jax.checkpoint(attend), (grouped_heads, starts, block_offsets))
    attended = low(low_back(attended.reshape(total_rows, QUERY_HEAD_COUNT * HEAD_SIZE)))
    branch = low_back(matrix_product(attended, output_w.T))
    middle = inputs + branch
    normed_two = low(rms_norm(middle, gains[1]))
    gate = low_back(matrix_product(normed_two, gateup_w[0]))
    upward = low_back(matrix_product(normed_two, gateup_w[1]))
    hidden = low(jax.nn.silu(gate) * upward)
    return middle + low_back(matrix_product(hidden, down_w.T))

def adamw(param, grad, first, second):
    first_new = beta_first * first + (1.0 - beta_first) * grad
    second_new = beta_second * second + (1.0 - beta_second) * grad * grad
    first_hat = first_new / (1.0 - beta_first ** STEP)
    second_hat = second_new / (1.0 - beta_second ** STEP)
    change = -learn_rate * (first_hat / (jnp.sqrt(second_hat) + adam_eps) + weight_decay * param)
    return (first_new, second_new, change)

def reference(tokens, upstream, offsets, query_weight, keyval_weight, output_weight, gateup_weight, down_weight, norm_gains, first_query, first_keyval, first_output, first_gateup, first_down, first_gains, second_query, second_keyval, second_output, second_gateup, second_down, second_gains):
    params = (query_weight, keyval_weight, output_weight, gateup_weight, down_weight, norm_gains)
    firsts = (first_query, first_keyval, first_output, first_gateup, first_down, first_gains)
    seconds = (second_query, second_keyval, second_output, second_gateup, second_down, second_gains)
    inputs = tokens.astype(jnp.float32)
    cotangent = upstream.astype(jnp.float32)
    result, pullback = jax.vjp(lambda weights, value_rows: layer(weights, value_rows, offsets), params, inputs)
    grads, grad_tokens = pullback(cotangent)
    block_out = result.astype(jnp.bfloat16)
    squares = jnp.sum(grads[0] * grads[0])
    for grad in grads[1:]:
        squares = squares + jnp.sum(grad * grad)
    grad_norm = jnp.sqrt(squares)
    clipping_bound = math.sqrt(MODEL_WIDTH * (2 * QUERY_HEAD_COUNT * HEAD_SIZE + 2 * KEY_VALUE_HEADS * HEAD_SIZE + 3 * HIDDEN_UNITS) + 2 * MODEL_WIDTH)
    clip = jnp.minimum(1.0, clipping_bound / (grad_norm + 1e-06))
    states = [adamw(params[index], grads[index] * clip, firsts[index], seconds[index]) for index in range(6)]
    return (block_out, grad_tokens, grad_norm, grads[0], grads[1], grads[2], grads[3], grads[4], grads[5], states[0][0], states[1][0], states[2][0], states[3][0], states[4][0], states[5][0], states[0][1], states[1][1], states[2][1], states[3][1], states[4][1], states[5][1], states[0][2], states[1][2], states[2][2], states[3][2], states[4][2], states[5][2])
```

```python
import functools
import math

import jax
import jax.numpy as jnp
from jax import lax
from jax.experimental import pallas as pl
from jax.experimental.pallas import tpu as pltpu
from jax.sharding import PartitionSpec as P

MODEL_WIDTH = 2560
QUERY_HEAD_COUNT = 32
KEY_VALUE_HEADS = 8
HEAD_SIZE = 80
HIDDEN_UNITS = 7168
STEP = 10

eps_norm = 1e-05
rope_base = 1000000.0
beta_first = 0.9
beta_second = 0.95
learn_rate = 0.02
weight_decay = 0.1
adam_eps = 1e-08
masked_score = -1e30

low_type = jnp.bfloat16
wide_type = jnp.float32

HALF = HEAD_SIZE // 2
GROUP = QUERY_HEAD_COUNT // KEY_VALUE_HEADS
QROWS = GROUP * HEAD_SIZE
BOTH = 2 * HEAD_SIZE
EXP_SCALE = (HEAD_SIZE ** (-0.5)) * math.log2(math.e)
SCALE = HEAD_SIZE ** (-0.5)
AXES = ("dp", "mp")


def hop(block, move):
    dp_size, mp_size = lax.axis_size("dp"), lax.axis_size("mp")
    route = []
    for d in range(dp_size):
        for m in range(mp_size):
            target = move(d, m)
            if target is not None:
                route.append((d * mp_size + m, target[0] * mp_size + target[1]))
    return lax.ppermute(block, AXES, route)


def hop_core(block):
    return hop(block, lambda d, m: (d, m ^ 1))


def hop_x(block):
    return hop(block, lambda d, m: (d, m ^ 2))


def hop_low(block):
    return hop(block, lambda d, m: (d ^ 2, m))


def hop_y(block):
    return hop(block, lambda d, m: (d ^ 1, m))


def hop_ring(block):
    size = lax.axis_size("dp")
    return hop(block, lambda d, m: ((d + 4) % size, m))


def to_next(block, flip):
    size = lax.axis_size("dp")
    return hop(block, lambda d, m: ((d + 4) ^ flip, m) if d + 4 < size else None)


def to_previous(block, flip):
    return hop(block, lambda d, m: ((d - 4) ^ flip, m) if d >= 4 else None)


def bits():
    d = lax.axis_index("dp")
    m = lax.axis_index("mp")
    return d // 4, (d // 2) % 2, d % 2, m // 2, m % 2


def choose(bit, if_zero, if_one):
    return jnp.where(bit == 0, if_zero, if_one)


def ordered(bit, mine, other, axis):
    return choose(
        bit,
        jnp.concatenate([mine, other], axis=axis),
        jnp.concatenate([other, mine], axis=axis),
    )


def gather_rows(own):
    half = own.shape[0] // 2
    across = hop_x(own)
    along = hop_low(own)
    first = hop_x(along[:half])
    second = hop_low(across[half:])
    four = jnp.stack([own, across, along, jnp.concatenate([first, second], axis=0)])
    return jnp.stack([four, hop_core(four)])


def scatter_rows(mine, theirs):
    got = hop_core(theirs.astype(low_type))
    total = mine + got.astype(wide_type)
    half = total.shape[1] // 2
    low_total = total.astype(low_type)
    first = hop_x(low_total[3, :half])
    second = hop_low(low_total[3, half:])
    low_part = jnp.concatenate(
        [(total[2, :half] + first.astype(wide_type)).astype(low_type), low_total[2, half:]], axis=0
    )
    x_part = jnp.concatenate(
        [low_total[1, :half], (total[1, half:] + second.astype(wide_type)).astype(low_type)], axis=0
    )
    return total[0] + hop_x(x_part).astype(wide_type) + hop_low(low_part).astype(wide_type)


def gather_weight(own, other):
    h, l, y, _, _ = bits()
    ring = lax.axis_size("dp") // 4
    pair = ordered(l, own[None], hop_low(other)[None], 0)
    rows, columns = own.shape
    full = jnp.zeros((ring, 2, 2, rows, columns), own.dtype)

    def put(full, block, at_h, at_y):
        return lax.dynamic_update_slice(full, block[None, :, None], (at_h, 0, at_y, 0, 0))

    full = put(full, pair, h, y)
    travel = pair
    held = [(pair, h)]
    for step in range(1, ring):
        travel = hop_ring(travel)
        held.append((travel, (h - step) % ring))
    for index, (block, at_h) in enumerate(held):
        if index > 0:
            full = put(full, block, at_h, y)
        full = put(full, hop_y(block), at_h, 1 - y)
    return full.reshape(ring * 4 * rows, columns)


def reduce_weight(pairs):
    h, l, y, _, _ = bits()
    ring = lax.axis_size("dp") // 4

    def product(index_y, index_h=None):
        parts = []
        for left, right in pairs:
            width, count = left.shape
            blocks = left.reshape(ring, 2, 2, width // (4 * ring), count)
            rows = lax.dynamic_index_in_dim(blocks, index_y, 2, keepdims=False)
            if index_h is not None:
                rows = lax.dynamic_index_in_dim(rows, index_h, 0, keepdims=False)
            lead = rows.shape[:-1]
            out = jnp.dot(
                rows.reshape(-1, count), right, preferred_element_type=wide_type
            )
            parts.append(out.reshape(*lead, right.shape[1]))
        return parts[0] if len(parts) == 1 else jnp.concatenate(parts, axis=-1)

    got = hop_y(product(1 - y).astype(low_type))

    def term(index_h):
        there = lax.dynamic_index_in_dim(got, index_h, 0, keepdims=False)
        return product(y, index_h) + there.astype(wide_type)

    travel = term((h - 1) % ring)
    for step in range(1, ring):
        travel = hop_ring(travel.astype(low_type)).astype(wide_type) + term((h - 1 - step) % ring)
    mine = lax.dynamic_index_in_dim(travel, l, 0, keepdims=False)
    theirs = lax.dynamic_index_in_dim(travel, 1 - l, 0, keepdims=False)
    return mine, hop_low(theirs.astype(low_type)).astype(wide_type)


def sum_all(value):
    ring = lax.axis_size("dp") // 4
    for step in (hop_core, hop_x, hop_low, hop_y):
        value = value + step(value)
    travel = value
    for _ in range(1, ring):
        travel = hop_ring(travel)
        value = value + travel
    return value


def whole_gains(own):
    h, l, y, _, _ = bits()
    ring = lax.axis_size("dp") // 4
    pair = ordered(l, own[:, None], hop_low(own)[:, None], 1)
    quad = ordered(y, pair[:, :, None], hop_y(pair)[:, :, None], 2)
    full = jnp.zeros((own.shape[0], ring, 2, 2, own.shape[1]), own.dtype)
    travel = quad
    for step in range(ring):
        if step > 0:
            travel = hop_ring(travel)
        full = lax.dynamic_update_slice(full, travel[:, None], (0, (h - step) % ring, 0, 0, 0))
    return full.reshape(own.shape[0], -1)


def norm_back(incoming, unit_rows, inverse_root, gain):
    scaled = incoming * gain
    return inverse_root * (
        scaled - unit_rows * jnp.mean(scaled * unit_rows, axis=-1, keepdims=True)
    )


def contract_last(left_side, weight):
    return lax.dot_general(
        left_side, weight, (((1,), (1,)), ((), ())), preferred_element_type=wide_type
    )


def branch_sum(activation, weight):
    rows = activation.shape[0] // 2

    def part(index):
        out = contract_last(activation[index * rows : (index + 1) * rows], weight)
        return out.reshape(4, rows // 4, weight.shape[0])

    return scatter_rows(part(0), part(1))


def first_norm(inputs, gain):
    inverse = lax.rsqrt(jnp.mean(inputs * inputs, axis=-1, keepdims=True) + eps_norm)
    return inputs * inverse, inverse


def project_body(x_ref, g_ref, w_ref, cos_ref, sin_ref, a_ref, q_ref, kv_ref):
    rows = x_ref.shape[0] * x_ref.shape[2]
    width = x_ref.shape[3]
    x = x_ref[...].astype(wide_type).reshape(rows, width)
    unit = x * lax.rsqrt(jnp.mean(x * x, axis=-1, keepdims=True) + eps_norm)
    normed = (unit * g_ref[...]).astype(low_type)
    a_ref[...] = normed.reshape(a_ref.shape)
    flat = lax.dot_general(
        w_ref[...], normed, (((0,), (1,)), ((), ())), preferred_element_type=wide_type
    )
    cos, sin = cos_ref[0], sin_ref[0]

    def rotated(start):
        first = flat[start : start + HALF]
        second = flat[start + HALF : start + HEAD_SIZE]
        return jnp.concatenate(
            [first * cos - second * sin, second * cos + first * sin], axis=0
        ).astype(low_type)

    for head in range(GROUP):
        q_ref[0, :, head * rows : (head + 1) * rows] = rotated(head * HEAD_SIZE)
    kv_ref[0] = jnp.concatenate(
        [rotated(QROWS), flat[QROWS + HEAD_SIZE :].astype(low_type)], axis=0
    )


def project(rows4, gain, weight, cos, sin):
    _, tiles, per, width = rows4.shape
    wide = 2 * per
    return pl.pallas_call(
        project_body,
        grid=(tiles,),
        in_specs=[
            pl.BlockSpec((2, 1, per, width), lambda t: (0, t, 0, 0)),
            pl.BlockSpec((1, width), lambda t: (0, 0)),
            pl.BlockSpec(weight.shape, lambda t: (0, 0)),
            pl.BlockSpec((1, HALF, wide), lambda t: (t, 0, 0)),
            pl.BlockSpec((1, HALF, wide), lambda t: (t, 0, 0)),
        ],
        out_specs=[
            pl.BlockSpec((2, 1, per, width), lambda t: (0, t, 0, 0)),
            pl.BlockSpec((1, HEAD_SIZE, GROUP * wide), lambda t: (t, 0, 0)),
            pl.BlockSpec((1, BOTH, wide), lambda t: (t, 0, 0)),
        ],
        out_shape=[
            jax.ShapeDtypeStruct(rows4.shape, low_type),
            jax.ShapeDtypeStruct((tiles, HEAD_SIZE, GROUP * wide), low_type),
            jax.ShapeDtypeStruct((tiles, BOTH, wide), low_type),
        ],
        compiler_params=pltpu.CompilerParams(vmem_limit_bytes=48 * 2**20),
        cost_estimate=pl.CostEstimate(
            flops=2 * tiles * wide * width * weight.shape[1],
            bytes_accessed=2 * (2 * tiles * wide * width + weight.size),
            transcendentals=0,
        ),
    )(rows4, gain, weight, cos, sin)


def attend_body(
    seen_ref, base_ref, q_ref, kv_ref, pos_ref, start_ref, local_ref,
    o_ref, ot_ref, lse_ref, top_ref, sum_ref, acc_ref,
):
    tile = pl.program_id(0)
    key_tiles = kv_ref.shape[0]
    top_ref[...] = jnp.full(top_ref.shape, masked_score, wide_type)
    sum_ref[...] = jnp.zeros(sum_ref.shape, wide_type)
    acc_ref[...] = jnp.zeros(acc_ref.shape, wide_type)

    def step(k, carry):
        @pl.when(seen_ref[tile * key_tiles + k] != 0)
        def _():
            keys = kv_ref[k, :HEAD_SIZE]
            values = kv_ref[k, HEAD_SIZE:]
            raw = lax.dot_general(
                keys, q_ref[0], (((0,), (0,)), ((), ())), preferred_element_type=wide_type
            )
            key_pos = base_ref[k] + local_ref[...]
            allowed = (key_pos <= pos_ref[0]) & (key_pos >= start_ref[0])
            raw = jnp.where(allowed, raw, masked_score)
            top_old = top_ref[...]
            top = jnp.maximum(top_old, jnp.max(raw, axis=0, keepdims=True))
            shrink = jnp.exp2((top_old - top) * EXP_SCALE)
            probs = jnp.where(allowed, jnp.exp2((raw - top) * EXP_SCALE), 0.0)
            sum_ref[...] = sum_ref[...] * shrink + jnp.sum(probs, axis=0, keepdims=True)
            acc_ref[...] = acc_ref[...] * shrink + jnp.dot(
                values, probs.astype(low_type), preferred_element_type=wide_type
            )
            top_ref[...] = top

        return carry

    lax.fori_loop(0, key_tiles, step, 0)
    out = acc_ref[...] / sum_ref[...]
    ot_ref[0] = out
    lse_ref[0] = top_ref[...] * EXP_SCALE + jnp.log2(sum_ref[...])
    rows = out.shape[1] // GROUP
    stacked = jnp.concatenate(
        [out[:, head * rows : (head + 1) * rows] for head in range(GROUP)], axis=0
    )
    o_ref[...] = stacked.T.astype(low_type).reshape(o_ref.shape)


def attend(seen, base, q, kv, pos, start, local):
    tiles, _, columns = q.shape
    key_tiles, _, wide = kv.shape
    per = wide // 2
    pairs = tiles * 3 * columns * wide
    return pl.pallas_call(
        attend_body,
        grid=(tiles,),
        in_specs=[
            pl.BlockSpec(memory_space=pltpu.SMEM),
            pl.BlockSpec(memory_space=pltpu.SMEM),
            pl.BlockSpec((1, HEAD_SIZE, columns), lambda t: (t, 0, 0)),
            pl.BlockSpec(kv.shape, lambda t: (0, 0, 0)),
            pl.BlockSpec((1, 1, columns), lambda t: (t, 0, 0)),
            pl.BlockSpec((1, 1, columns), lambda t: (t, 0, 0)),
            pl.BlockSpec(local.shape, lambda t: (0, 0)),
        ],
        out_specs=[
            pl.BlockSpec((2, 1, per, QROWS), lambda t: (0, t, 0, 0)),
            pl.BlockSpec((1, HEAD_SIZE, columns), lambda t: (t, 0, 0)),
            pl.BlockSpec((1, 1, columns), lambda t: (t, 0, 0)),
        ],
        out_shape=[
            jax.ShapeDtypeStruct((2, tiles, per, QROWS), low_type),
            jax.ShapeDtypeStruct((tiles, HEAD_SIZE, columns), wide_type),
            jax.ShapeDtypeStruct((tiles, 1, columns), wide_type),
        ],
        scratch_shapes=[
            pltpu.VMEM((1, columns), wide_type),
            pltpu.VMEM((1, columns), wide_type),
            pltpu.VMEM((HEAD_SIZE, columns), wide_type),
        ],
        compiler_params=pltpu.CompilerParams(vmem_limit_bytes=48 * 2**20),
        cost_estimate=pl.CostEstimate(
            flops=4 * pairs * 256, bytes_accessed=8 * q.size, transcendentals=pairs
        ),
    )(seen, base, q, kv, pos, start, local)


def attend_back_body(
    seen_ref, base_ref, q_ref, kv_ref, pos_ref, start_ref, local_ref,
    go_ref, ot_ref, lse_ref, cos_ref, sin_ref, dq_ref, dkv_ref, acc_ref,
):
    tile = pl.program_id(0)
    key_tiles = kv_ref.shape[0]

    @pl.when(tile == 0)
    def _():
        dkv_ref[...] = jnp.zeros(dkv_ref.shape, wide_type)

    rows = q_ref.shape[2] // GROUP
    turned = go_ref[...].reshape(rows, QROWS).astype(wide_type).T
    grad_wide = jnp.concatenate(
        [turned[head * HEAD_SIZE : (head + 1) * HEAD_SIZE] for head in range(GROUP)], axis=1
    )
    delta = jnp.sum(grad_wide * ot_ref[0], axis=0, keepdims=True)
    grad_out = grad_wide.astype(low_type)
    acc_ref[...] = jnp.zeros(acc_ref.shape, wide_type)

    def step(k, carry):
        @pl.when(seen_ref[tile * key_tiles + k] != 0)
        def _():
            keys = kv_ref[k, :HEAD_SIZE]
            values = kv_ref[k, HEAD_SIZE:]
            raw = lax.dot_general(
                keys, q_ref[0], (((0,), (0,)), ((), ())), preferred_element_type=wide_type
            )
            key_pos = base_ref[k] + local_ref[...]
            allowed = (key_pos <= pos_ref[0]) & (key_pos >= start_ref[0])
            probs = jnp.where(allowed, jnp.exp2(raw * EXP_SCALE - lse_ref[0]), 0.0)
            grad_probs = lax.dot_general(
                values, grad_out, (((0,), (0,)), ((), ())), preferred_element_type=wide_type
            )
            grad_scores = (probs * (grad_probs - delta)).astype(low_type)
            acc_ref[...] += jnp.dot(keys, grad_scores, preferred_element_type=wide_type)
            grad_keys = lax.dot_general(
                q_ref[0], grad_scores, (((1,), (1,)), ((), ())), preferred_element_type=wide_type
            )
            grad_values = lax.dot_general(
                grad_out,
                probs.astype(low_type),
                (((1,), (1,)), ((), ())),
                preferred_element_type=wide_type,
            )
            dkv_ref[k, :HEAD_SIZE] += grad_keys * SCALE
            dkv_ref[k, HEAD_SIZE:] += grad_values

        return carry

    lax.fori_loop(0, key_tiles, step, 0)
    cos, sin = cos_ref[0], sin_ref[0]
    for head in range(GROUP):
        part = acc_ref[:, head * rows : (head + 1) * rows] * SCALE
        first, second = part[:HALF], part[HALF:]
        dq_ref[0, head * HEAD_SIZE : (head + 1) * HEAD_SIZE] = jnp.concatenate(
            [first * cos + second * sin, second * cos - first * sin], axis=0
        ).astype(low_type)


def attend_back(seen, base, q, kv, pos, start, local, grad_out, out_turned, lse, cos, sin):
    tiles, _, columns = q.shape
    key_tiles, _, wide = kv.shape
    per = wide // 2
    pairs = tiles * 3 * columns * wide
    return pl.pallas_call(
        attend_back_body,
        grid=(tiles,),
        in_specs=[
            pl.BlockSpec(memory_space=pltpu.SMEM),
            pl.BlockSpec(memory_space=pltpu.SMEM),
            pl.BlockSpec((1, HEAD_SIZE, columns), lambda t: (t, 0, 0)),
            pl.BlockSpec(kv.shape, lambda t: (0, 0, 0)),
            pl.BlockSpec((1, 1, columns), lambda t: (t, 0, 0)),
            pl.BlockSpec((1, 1, columns), lambda t: (t, 0, 0)),
            pl.BlockSpec(local.shape, lambda t: (0, 0)),
            pl.BlockSpec((2, 1, per, QROWS), lambda t: (0, t, 0, 0)),
            pl.BlockSpec((1, HEAD_SIZE, columns), lambda t: (t, 0, 0)),
            pl.BlockSpec((1, 1, columns), lambda t: (t, 0, 0)),
            pl.BlockSpec((1, HALF, wide), lambda t: (t, 0, 0)),
            pl.BlockSpec((1, HALF, wide), lambda t: (t, 0, 0)),
        ],
        out_specs=[
            pl.BlockSpec((1, QROWS, wide), lambda t: (t, 0, 0)),
            pl.BlockSpec(kv.shape, lambda t: (0, 0, 0)),
        ],
        out_shape=[
            jax.ShapeDtypeStruct((tiles, QROWS, wide), low_type),
            jax.ShapeDtypeStruct(kv.shape, wide_type),
        ],
        scratch_shapes=[pltpu.VMEM((HEAD_SIZE, columns), wide_type)],
        compiler_params=pltpu.CompilerParams(vmem_limit_bytes=48 * 2**20),
        cost_estimate=pl.CostEstimate(
            flops=10 * pairs * 256, bytes_accessed=16 * q.size, transcendentals=pairs
        ),
    )(seen, base, q, kv, pos, start, local, grad_out, out_turned, lse, cos, sin)


def finish_body(dq_ref, dkv_ref, cos_ref, sin_ref, out_ref):
    cos, sin = cos_ref[0], sin_ref[0]
    first, second = dkv_ref[0, :HALF], dkv_ref[0, HALF:HEAD_SIZE]
    turned = jnp.concatenate(
        [
            dq_ref[0].astype(wide_type),
            first * cos + second * sin,
            second * cos - first * sin,
            dkv_ref[0, HEAD_SIZE:],
        ],
        axis=0,
    )
    out_ref[...] = turned.T.astype(low_type).reshape(out_ref.shape)


def finish(dq, dkv, cos, sin):
    tiles, _, wide = dq.shape
    per = wide // 2
    return pl.pallas_call(
        finish_body,
        grid=(tiles,),
        in_specs=[
            pl.BlockSpec((1, QROWS, wide), lambda t: (t, 0, 0)),
            pl.BlockSpec((1, BOTH, wide), lambda t: (t, 0, 0)),
            pl.BlockSpec((1, HALF, wide), lambda t: (t, 0, 0)),
            pl.BlockSpec((1, HALF, wide), lambda t: (t, 0, 0)),
        ],
        out_specs=pl.BlockSpec((2, 1, per, QROWS + BOTH), lambda t: (0, t, 0, 0)),
        out_shape=jax.ShapeDtypeStruct((2, tiles, per, QROWS + BOTH), low_type),
        compiler_params=pltpu.CompilerParams(vmem_limit_bytes=48 * 2**20),
    )(dq, dkv, cos, sin)


def adamw(param, grad, first, second):
    first_new = beta_first * first + (1.0 - beta_first) * grad
    second_new = beta_second * second + (1.0 - beta_second) * grad * grad
    first_hat = first_new / (1.0 - beta_first**STEP)
    second_hat = second_new / (1.0 - beta_second**STEP)
    change = -learn_rate * (first_hat / (jnp.sqrt(second_hat) + adam_eps) + weight_decay * param)
    return (first_new, second_new, change)


def on_device(
    tokens,
    upstream,
    offsets,
    query_weight,
    keyval_weight,
    output_weight,
    gateup_weight,
    down_weight,
    norm_gains,
    first_query,
    first_keyval,
    first_output,
    first_gateup,
    first_down,
    first_gains,
    second_query,
    second_keyval,
    second_output,
    second_gateup,
    second_down,
    second_gains,
):
    h, l, y, xbit, cbit = bits()
    block_rows = offsets.shape[0]
    per = tokens.shape[0]
    width = tokens.shape[1]
    wide = 2 * per
    count = 8 * per
    hidden_part = down_weight.shape[1] // 2

    rows4 = gather_rows(tokens)
    gains = whole_gains(norm_gains.astype(low_type)).astype(wide_type)

    def halves(array, axis=-1):
        size = array.shape[axis] // 2
        return (
            lax.slice_in_dim(array, 0, size, axis=axis),
            lax.slice_in_dim(array, size, 2 * size, axis=axis),
        )

    def split(arrays):
        lower = jnp.concatenate([halves(a)[0].astype(low_type) for a in arrays], axis=-1)
        upper = jnp.concatenate([halves(a)[1].astype(low_type) for a in arrays], axis=-1)
        return choose(l, lower, upper), choose(l, upper, lower)

    qkv_full = gather_weight(*split([query_weight, keyval_weight[0], keyval_weight[1]]))
    output_full = gather_weight(*split([output_weight]))
    gate_full = gather_weight(*split([gateup_weight[0]]))
    up_full = gather_weight(*split([gateup_weight[1]]))
    down_full = gather_weight(*split([down_weight]))

    def relative(own):
        four = own.reshape(2, 2, per)
        four = choose(xbit, four, four[::-1])
        return choose(cbit, four, four[:, ::-1])

    offset_tiles = jnp.concatenate(
        [relative(offsets), relative(hop_low(offsets))], axis=0
    ).reshape(4, wide)
    lane = jnp.arange(wide, dtype=jnp.int32)
    local = choose(cbit, lane, lane ^ per)
    mine = jnp.arange(4, dtype=jnp.int32)

    def bases(group_h, group_y, low_bits, x_bits):
        block = 4 * group_h + 2 * low_bits + group_y
        return block * block_rows + x_bits * wide

    low_bits, x_bits = l ^ (mine // 2), xbit ^ (mine % 2)
    own_base = bases(h, y, low_bits, x_bits)
    one = jnp.ones((2,), jnp.int32)
    key_base = jnp.concatenate(
        [
            own_base,
            bases(h, 1 - y, low_bits, x_bits),
            bases(h - 1, y, one, x_bits[:2]),
            bases(h - 1, 1 - y, one, x_bits[:2]),
        ]
    ).astype(jnp.int32)
    query_pos = own_base[:, None] + local[None, :]
    doc_start = query_pos - offset_tiles
    seen = (
        (key_base[None, :] <= own_base[:, None] + wide - 1)
        & (key_base[None, :] + wide - 1 >= jnp.min(doc_start, axis=1, keepdims=True))
    ).astype(jnp.int32).reshape(-1)
    spread = lambda a: jnp.tile(a, (1, GROUP)).reshape(4, 1, GROUP * wide)
    query_lanes, start_lanes = spread(query_pos), spread(doc_start)
    local_column = local.reshape(wide, 1)
    freqs = rope_base ** (-(jnp.arange(HALF).astype(wide_type) * 2.0 / HEAD_SIZE))
    angle = freqs[None, :, None] * offset_tiles.astype(wide_type)[:, None, :]
    cos, sin = jnp.cos(angle), jnp.sin(angle)

    normed4, q_turned, kv_own = project(rows4, gains[0:1], qkv_full, cos, sin)
    normed_one = normed4.reshape(count, width)

    def last_block(tiles):
        return choose(l, tiles[2:], tiles[:2])

    near = last_block(kv_own)
    kv = jnp.concatenate(
        [kv_own, hop_y(kv_own), to_next(near, 0), to_next(near, 1)], axis=0
    )
    layout = (seen, key_base, q_turned, kv, query_lanes, start_lanes, local_column)
    attended4, out_turned, lse = attend(*layout)
    attended_low = attended4.reshape(count, QROWS)

    inputs = tokens.astype(wide_type)
    inverse_one = lax.rsqrt(jnp.mean(inputs * inputs, axis=-1, keepdims=True) + eps_norm)
    unit_one = inputs * inverse_one
    middle = inputs + branch_sum(attended_low, output_full)
    inverse_two = lax.rsqrt(jnp.mean(middle * middle, axis=-1, keepdims=True) + eps_norm)
    unit_two = middle * inverse_two
    normed_two = gather_rows((unit_two * gains[1]).astype(low_type)).reshape(count, width)
    out_rows = gather_rows(upstream).reshape(count, width)

    gate = jnp.dot(normed_two, gate_full, preferred_element_type=wide_type)
    upward = jnp.dot(normed_two, up_full, preferred_element_type=wide_type)
    sigma = jax.nn.sigmoid(gate)
    hidden = (gate * sigma * upward).astype(low_type)
    down_share = reduce_weight([(out_rows.T, hidden)])
    grad_hidden = jnp.dot(out_rows, down_full, preferred_element_type=wide_type)
    grad_gate = (grad_hidden * upward * sigma * (1.0 + gate * (1.0 - sigma))).astype(low_type)
    grad_up = (grad_hidden * gate * sigma).astype(low_type)
    half = count // 2

    def ffn_part(index):
        rows = slice(index * half, (index + 1) * half)
        out = contract_last(grad_gate[rows], gate_full) + contract_last(grad_up[rows], up_full)
        return out.reshape(4, per, width)

    grad_normed_two = scatter_rows(ffn_part(0), ffn_part(1))
    block_out = (middle + branch_sum(hidden, down_full)).astype(low_type)
    turned_two = normed_two.T
    gate_share = reduce_weight([(turned_two, grad_gate)])
    up_share = reduce_weight([(turned_two, grad_up)])
    gain_two = jnp.sum(grad_normed_two * unit_two, axis=0)
    grad_middle = upstream.astype(wide_type) + norm_back(
        grad_normed_two, unit_two, inverse_two, gains[1]
    )
    branch_grad = gather_rows(grad_middle.astype(low_type)).reshape(count, width)
    grad_attended = jnp.dot(branch_grad, output_full, preferred_element_type=wide_type).astype(
        low_type
    )
    dq_turned, dkv_all = attend_back(
        *layout, grad_attended.reshape(2, 4, per, QROWS), out_turned, lse, cos, sin
    )
    dkv_sent = dkv_all.astype(low_type)
    dkv_own = dkv_all[:4] + hop_y(dkv_sent[4:8]).astype(wide_type)
    dkv_late = to_previous(dkv_sent[8:10], 0).astype(wide_type) + to_previous(
        dkv_sent[10:12], 1
    ).astype(wide_type)
    nothing = jnp.zeros_like(dkv_late)
    dkv_own = dkv_own + choose(
        l,
        jnp.concatenate([nothing, dkv_late], axis=0),
        jnp.concatenate([dkv_late, nothing], axis=0),
    )
    dqkv = finish(dq_turned, dkv_own, cos, sin).reshape(count, QROWS + BOTH)
    grad_normed_one = branch_sum(dqkv, qkv_full)
    attn_share = reduce_weight([(normed_one.T, dqkv), (branch_grad.T, attended_low)])
    gain_one = jnp.sum(grad_normed_one * unit_one, axis=0)
    grad_tokens = grad_middle + norm_back(grad_normed_one, unit_one, inverse_one, gains[0])
    gain_total = sum_all(jnp.stack([gain_one, gain_two]))

    def joined(share, start, stop):
        return ordered(l, share[0][:, start:stop], share[1][:, start:stop], 1)

    edge_one = QROWS + HEAD_SIZE
    edge_two = QROWS + BOTH
    edge_three = edge_two + QROWS
    grad_query = joined(attn_share, 0, QROWS)
    grad_keyval = jnp.stack(
        [joined(attn_share, QROWS, edge_one), joined(attn_share, edge_one, edge_two)]
    )
    grad_output = joined(attn_share, edge_two, edge_three)
    grad_gateup = jnp.stack(
        [joined(gate_share, 0, hidden_part), joined(up_share, 0, hidden_part)]
    )
    grad_down = joined(down_share, 0, hidden_part)
    squares = [
        jnp.sum(part * part)
        for share in (down_share, gate_share, up_share, attn_share)
        for part in share
    ]
    weight_square = sum_all(functools.reduce(jnp.add, squares).reshape(1, 1))[0, 0]
    grad_norm = jnp.sqrt(weight_square + jnp.sum(gain_total * gain_total))
    rows_owned = query_weight.shape[0]
    grad_gains = lax.dynamic_slice_in_dim(
        gain_total, lax.axis_index("dp") * rows_owned, rows_owned, 1
    )
    clipping_bound = math.sqrt(
        MODEL_WIDTH
        * (2 * QUERY_HEAD_COUNT * HEAD_SIZE + 2 * KEY_VALUE_HEADS * HEAD_SIZE + 3 * HIDDEN_UNITS)
        + 2 * MODEL_WIDTH
    )
    clip = jnp.minimum(1.0, clipping_bound / (grad_norm + 1e-06))
    params = (query_weight, keyval_weight, output_weight, gateup_weight, down_weight, norm_gains)
    firsts = (first_query, first_keyval, first_output, first_gateup, first_down, first_gains)
    seconds = (second_query, second_keyval, second_output, second_gateup, second_down, second_gains)
    grads = (grad_query, grad_keyval, grad_output, grad_gateup, grad_down, grad_gains)
    states = [
        adamw(params[index], grads[index] * clip, firsts[index], seconds[index])
        for index in range(6)
    ]
    return (
        block_out,
        grad_tokens,
        grad_norm,
        *grads,
        *[state[0] for state in states],
        *[state[1] for state in states],
        *[state[2] for state in states],
    )


def solution(mesh):
    weights = (
        P("dp", "mp"),
        P(None, "dp", "mp"),
        P("dp", "mp"),
        P(None, "dp", "mp"),
        P("dp", "mp"),
        P(None, "dp"),
    )
    rows = P(("dp", "mp"), None)
    return jax.shard_map(
        on_device,
        mesh=mesh,
        in_specs=(rows, rows, P("dp"), *weights, *weights, *weights),
        out_specs=(rows, rows, P(), *weights, *weights, *weights, *weights),
        check_vma=False,
    )
```

```python
import functools
import math

import jax
import jax.numpy as jnp
from jax import lax
from jax.experimental import pallas as pl
from jax.experimental.pallas import tpu as pltpu
from jax.sharding import PartitionSpec as P

MODEL_WIDTH = 2560
QUERY_HEAD_COUNT = 32
KEY_VALUE_HEADS = 8
HEAD_SIZE = 80
HIDDEN_UNITS = 7168
STEP = 10

eps_norm = 1e-05
rope_base = 1000000.0
beta_first = 0.9
beta_second = 0.95
learn_rate = 0.02
weight_decay = 0.1
adam_eps = 1e-08
masked_score = -1e30

low_type = jnp.bfloat16
wide_type = jnp.float32

HALF = HEAD_SIZE // 2
GROUP = QUERY_HEAD_COUNT // KEY_VALUE_HEADS
QROWS = GROUP * HEAD_SIZE
BOTH = 2 * HEAD_SIZE
EDGE = QROWS + BOTH
EXP_SCALE = (HEAD_SIZE ** (-0.5)) * math.log2(math.e)
SCALE = HEAD_SIZE ** (-0.5)
AXES = ("dp", "mp")


def hop(block, move):
    dp_size, mp_size = lax.axis_size("dp"), lax.axis_size("mp")
    route = []
    for d in range(dp_size):
        for m in range(mp_size):
            target = move(d, m)
            if target is not None:
                route.append((d * mp_size + m, target[0] * mp_size + target[1]))
    return lax.ppermute(block, AXES, route)


def hop_core(block):
    return hop(block, lambda d, m: (d, m ^ 1))


def hop_x(block):
    return hop(block, lambda d, m: (d, m ^ 2))


def hop_low(block):
    return hop(block, lambda d, m: (d ^ 2, m))


def hop_y(block):
    return hop(block, lambda d, m: (d ^ 1, m))


def hop_ring(block):
    size = lax.axis_size("dp")
    return hop(block, lambda d, m: ((d + 4) % size, m))


def to_next(block, flip):
    size = lax.axis_size("dp")

    def move(d, m):
        if d + 4 >= size or (flip and d % 2 == 0):
            return None
        return (d + 4) ^ flip, m

    return hop(block, move)


def to_previous(block, flip):
    def move(d, m):
        if d < 4 or (flip and d % 2 == 1):
            return None
        return (d - 4) ^ flip, m

    return hop(block, move)


def bits():
    d = lax.axis_index("dp")
    m = lax.axis_index("mp")
    return d // 4, (d // 2) % 2, d % 2, m // 2, m % 2


def choose(bit, if_zero, if_one):
    return jnp.where(bit == 0, if_zero, if_one)


def ordered(bit, mine, other, axis):
    return choose(
        bit,
        jnp.concatenate([mine, other], axis=axis),
        jnp.concatenate([other, mine], axis=axis),
    )


def keep_body(held_ref, out_ref):
    out_ref[...] = held_ref[...]


class Windows:
    def __init__(self, held):
        self.held = held

    def __call__(self, *arrays):
        *given, held = lax.optimization_barrier((*arrays, self.held))
        self.held = pl.pallas_call(
            keep_body,
            out_shape=jax.ShapeDtypeStruct(held.shape, held.dtype),
            cost_estimate=pl.CostEstimate(flops=10**12, bytes_accessed=0, transcendentals=0),
        )(held)
        return given


def rest_of_ring(first):
    blocks = [first]
    for _ in range(lax.axis_size("dp") // 4 - 2):
        blocks.append(hop_ring(blocks[-1]))
    return blocks


def sum_all(value):
    ring = lax.axis_size("dp") // 4
    for step in (hop_core, hop_x, hop_low, hop_y):
        value = value + step(value)
    travel = value
    for _ in range(1, ring):
        travel = hop_ring(travel)
        value = value + travel
    return value


def norm_back(incoming, unit_rows, inverse_root, gain):
    scaled = incoming * gain
    return inverse_root * (
        scaled - unit_rows * jnp.mean(scaled * unit_rows, axis=-1, keepdims=True)
    )


VMEM_LIMIT = 56 * 2**20


def call(body, grid, in_specs, out_specs, out_shape, scratch=(), flops=0):
    return pl.pallas_call(
        body,
        grid=grid,
        in_specs=in_specs,
        out_specs=out_specs,
        out_shape=out_shape,
        scratch_shapes=list(scratch),
        compiler_params=pltpu.CompilerParams(vmem_limit_bytes=VMEM_LIMIT),
        cost_estimate=pl.CostEstimate(flops=flops, bytes_accessed=0, transcendentals=0),
    )


def shape(dims, kind):
    return jax.ShapeDtypeStruct(dims, kind)


def whole(array):
    zeros = (0,) * array.ndim
    return pl.BlockSpec(array.shape, lambda *_: zeros)


def tile_of(*dims):
    rest = (0,) * (len(dims) - 1)
    return pl.BlockSpec(dims, lambda t: (t, *rest))


def dot(left, right, left_dim, right_dim):
    return lax.dot_general(
        left, right, (((left_dim,), (right_dim,)), ((), ())), preferred_element_type=wide_type
    )


def any_spec():
    return pl.BlockSpec(memory_space=pl.ANY)


def smem_spec():
    return pl.BlockSpec(memory_space=pltpu.SMEM)


class Pieces:
    def __init__(self, blocks, places):
        self.blocks = blocks
        self.places = places
        _, self.rows, self.columns = blocks[0].shape

    def count(self):
        return 1 + len(self.blocks)

    def specs(self):
        return [smem_spec()] + [any_spec()] * len(self.blocks)

    def values(self):
        return [self.places, *self.blocks]

    def scratch(self):
        number = 2 * len(self.blocks)
        return [
            pltpu.VMEM((number * self.rows, self.columns), low_type),
            pltpu.SemaphoreType.DMA((number,)),
        ]


def load_pieces(refs, scratch):
    place_ref, *block_refs = refs
    weight_ref, sem_ref = scratch
    copies = []
    for index, block_ref in enumerate(block_refs):
        rows = block_ref.shape[1]
        for part in range(2):
            number = 2 * index + part
            start = pl.multiple_of(place_ref[number] * rows, rows & -rows)
            copies.append(
                pltpu.make_async_copy(
                    block_ref.at[part], weight_ref.at[pl.ds(start, rows)], sem_ref.at[number]
                )
            )
    for copy in copies:
        copy.start()
    for copy in copies:
        copy.wait()


def halves_body(bit_ref, weight_ref, own_ref, other_ref):
    size = own_ref.shape[1]
    for out_ref, which in ((own_ref, bit_ref[0]), (other_ref, 1 - bit_ref[0])):
        start = pl.multiple_of(which * size, size & -size)
        out_ref[...] = weight_ref[:, pl.ds(start, size)].astype(low_type)


def halves(bit, weight, layer=None):
    rows, columns = weight.shape[-2:]
    step = rows // 5
    if layer is None:
        spec = pl.BlockSpec((step, columns), lambda i: (i, 0))
    else:
        spec = pl.BlockSpec((pl.squeezed, step, columns), lambda i: (layer, i, 0))
    half = pl.BlockSpec((step, columns // 2), lambda i: (i, 0))
    return call(
        halves_body,
        (5,),
        [smem_spec(), spec],
        [half, half],
        [shape((rows, columns // 2), low_type)] * 2,
    )(bit.astype(jnp.int32).reshape(1), weight)


def pack_body(*refs):
    *parts, out_ref = refs
    start = 0
    for part in parts:
        if len(part.shape) == 2:
            out_ref[start] = part[...]
            start += 1
        else:
            out_ref[start : start + part.shape[0]] = part[...]
            start += part.shape[0]


def pack(*parts):
    rows, width = parts[0].shape[-2:]
    step = width // 4
    specs, number = [], 0
    for part in parts:
        if part.ndim == 2:
            specs.append(pl.BlockSpec((rows, step), lambda n: (0, n)))
            number += 1
        else:
            specs.append(pl.BlockSpec((part.shape[0], rows, step), lambda n: (0, 0, n)))
            number += part.shape[0]
    return call(
        pack_body,
        (4,),
        specs,
        pl.BlockSpec((number, rows, step), lambda n: (0, 0, n)),
        shape((number, rows, width), parts[0].dtype),
    )(*parts)


def both_cores(near_ref, far_ref):
    return jnp.concatenate([near_ref[0], far_ref[0]], axis=0)


def project_body(count, x_ref, xc_ref, cos_ref, sin_ref, *refs):
    pieces = refs[:count]
    at_ref, q_ref, kv_ref, g_ref, w_ref, sem_ref = refs[count:]

    @pl.when(pl.program_id(0) == 0)
    def _():
        load_pieces(pieces, (w_ref, sem_ref))
        turned = w_ref[:, 384:].astype(wide_type).T
        g_ref[...] = turned[EDGE - 384 : EDGE - 384 + 2]

    x = both_cores(x_ref, xc_ref).astype(wide_type)
    rows = x.shape[0]
    unit = x * lax.rsqrt(jnp.mean(x * x, axis=-1, keepdims=True) + eps_norm)
    normed = (unit * g_ref[0:1]).astype(low_type)
    at_ref[...] = normed.T
    flat = dot(w_ref[...], normed, 0, 1)
    cos, sin = cos_ref[0], sin_ref[0]

    def rotated(start):
        first = flat[start : start + HALF]
        second = flat[start + HALF : start + HEAD_SIZE]
        return jnp.concatenate(
            [first * cos - second * sin, second * cos + first * sin], axis=0
        ).astype(low_type)

    for head in range(GROUP):
        q_ref[0, :, head * rows : (head + 1) * rows] = rotated(head * HEAD_SIZE)
    kv_ref[0] = jnp.concatenate(
        [rotated(QROWS), flat[QROWS + HEAD_SIZE : EDGE].astype(low_type)], axis=0
    )


def project(near, far, weight, cos, sin):
    tiles, per, width = near.shape
    wide = 2 * per
    return call(
        functools.partial(project_body, weight.count()),
        (tiles,),
        [
            tile_of(1, per, width),
            tile_of(1, per, width),
            tile_of(1, HALF, wide),
            tile_of(1, HALF, wide),
            *weight.specs(),
        ],
        [
            pl.BlockSpec((width, wide), lambda t: (0, t)),
            tile_of(1, HEAD_SIZE, GROUP * wide),
            tile_of(1, BOTH, wide),
            pl.BlockSpec((2, width), lambda t: (0, 0)),
        ],
        [
            shape((width, tiles * wide), low_type),
            shape((tiles, HEAD_SIZE, GROUP * wide), low_type),
            shape((tiles, BOTH, wide), low_type),
            shape((2, width), wide_type),
        ],
        weight.scratch(),
    )(near, far, cos, sin, *weight.values())


def load_keys(kv_refs, kv_ref, sem_ref):
    copies, start = [], 0
    for index, part in enumerate(kv_refs):
        size = part.shape[0]
        copies.append(
            pltpu.make_async_copy(part, kv_ref.at[start : start + size], sem_ref.at[index])
        )
        start += size
    for copy in copies:
        copy.start()
    for copy in copies:
        copy.wait()


def attend_body(count, seen_ref, base_ref, q_ref, pos_ref, start_ref, local_ref, *refs):
    kv_parts, pieces = refs[:4], refs[4 : 4 + count]
    o_ref, ot_ref, lse_ref, near_ref, far_ref = refs[4 + count : 9 + count]
    top_ref, sum_ref, acc_ref, kv_ref, kv_sem, w_ref, sem_ref = refs[9 + count :]
    tile = pl.program_id(0)
    key_tiles = kv_ref.shape[0]

    @pl.when(tile == 0)
    def _():
        load_keys(kv_parts, kv_ref, kv_sem)
        load_pieces(pieces, (w_ref, sem_ref))

    top_ref[...] = jnp.full(top_ref.shape, masked_score, wide_type)
    sum_ref[...] = jnp.zeros(sum_ref.shape, wide_type)
    acc_ref[...] = jnp.zeros(acc_ref.shape, wide_type)

    def step(k, carry):
        @pl.when(seen_ref[tile * key_tiles + k] != 0)
        def _():
            raw = dot(kv_ref[k, :HEAD_SIZE], q_ref[0], 0, 0)
            key_pos = base_ref[k] + local_ref[...]
            allowed = (key_pos <= pos_ref[0]) & (key_pos >= start_ref[0])
            raw = jnp.where(allowed, raw, masked_score)
            top_old = top_ref[...]
            top = jnp.maximum(top_old, jnp.max(raw, axis=0, keepdims=True))
            shrink = jnp.exp2((top_old - top) * EXP_SCALE)
            probs = jnp.where(allowed, jnp.exp2((raw - top) * EXP_SCALE), 0.0)
            sum_ref[...] = sum_ref[...] * shrink + jnp.sum(probs, axis=0, keepdims=True)
            acc_ref[...] = acc_ref[...] * shrink + dot(
                kv_ref[k, HEAD_SIZE:], probs.astype(low_type), 1, 0
            )
            top_ref[...] = top

        return carry

    lax.fori_loop(0, key_tiles, step, 0)
    out = acc_ref[...] / sum_ref[...]
    ot_ref[0] = out
    lse_ref[0] = top_ref[...] * EXP_SCALE + jnp.log2(sum_ref[...])
    rows = out.shape[1] // GROUP
    stacked = jnp.concatenate(
        [out[:, head * rows : (head + 1) * rows] for head in range(GROUP)], axis=0
    )
    attended = stacked.T.astype(low_type)
    o_ref[0] = attended
    branch = dot(attended, w_ref[...], 1, 1)
    near_ref[0] = branch[: rows // 2].astype(low_type)
    far_ref[0] = branch[rows // 2 :].astype(low_type)


def key_scratch(kv):
    number = sum(part.shape[0] for part in kv)
    return [
        pltpu.VMEM((number, *kv[0].shape[1:]), low_type),
        pltpu.SemaphoreType.DMA((len(kv),)),
    ]


def attend(layout, kv, weight):
    seen, base, q, pos, start, local = layout
    tiles, _, columns = q.shape
    wide = kv[0].shape[2]
    width = 2 * len(weight.blocks) * weight.rows
    return call(
        functools.partial(attend_body, weight.count()),
        (tiles,),
        [
            smem_spec(),
            smem_spec(),
            tile_of(1, HEAD_SIZE, columns),
            tile_of(1, 1, columns),
            tile_of(1, 1, columns),
            whole(local),
            *[any_spec()] * 4,
            *weight.specs(),
        ],
        [
            tile_of(1, wide, QROWS),
            tile_of(1, HEAD_SIZE, columns),
            tile_of(1, 1, columns),
            tile_of(1, wide // 2, width),
            tile_of(1, wide // 2, width),
        ],
        [
            shape((tiles, wide, QROWS), low_type),
            shape((tiles, HEAD_SIZE, columns), wide_type),
            shape((tiles, 1, columns), wide_type),
            shape((tiles, wide // 2, width), low_type),
            shape((tiles, wide // 2, width), low_type),
        ],
        [
            pltpu.VMEM((1, columns), wide_type),
            pltpu.VMEM((1, columns), wide_type),
            pltpu.VMEM((HEAD_SIZE, columns), wide_type),
            *key_scratch(kv),
            *weight.scratch(),
        ],
    )(*layout, *kv, *weight.values())


def attend_back_body(
    count, seen_ref, base_ref, q_ref, pos_ref, start_ref, local_ref,
    z_ref, zc_ref, ot_ref, lse_ref, cos_ref, sin_ref, *refs,
):
    kv_parts, pieces = refs[:4], refs[4 : 4 + count]
    dq_ref, *dkv_parts = refs[4 + count : 9 + count]
    acc_ref, dkv_ref, kv_ref, kv_sem, w_ref, sem_ref = refs[9 + count :]
    tile = pl.program_id(0)
    key_tiles = kv_ref.shape[0]

    @pl.when(tile == 0)
    def _():
        load_keys(kv_parts, kv_ref, kv_sem)
        load_pieces(pieces, (w_ref, sem_ref))
        dkv_ref[...] = jnp.zeros(dkv_ref.shape, wide_type)

    rows = q_ref.shape[2] // GROUP
    turned = dot(w_ref[...], both_cores(z_ref, zc_ref), 0, 1).astype(low_type)
    grad_out = jnp.concatenate(
        [turned[head * HEAD_SIZE : (head + 1) * HEAD_SIZE] for head in range(GROUP)], axis=1
    )
    delta = jnp.sum(grad_out.astype(wide_type) * ot_ref[0], axis=0, keepdims=True)
    acc_ref[...] = jnp.zeros(acc_ref.shape, wide_type)

    def step(k, carry):
        @pl.when(seen_ref[tile * key_tiles + k] != 0)
        def _():
            raw = dot(kv_ref[k, :HEAD_SIZE], q_ref[0], 0, 0)
            key_pos = base_ref[k] + local_ref[...]
            allowed = (key_pos <= pos_ref[0]) & (key_pos >= start_ref[0])
            probs = jnp.where(allowed, jnp.exp2(raw * EXP_SCALE - lse_ref[0]), 0.0)
            grad_probs = dot(kv_ref[k, HEAD_SIZE:], grad_out, 0, 0)
            grad_scores = (probs * (grad_probs - delta)).astype(low_type)
            acc_ref[...] += dot(kv_ref[k, :HEAD_SIZE], grad_scores, 1, 0)
            dkv_ref[k, :HEAD_SIZE] += dot(q_ref[0], grad_scores, 1, 1) * SCALE
            dkv_ref[k, HEAD_SIZE:] += dot(grad_out, probs.astype(low_type), 1, 1)

        return carry

    lax.fori_loop(0, key_tiles, step, 0)
    cos, sin = cos_ref[0], sin_ref[0]
    for head in range(GROUP):
        part = acc_ref[:, head * rows : (head + 1) * rows] * SCALE
        first, second = part[:HALF], part[HALF:]
        dq_ref[0, head * HEAD_SIZE : (head + 1) * HEAD_SIZE] = jnp.concatenate(
            [first * cos + second * sin, second * cos - first * sin], axis=0
        ).astype(low_type)

    @pl.when(tile == pl.num_programs(0) - 1)
    def _():
        start = 0
        for part in dkv_parts:
            size = part.shape[0]
            part[...] = dkv_ref[start : start + size].astype(part.dtype)
            start += size


def attend_back(layout, kv, weight, near, far, out_turned, lse, cos, sin):
    seen, base, q, pos, start, local = layout
    tiles, _, columns = q.shape
    wide = kv[0].shape[2]
    width = near.shape[2]
    kinds = (wide_type, low_type, low_type, low_type)
    held = key_scratch(kv)
    return call(
        functools.partial(attend_back_body, weight.count()),
        (tiles,),
        [
            smem_spec(),
            smem_spec(),
            tile_of(1, HEAD_SIZE, columns),
            tile_of(1, 1, columns),
            tile_of(1, 1, columns),
            whole(local),
            tile_of(1, wide // 2, width),
            tile_of(1, wide // 2, width),
            tile_of(1, HEAD_SIZE, columns),
            tile_of(1, 1, columns),
            tile_of(1, HALF, wide),
            tile_of(1, HALF, wide),
            *[any_spec()] * 4,
            *weight.specs(),
        ],
        [tile_of(1, QROWS, wide)] + [whole(part) for part in kv],
        [shape((tiles, QROWS, wide), low_type)]
        + [shape(part.shape, kind) for part, kind in zip(kv, kinds)],
        [
            pltpu.VMEM((HEAD_SIZE, columns), wide_type),
            pltpu.VMEM(held[0].shape, wide_type),
            *held,
            *weight.scratch(),
        ],
    )(*layout, near, far, out_turned, lse, cos, sin, *kv, *weight.values())


def finish_body(late_ref, dq_ref, own_ref, y_ref, a_ref, b_ref, cos_ref, sin_ref, out_ref):
    late = (pl.program_id(0) // 2 == late_ref[0]).astype(wide_type)
    total = own_ref[0] + y_ref[0].astype(wide_type)
    total = total + late * (a_ref[0].astype(wide_type) + b_ref[0].astype(wide_type))
    cos, sin = cos_ref[0], sin_ref[0]
    first, second = total[:HALF], total[HALF:HEAD_SIZE]
    turned = jnp.concatenate(
        [
            dq_ref[0].astype(wide_type),
            first * cos + second * sin,
            second * cos - first * sin,
            total[HEAD_SIZE:],
            jnp.zeros((2, total.shape[1]), wide_type),
        ],
        axis=0,
    )
    out_ref[0] = turned.T.astype(low_type)


def finish(late, dq, own, from_y, from_a, from_b, cos, sin):
    tiles, _, wide = dq.shape
    return call(
        finish_body,
        (tiles,),
        [
            smem_spec(),
            tile_of(1, QROWS, wide),
            tile_of(1, BOTH, wide),
            tile_of(1, BOTH, wide),
            pl.BlockSpec((1, BOTH, wide), lambda t: (t % 2, 0, 0)),
            pl.BlockSpec((1, BOTH, wide), lambda t: (t % 2, 0, 0)),
            tile_of(1, HALF, wide),
            tile_of(1, HALF, wide),
        ],
        tile_of(1, wide, EDGE + 2),
        shape((tiles, wide, EDGE + 2), low_type),
    )(late, dq, own, from_y, from_a, from_b, cos, sin)


def turn_body(near_ref, far_ref, out_ref):
    out_ref[...] = both_cores(near_ref, far_ref).T


def turn(near, far):
    tiles, per, width = near.shape
    return call(
        turn_body,
        (tiles,),
        [tile_of(1, per, width), tile_of(1, per, width)],
        pl.BlockSpec((width, 2 * per), lambda t: (0, t)),
        shape((width, 2 * per * tiles), low_type),
    )(near, far)


def ffn_body(count, near_ref, far_ref, *refs):
    gate_pieces, up_pieces = refs[:count], refs[count : 2 * count]
    at_ref, hid_ref, one_ref, two_ref, gate_ref, gate_sem, up_ref, up_sem = refs[2 * count :]

    @pl.when(pl.program_id(0) == 0)
    def _():
        load_pieces(gate_pieces, (gate_ref, gate_sem))
        load_pieces(up_pieces, (up_ref, up_sem))

    normed = both_cores(near_ref, far_ref)
    at_ref[...] = normed.T
    gate = dot(normed, gate_ref[...], 1, 0)
    upward = dot(normed, up_ref[...], 1, 0)
    sigma = 1.0 / (1.0 + jnp.exp(-gate))
    passed = gate * sigma
    hid_ref[0] = (passed * upward).astype(low_type)
    one_ref[0] = upward * sigma * (1.0 + gate * (1.0 - sigma))
    two_ref[0] = passed


def ffn(near, far, gate_weight, up_weight):
    tiles, per, width = near.shape
    wide = 2 * per
    hidden = gate_weight.columns
    return call(
        functools.partial(ffn_body, gate_weight.count()),
        (tiles,),
        [
            tile_of(1, per, width),
            tile_of(1, per, width),
            *gate_weight.specs(),
            *up_weight.specs(),
        ],
        [
            pl.BlockSpec((width, wide), lambda t: (0, t)),
            tile_of(1, wide, hidden),
            tile_of(1, wide, hidden),
            tile_of(1, wide, hidden),
        ],
        [
            shape((width, tiles * wide), low_type),
            shape((tiles, wide, hidden), low_type),
            shape((tiles, wide, hidden), wide_type),
            shape((tiles, wide, hidden), wide_type),
        ],
        gate_weight.scratch() + up_weight.scratch(),
    )(near, far, *gate_weight.values(), *up_weight.values())


def ffn_back_body(count, near_ref, far_ref, one_ref, two_ref, *refs):
    dgate_ref, dup_ref, w_ref, sem_ref = refs[count:]

    @pl.when(pl.program_id(0) == 0)
    def _():
        load_pieces(refs[:count], (w_ref, sem_ref))

    grad_hidden = dot(both_cores(near_ref, far_ref), w_ref[...], 1, 0)
    dgate_ref[0] = (grad_hidden * one_ref[0]).astype(low_type)
    dup_ref[0] = (grad_hidden * two_ref[0]).astype(low_type)


def ffn_back(near, far, weight, one, two):
    tiles, per, width = near.shape
    wide = 2 * per
    hidden = weight.columns
    part = tile_of(1, wide, hidden)
    return call(
        functools.partial(ffn_back_body, weight.count()),
        (tiles,),
        [tile_of(1, per, width), tile_of(1, per, width), part, part, *weight.specs()],
        [part, part],
        [shape((tiles, wide, hidden), low_type)] * 2,
        weight.scratch(),
    )(near, far, one, two, *weight.values())


def put_blocks(total, out_refs):
    for index, out_ref in enumerate(out_refs):
        out_ref[...] = total[index].astype(out_ref.dtype)


def block_outputs(per, width, step):
    spec = pl.BlockSpec((per, step), lambda n: (0, n))
    kinds = (wide_type, low_type, low_type, low_type)
    return [spec] * 4, [shape((per, width), kind) for kind in kinds]


def combine_body(near_ref, got_ref, *out_refs):
    put_blocks(near_ref[...].astype(wide_type) + got_ref[...].astype(wide_type), out_refs)


def combine(near, got):
    blocks, per, width = near.shape
    step = 512
    spec = pl.BlockSpec((blocks, per, step), lambda n: (0, 0, n))
    out_specs, out_shape = block_outputs(per, width, step)
    return call(combine_body, (width // step,), [spec, spec], out_specs, out_shape)(near, got)


def branch_body(lefts, count, with_got, *refs):
    left_refs, refs = refs[:lefts], refs[lefts:]
    pieces, refs = [refs[i * count : (i + 1) * count] for i in range(lefts)], refs[lefts * count :]
    got_ref, refs = (refs[0], refs[1:]) if with_got else (None, refs)
    outs, scratch = refs[: -2 * lefts], refs[-2 * lefts :]
    step = outs[0].shape[-1]

    @pl.when(pl.program_id(0) == 0)
    def _():
        for index in range(lefts):
            load_pieces(pieces[index], scratch[2 * index : 2 * index + 2])

    start = pl.multiple_of(pl.program_id(0) * step, step)
    total = None
    for index in range(lefts):
        left = left_refs[index][...]
        rows = left.shape[0] * left.shape[2]
        weight = scratch[2 * index][pl.ds(start, step), :]
        term = dot(left.reshape(rows, left.shape[3]), weight, 1, 1)
        total = term if total is None else total + term
    total = total.reshape(4, total.shape[0] // 4, step)
    if got_ref is None:
        outs[0][...] = total.astype(low_type)
    else:
        put_blocks(total + got_ref[...].astype(wide_type), outs)


def branch(pairs, core, got=None):
    step = 512
    specs, lefts, weight_specs, weights, scratch = [], [], [], [], []
    for left, weight in pairs:
        tiles, wide, inner = left.shape
        lefts.append(left.reshape(tiles, 2, wide // 2, inner))
        specs.append(pl.BlockSpec((tiles, 1, wide // 2, inner), lambda n: (0, core, 0, 0)))
        weight_specs += weight.specs()
        weights += weight.values()
        scratch += weight.scratch()
    width = 2 * len(weight.blocks) * weight.rows
    per = wide // 2
    block = pl.BlockSpec((tiles, per, step), lambda n: (0, 0, n))
    if got is None:
        out_specs, out_shape = [block], [shape((tiles, per, width), low_type)]
    else:
        out_specs, out_shape = block_outputs(per, width, step)
    outs = call(
        functools.partial(branch_body, len(pairs), weight.count(), got is not None),
        (width // step,),
        specs + weight_specs + ([] if got is None else [block]),
        out_specs,
        out_shape,
        scratch,
    )(*lefts, *weights, *([] if got is None else [got]))
    return outs[0] if got is None else outs


def weight_body(count, index_ref, first_ref, second_ref, right_ref, *refs):
    left = jnp.concatenate([first_ref[0], second_ref[0]], axis=0)
    total = dot(left, right_ref[...], 1, 0)
    rows = total.shape[0] // 2
    for part in range(2):
        block = total[part * rows : (part + 1) * rows]
        for position in range(count):
            block = block + refs[2 * position + part][0].astype(wide_type)
        refs[-1][part] = block.astype(refs[-1].dtype)


def weight_rows(turned, right, places, addends, kind):
    tokens = turned.shape[1]
    columns = right.shape[-1]
    blocks = lax.axis_size("dp")
    rows = turned.shape[0] // blocks
    number = len(places)
    flat = [jnp.asarray(p, jnp.int32) for p in places]

    def named(offset, part, last):
        return pl.BlockSpec(
            (1, rows, last), lambda i, index: (index[offset + 2 * i + part], 0, 0)
        )

    specs = [
        named(0, 0, tokens),
        named(0, 1, tokens),
        pl.BlockSpec((tokens, columns), lambda i, index: (0, 0)),
    ]
    given = []
    for position, (array, where) in enumerate(addends):
        flat += [jnp.asarray(p, jnp.int32) for p in where]
        for part in range(2):
            specs.append(named((position + 1) * number, part, columns))
            given.append(array)
    left = turned.reshape(blocks, rows, tokens)
    return pl.pallas_call(
        functools.partial(weight_body, len(addends)),
        grid_spec=pltpu.PrefetchScalarGridSpec(
            num_scalar_prefetch=1,
            grid=(number // 2,),
            in_specs=specs,
            out_specs=pl.BlockSpec((2, rows, columns), lambda i, index: (i, 0, 0)),
        ),
        out_shape=shape((number, rows, columns), kind),
        compiler_params=pltpu.CompilerParams(vmem_limit_bytes=VMEM_LIMIT),
        cost_estimate=pl.CostEstimate(flops=0, bytes_accessed=0, transcendentals=0),
    )(jnp.stack(flat), left, left, right.reshape(tokens, columns), *given)


def share_first(turned, right):
    _, _, y, _, _ = bits()
    ring = lax.axis_size("dp") // 4
    places = [4 * g + 2 * b + (1 - y) for g in range(ring) for b in range(2)]
    return weight_rows(turned, right, places, [], low_type)


def share_term(turned, right, got, step, travel=None):
    h, l, y, _, _ = bits()
    ring = lax.axis_size("dp") // 4
    group = (h - 1 - step) % ring
    last = step == ring - 1
    order = [l, 1 - l] if last else [0, 1]
    places = [4 * group + 2 * b + y for b in order]
    addends = [(got, [2 * group + b for b in order])]
    if travel is not None:
        addends.append((travel, order))
    return weight_rows(turned, right, places, addends, wide_type if last else low_type)


def share_rest(turned, right, got, term):
    ring = lax.axis_size("dp") // 4
    travel = hop_ring(term)
    for step in range(1, ring - 1):
        travel = hop_ring(share_term(turned, right, got, step, travel))
    return travel


def share_third(turned, right, got, travel):
    ring = lax.axis_size("dp") // 4
    own = share_term(turned, right, got, ring - 1, travel)
    return own[0], own[1].astype(low_type)


def adamw(param, grad, first, second):
    first_new = beta_first * first + (1.0 - beta_first) * grad
    second_new = beta_second * second + (1.0 - beta_second) * grad * grad
    first_hat = first_new / (1.0 - beta_first**STEP)
    second_hat = second_new / (1.0 - beta_second**STEP)
    change = -learn_rate * (first_hat / (jnp.sqrt(second_hat) + adam_eps) + weight_decay * param)
    return (first_new, second_new, change)


def on_device(
    tokens,
    upstream,
    offsets,
    query_weight,
    keyval_weight,
    output_weight,
    gateup_weight,
    down_weight,
    norm_gains,
    first_query,
    first_keyval,
    first_output,
    first_gateup,
    first_down,
    first_gains,
    second_query,
    second_keyval,
    second_output,
    second_gateup,
    second_down,
    second_gains,
):
    h, l, y, xbit, cbit = bits()
    pin = Windows(norm_gains)
    ring = lax.axis_size("dp") // 4
    block_rows = offsets.shape[0]
    per, width = tokens.shape
    wide = 2 * per

    def split(bit, arrays, more=()):
        lower, upper = [], []
        for array in arrays:
            half = array.shape[-1] // 2
            lower.append(array[:, :half].astype(low_type))
            upper.append(array[:, half:].astype(low_type))
        lower = jnp.concatenate([*lower, *more], axis=1)
        upper = jnp.concatenate([*upper, *more], axis=1)
        return choose(bit, lower, upper), choose(bit, upper, lower)

    def paired(own, other):
        return ordered(l, own[None], other[None], 0)

    places = jnp.stack(
        [
            4 * ((h - step) % ring) + 2 * b + (y ^ flip)
            for step in range(ring)
            for flip in range(2)
            for b in range(2)
        ]
    ).astype(jnp.int32)

    def legs(pair, pair_y, rings, rings_y):
        blocks = [pair, pair_y]
        for block, block_y in zip(rings, rings_y):
            blocks += [block, block_y]
        return Pieces(blocks, places)

    def arrived(own, *others):
        for other in others:
            own = own + other.astype(wide_type)
        return own

    def onward(block, corner):
        return (block.astype(wide_type) + corner.astype(wide_type)).astype(low_type)

    gain_columns = norm_gains.astype(low_type).T
    q_own, q_other = split(
        l, [query_weight, keyval_weight[0], keyval_weight[1]], [gain_columns]
    )
    o_own, o_other = split(l, [output_weight])
    q_other, o_other, other_offsets = hop_low(q_other), hop_low(o_other), hop_low(offsets)

    q_other, o_other, other_offsets, bit, own_rows = pin(
        q_other, o_other, other_offsets, l, tokens
    )
    q_pair = paired(q_own, q_other)
    q_ring, q_y = hop_ring(q_pair), hop_y(q_pair)
    tx, tz = hop_x(own_rows), hop_low(own_rows)
    o_pair = paired(o_own, o_other)
    g_own, g_other = halves(bit, gateup_weight, 0)

    def relative(own):
        four = own.reshape(2, 2, per)
        four = choose(xbit, four, four[::-1])
        return choose(cbit, four, four[:, ::-1])

    offset_tiles = jnp.concatenate([relative(offsets), relative(other_offsets)], axis=0)
    offset_tiles = offset_tiles.reshape(4, wide)
    lane = jnp.arange(wide, dtype=jnp.int32)
    local = choose(cbit, lane, lane ^ per)
    mine = jnp.arange(4, dtype=jnp.int32)

    def bases(group_h, group_y, low_bits, x_bits):
        block = 4 * group_h + 2 * low_bits + group_y
        return block * block_rows + x_bits * wide

    low_bits, x_bits = l ^ (mine // 2), xbit ^ (mine % 2)
    own_base = bases(h, y, low_bits, x_bits)
    one = jnp.ones((2,), jnp.int32)
    key_base = jnp.concatenate(
        [
            own_base,
            bases(h, 1 - y, low_bits, x_bits),
            bases(h - 1, y, one, x_bits[:2]),
            bases(h - 1, 1 - y, one, x_bits[:2]),
        ]
    ).astype(jnp.int32)
    query_pos = own_base[:, None] + local[None, :]
    doc_start = query_pos - offset_tiles
    seen = (
        (key_base[None, :] <= own_base[:, None] + wide - 1)
        & (key_base[None, :] + wide - 1 >= jnp.min(doc_start, axis=1, keepdims=True))
    ).astype(jnp.int32).reshape(-1)
    spread = lambda a: jnp.tile(a, (1, GROUP)).reshape(4, 1, GROUP * wide)
    query_lanes, start_lanes = spread(query_pos), spread(doc_start)
    local_column = local.reshape(wide, 1)
    freqs = rope_base ** (-(jnp.arange(HALF).astype(wide_type) * 2.0 / HEAD_SIZE))
    angle = freqs[None, :, None] * offset_tiles.astype(wide_type)[:, None, :]
    cos, sin = jnp.cos(angle), jnp.sin(angle)

    tx, tz, g_other = pin(tx, tz, g_other)
    tf = hop_x(tz)
    g_other = hop_low(g_other)

    tf, q_y, bit, up_own = pin(tf, q_y, bit, upstream)
    near = pack(own_rows, tx, tz, tf)
    far = hop_core(near)
    u_own, u_other = halves(bit, gateup_weight, 1)

    far, q_ring, g_other, u_other, o_pair, up_own = pin(
        far, q_ring, g_other, u_other, o_pair, up_own
    )
    q_far = rest_of_ring(q_ring)
    q_far_y = [hop_y(block) for block in q_far]
    o_ring = hop_ring(o_pair)
    u_other = hop_low(u_other)
    ux = hop_x(up_own)
    g_pair = paired(g_own, g_other)

    up_own, o_pair, *q_far_y = pin(up_own, o_pair, *q_far_y)
    qkv_full = legs(q_pair, q_y, q_far, q_far_y)
    turned_one, q_turned, kv_own, gains = project(near, far, qkv_full, cos, sin)
    uz, o_y = hop_low(up_own), hop_y(o_pair)

    kv_own, o_y, o_ring, u_other, ux, bit = pin(kv_own, o_y, o_ring, u_other, ux, bit)
    late = choose(l, kv_own[2:], kv_own[:2])
    kv_a, kv_b, kv_y = to_next(late, 0), to_next(late, 1), hop_y(kv_own)
    o_far = rest_of_ring(o_ring)
    o_far_y = [hop_y(block) for block in o_far]
    d_own, d_other = halves(bit, down_weight)
    u_pair = paired(u_own, u_other)

    kv_y, kv_a, kv_b, uz, g_pair, d_other, *o_far_y = pin(
        kv_y, kv_a, kv_b, uz, g_pair, d_other, *o_far_y
    )
    g_ring, g_y = hop_ring(g_pair), hop_y(g_pair)
    d_other = hop_low(d_other)
    uf = hop_x(uz)
    output_full = legs(o_pair, o_y, o_far, o_far_y)
    layout = (seen, key_base, q_turned, query_lanes, start_lanes, local_column)
    kv = (kv_own, kv_y, kv_a, kv_b)
    attended, out_turned, lse, branch_near, branch_far = attend(layout, kv, output_full)
    z_got = hop_core(branch_far)

    z_got, g_y, uf, u_pair = pin(z_got, g_y, uf, u_pair)
    z_own, z_x, z_low, z_corner = combine(branch_near, z_got)
    zc, zx = hop_x(z_corner), hop_x(z_x)
    u_y = hop_y(u_pair)
    inputs = tokens.astype(wide_type)
    inverse_one = lax.rsqrt(jnp.mean(inputs * inputs, axis=-1, keepdims=True) + eps_norm)
    unit_one = inputs * inverse_one

    zc, g_ring, u_pair, uf = pin(zc, g_ring, u_pair, uf)
    zz = hop_low(onward(z_low, zc))
    g_far = rest_of_ring(g_ring)
    u_ring = hop_ring(u_pair)
    near_up = pack(up_own, ux, uz, uf)

    zx, zz, u_y, near_up, d_other = pin(zx, zz, u_y, near_up, d_other)
    g_far_y = [hop_y(block) for block in g_far]
    middle = inputs + arrived(z_own, zx, zz)
    inverse_two = lax.rsqrt(jnp.mean(middle * middle, axis=-1, keepdims=True) + eps_norm)
    unit_two = middle * inverse_two
    own_two = (unit_two * gains[1]).astype(low_type)
    az, ax = hop_low(own_two), hop_x(own_two)
    far_up = hop_core(near_up)
    d_pair = paired(d_own, d_other)

    ax, az, d_pair, far_up = pin(ax, az, d_pair, far_up)
    af = hop_x(az)
    d_y = hop_y(d_pair)

    af, *g_far_y = pin(af, *g_far_y)
    gate_full = legs(g_pair, g_y, g_far, g_far_y)
    near_two = pack(own_two, ax, az, af)
    far_two = hop_core(near_two)

    far_two, u_ring, d_y, d_pair = pin(far_two, u_ring, d_y, d_pair)
    u_far = rest_of_ring(u_ring)
    u_far_y = [hop_y(block) for block in u_far]
    d_ring = hop_ring(d_pair)
    turned_up = turn(near_up, far_up)

    turned_up, *u_far_y = pin(turned_up, *u_far_y)
    up_full = legs(u_pair, u_y, u_far, u_far_y)
    turned_two, hidden, first_factor, second_factor = ffn(
        near_two, far_two, gate_full, up_full
    )
    down_first = share_first(turned_up, hidden)

    d_ring, down_first = pin(d_ring, down_first)
    d_far = rest_of_ring(d_ring)
    d_far_y = [hop_y(block) for block in d_far]

    down_first, hidden, *d_far_y = pin(down_first, hidden, *d_far_y)
    down_sent = hop_y(down_first)
    down_full = legs(d_pair, d_y, d_far, d_far_y)
    grad_gate, grad_up = ffn_back(near_up, far_up, down_full, first_factor, second_factor)
    ffn_pairs = [(grad_gate, gate_full), (grad_up, up_full)]
    s_got = hop_core(branch(ffn_pairs, 1))
    gate_first = share_first(turned_two, grad_gate)

    s_got, grad_up, gate_first = pin(s_got, grad_up, gate_first)
    s_own, s_x, s_low, s_corner = branch(ffn_pairs, 0, s_got)
    sc, sx = hop_x(s_corner), hop_x(s_x)

    sc, grad_up = pin(sc, grad_up)
    sz = hop_low(onward(s_low, sc))
    up_first = share_first(turned_two, grad_up)

    sx, sz, down_got, gate_first, up_first, hidden = pin(
        sx, sz, down_sent, gate_first, up_first, hidden
    )
    grad_normed_two = arrived(s_own, sx, sz)
    gain_two = jnp.sum(grad_normed_two * unit_two, axis=0)
    grad_middle = upstream.astype(wide_type) + norm_back(
        grad_normed_two, unit_two, inverse_two, gains[1]
    )
    own_three = grad_middle.astype(low_type)
    bz, bx = hop_low(own_three), hop_x(own_three)
    gate_sent = hop_y(gate_first)
    down_travel = share_rest(
        turned_up, hidden, down_got, share_term(turned_up, hidden, down_got, 0)
    )

    bx, bz = pin(bx, bz)
    bf = hop_x(bz)

    (bf,) = pin(bf)
    near_three = pack(own_three, bx, bz, bf)
    far_three = hop_core(near_three)

    far_three, gate_got, down_travel, up_first, grad_gate = pin(
        far_three, gate_sent, down_travel, up_first, grad_gate
    )
    up_sent = hop_y(up_first)
    gate_travel = share_rest(
        turned_two, grad_gate, gate_got, share_term(turned_two, grad_gate, gate_got, 0)
    )
    dq_turned, dkv_own, dkv_y, dkv_a, dkv_b = attend_back(
        layout, kv, output_full, near_three, far_three, out_turned, lse, cos, sin
    )

    dkv_y, dkv_a, dkv_b, near_three = pin(dkv_y, dkv_a, dkv_b, near_three)
    dkv_a, dkv_b, dkv_y = to_previous(dkv_a, 0), to_previous(dkv_b, 1), hop_y(dkv_y)
    turned_three = turn(near_three, far_three)
    output_first = share_first(turned_three, attended)

    dkv_y, dkv_a, dkv_b, output_first = pin(dkv_y, dkv_a, dkv_b, output_first)
    dqkv = finish(
        (1 - l).astype(jnp.int32).reshape(1), dq_turned, dkv_own, dkv_y, dkv_a, dkv_b, cos, sin
    )
    attn_pairs = [(dqkv, qkv_full)]
    r_got = hop_core(branch(attn_pairs, 1))
    output_sent = hop_y(output_first)
    qkv_sent = hop_y(share_first(turned_one, dqkv))

    r_got, up_got, gate_travel, hidden = pin(r_got, up_sent, gate_travel, hidden)
    r_own, r_x, r_low, r_corner = branch(attn_pairs, 0, r_got)
    rc, rx = hop_x(r_corner), hop_x(r_x)
    up_travel = share_rest(
        turned_two, grad_up, up_got, share_term(turned_two, grad_up, up_got, 0)
    )

    rc, output_got, hidden = pin(rc, output_sent, hidden)
    rz = hop_low(onward(r_low, rc))
    output_term = share_term(turned_three, attended, output_got, 0)
    down_mine, down_theirs = share_third(turned_up, hidden, down_got, down_travel)

    rx, rz, qkv_got, output_term, down_theirs, hidden = pin(
        rx, rz, qkv_sent, output_term, down_theirs, hidden
    )
    output_travel = share_rest(turned_three, attended, output_got, output_term)
    qkv_travel = share_rest(
        turned_one, dqkv, qkv_got, share_term(turned_one, dqkv, qkv_got, 0)
    )
    down_other = hop_low(down_theirs)
    down_pairs = [(hidden, down_full)]
    f_got = hop_core(branch(down_pairs, 1))
    gate_mine, gate_theirs = share_third(turned_two, grad_gate, gate_got, gate_travel)
    grad_normed_one = arrived(r_own, rx, rz)
    gain_one = jnp.sum(grad_normed_one * unit_one, axis=0)
    grad_tokens = grad_middle + norm_back(grad_normed_one, unit_one, inverse_one, gains[0])

    f_got, up_travel, gate_theirs, down_other = pin(f_got, up_travel, gate_theirs, down_other)
    gate_other = hop_low(gate_theirs)
    f_own, f_x, f_low, f_corner = branch(down_pairs, 0, f_got)
    fc, fx = hop_x(f_corner), hop_x(f_x)
    up_mine, up_theirs = share_third(turned_two, grad_up, up_got, up_travel)

    output_travel, qkv_travel, up_theirs, gate_other, fc = pin(
        output_travel, qkv_travel, up_theirs, gate_other, fc
    )
    qkv_mine, qkv_theirs = share_third(turned_one, dqkv, qkv_got, qkv_travel)
    qkv_other = hop_low(qkv_theirs)
    output_mine, output_theirs = share_third(turned_three, attended, output_got, output_travel)
    output_other = hop_low(output_theirs)
    up_other = hop_low(up_theirs)
    fz = hop_low(onward(f_low, fc))
    block_out = (middle + arrived(f_own, fx, fz)).astype(low_type)

    def joined(mine, other, start, stop):
        return ordered(l, mine[:, start:stop], other[:, start:stop].astype(wide_type), 1)

    edge_one = QROWS + HEAD_SIZE
    hidden_part = down_mine.shape[1]
    grad_query = joined(qkv_mine, qkv_other, 0, QROWS)
    grad_keyval = jnp.stack(
        [
            joined(qkv_mine, qkv_other, QROWS, edge_one),
            joined(qkv_mine, qkv_other, edge_one, EDGE),
        ]
    )
    grad_output = joined(output_mine, output_other, 0, QROWS)
    grad_gateup = jnp.stack(
        [
            joined(gate_mine, gate_other, 0, hidden_part),
            joined(up_mine, up_other, 0, hidden_part),
        ]
    )
    grad_down = joined(down_mine, down_other, 0, hidden_part)
    shares = (
        down_mine, down_other, gate_mine, gate_other, up_mine, up_other,
        output_mine, output_other, qkv_mine, qkv_other,
    )
    squares = [jnp.sum(jnp.square(part.astype(wide_type))) for part in shares]
    square_row = jnp.full((1, width), functools.reduce(jnp.add, squares) / width)
    totals = sum_all(jnp.concatenate([gain_one[None], gain_two[None], square_row], axis=0))
    gain_total = totals[:2]
    grad_norm = jnp.sqrt(totals[2, 0] * width + jnp.sum(gain_total * gain_total))
    rows_owned = query_weight.shape[0]
    grad_gains = lax.dynamic_slice_in_dim(
        gain_total, lax.axis_index("dp") * rows_owned, rows_owned, 1
    )
    clipping_bound = math.sqrt(
        MODEL_WIDTH
        * (2 * QUERY_HEAD_COUNT * HEAD_SIZE + 2 * KEY_VALUE_HEADS * HEAD_SIZE + 3 * HIDDEN_UNITS)
        + 2 * MODEL_WIDTH
    )
    clip = jnp.minimum(1.0, clipping_bound / (grad_norm + 1e-06))
    params = (query_weight, keyval_weight, output_weight, gateup_weight, down_weight, pin.held)
    firsts = (first_query, first_keyval, first_output, first_gateup, first_down, first_gains)
    seconds = (second_query, second_keyval, second_output, second_gateup, second_down, second_gains)
    grads = (grad_query, grad_keyval, grad_output, grad_gateup, grad_down, grad_gains)
    states = [
        adamw(params[index], grads[index] * clip, firsts[index], seconds[index])
        for index in range(6)
    ]
    return (
        block_out,
        grad_tokens,
        grad_norm,
        *grads,
        *[state[0] for state in states],
        *[state[1] for state in states],
        *[state[2] for state in states],
    )


def solution(mesh):
    weights = (
        P("dp", "mp"),
        P(None, "dp", "mp"),
        P("dp", "mp"),
        P(None, "dp", "mp"),
        P("dp", "mp"),
        P(None, "dp"),
    )
    rows = P(("dp", "mp"), None)
    return jax.shard_map(
        on_device,
        mesh=mesh,
        in_specs=(rows, rows, P("dp"), *weights, *weights, *weights),
        out_specs=(rows, rows, P(), *weights, *weights, *weights, *weights),
        check_vma=False,
    )
```

```python
import functools
import math

import jax
import jax.numpy as jnp
from jax import lax
from jax.experimental import pallas as pl
from jax.experimental.pallas import tpu as pltpu
from jax.sharding import PartitionSpec as P

MODEL_WIDTH = 2560
QUERY_HEAD_COUNT = 32
KEY_VALUE_HEADS = 8
HEAD_SIZE = 80
HIDDEN_UNITS = 7168
STEP = 10

eps_norm = 1e-05
rope_base = 1000000.0
beta_first = 0.9
beta_second = 0.95
learn_rate = 0.02
weight_decay = 0.1
adam_eps = 1e-08
masked_score = -1e30

low_type = jnp.bfloat16
wide_type = jnp.float32

HALF = HEAD_SIZE // 2
GROUP = QUERY_HEAD_COUNT // KEY_VALUE_HEADS
QROWS = GROUP * HEAD_SIZE
BOTH = 2 * HEAD_SIZE
EDGE = QROWS + BOTH
EXP_SCALE = (HEAD_SIZE ** (-0.5)) * math.log2(math.e)
SCALE = HEAD_SIZE ** (-0.5)
AXES = ("dp", "mp")


def hop(block, move):
    dp_size, mp_size = lax.axis_size("dp"), lax.axis_size("mp")
    route = []
    for d in range(dp_size):
        for m in range(mp_size):
            target = move(d, m)
            if target is not None:
                route.append((d * mp_size + m, target[0] * mp_size + target[1]))
    return lax.ppermute(block, AXES, route)


def hop_core(block):
    return hop(block, lambda d, m: (d, m ^ 1))


def hop_x(block):
    return hop(block, lambda d, m: (d, m ^ 2))


def hop_low(block):
    return hop(block, lambda d, m: (d ^ 2, m))


def hop_y(block):
    return hop(block, lambda d, m: (d ^ 1, m))


def hop_ring(block):
    size = lax.axis_size("dp")
    return hop(block, lambda d, m: ((d + 4) % size, m))


def to_next(block, flip):
    size = lax.axis_size("dp")

    def move(d, m):
        if d + 4 >= size or (flip and d % 2 == 0):
            return None
        return (d + 4) ^ flip, m

    return hop(block, move)


def to_previous(block, flip):
    def move(d, m):
        if d < 4 or (flip and d % 2 == 1):
            return None
        return (d - 4) ^ flip, m

    return hop(block, move)


def bits():
    d = lax.axis_index("dp")
    m = lax.axis_index("mp")
    return d // 4, (d // 2) % 2, d % 2, m // 2, m % 2


def choose(bit, if_zero, if_one):
    return jnp.where(bit == 0, if_zero, if_one)


def ordered(bit, mine, other, axis):
    return choose(
        bit,
        jnp.concatenate([mine, other], axis=axis),
        jnp.concatenate([other, mine], axis=axis),
    )


def keep_body(held_ref, out_ref):
    out_ref[...] = held_ref[...]


class Windows:
    def __init__(self, held):
        self.held = held

    def __call__(self, *arrays):
        *given, held = lax.optimization_barrier((*arrays, self.held))
        self.held = pl.pallas_call(
            keep_body,
            out_shape=jax.ShapeDtypeStruct(held.shape, held.dtype),
            cost_estimate=pl.CostEstimate(flops=10**12, bytes_accessed=0, transcendentals=0),
        )(held)
        return given

    def apart(self, *arrays):
        self.held = hop_core(self.held)
        return self(*arrays)


def rest_of_ring(first):
    blocks = [first]
    for _ in range(lax.axis_size("dp") // 4 - 2):
        blocks.append(hop_ring(blocks[-1]))
    return blocks


def sum_rest(value):
    ring = lax.axis_size("dp") // 4
    for step in (hop_low, hop_y):
        value = value + step(value)
    travel = value
    for _ in range(1, ring):
        travel = hop_ring(travel)
        value = value + travel
    return value


def norm_back(incoming, unit_rows, inverse_root, gain):
    scaled = incoming * gain
    return inverse_root * (
        scaled - unit_rows * jnp.mean(scaled * unit_rows, axis=-1, keepdims=True)
    )


VMEM_LIMIT = 56 * 2**20


def call(body, grid, in_specs, out_specs, out_shape, scratch=(), flops=10**10):
    return pl.pallas_call(
        body,
        grid=grid,
        in_specs=in_specs,
        out_specs=out_specs,
        out_shape=out_shape,
        scratch_shapes=list(scratch),
        compiler_params=pltpu.CompilerParams(vmem_limit_bytes=VMEM_LIMIT),
        cost_estimate=pl.CostEstimate(flops=flops, bytes_accessed=0, transcendentals=0),
    )


def shape(dims, kind):
    return jax.ShapeDtypeStruct(dims, kind)


def whole(array):
    zeros = (0,) * array.ndim
    return pl.BlockSpec(array.shape, lambda *_: zeros)


def tile_of(*dims):
    rest = (0,) * (len(dims) - 1)
    return pl.BlockSpec(dims, lambda t: (t, *rest))


def dot(left, right, left_dim, right_dim):
    return lax.dot_general(
        left, right, (((left_dim,), (right_dim,)), ((), ())), preferred_element_type=wide_type
    )


def any_spec():
    return pl.BlockSpec(memory_space=pl.ANY)


def smem_spec():
    return pl.BlockSpec(memory_space=pltpu.SMEM)


class Pieces:
    def __init__(self, blocks, places):
        self.blocks = blocks
        self.places = places
        _, self.rows, self.columns = blocks[0].shape

    def count(self):
        return 1 + len(self.blocks)

    def specs(self):
        return [smem_spec()] + [any_spec()] * len(self.blocks)

    def values(self):
        return [self.places, *self.blocks]

    def scratch(self):
        number = 2 * len(self.blocks)
        return [
            pltpu.VMEM((number * self.rows, self.columns), low_type),
            pltpu.SemaphoreType.DMA((number,)),
        ]


def load_pieces(refs, scratch):
    place_ref, *block_refs = refs
    weight_ref, sem_ref = scratch
    copies = []
    for index, block_ref in enumerate(block_refs):
        rows = block_ref.shape[1]
        for part in range(2):
            number = 2 * index + part
            start = pl.multiple_of(place_ref[number] * rows, rows & -rows)
            copies.append(
                pltpu.make_async_copy(
                    block_ref.at[part], weight_ref.at[pl.ds(start, rows)], sem_ref.at[number]
                )
            )
    for copy in copies:
        copy.start()
    for copy in copies:
        copy.wait()


def halves_body(bit_ref, weight_ref, own_ref, other_ref):
    size = own_ref.shape[1]
    for out_ref, which in ((own_ref, bit_ref[0]), (other_ref, 1 - bit_ref[0])):
        start = pl.multiple_of(which * size, size & -size)
        out_ref[...] = weight_ref[:, pl.ds(start, size)].astype(low_type)


def halves(bit, weight, layer=None):
    rows, columns = weight.shape[-2:]
    step = rows // 5
    if layer is None:
        spec = pl.BlockSpec((step, columns), lambda i: (i, 0))
    else:
        spec = pl.BlockSpec((pl.squeezed, step, columns), lambda i: (layer, i, 0))
    half = pl.BlockSpec((step, columns // 2), lambda i: (i, 0))
    return call(
        halves_body,
        (5,),
        [smem_spec(), spec],
        [half, half],
        [shape((rows, columns // 2), low_type)] * 2,
    )(bit.astype(jnp.int32).reshape(1), weight)


def pack_body(*refs):
    *parts, out_ref = refs
    start = 0
    for part in parts:
        if len(part.shape) == 2:
            out_ref[start] = part[...]
            start += 1
        else:
            out_ref[start : start + part.shape[0]] = part[...]
            start += part.shape[0]


def pack(*parts):
    rows, width = parts[0].shape[-2:]
    step = width // 4
    specs, number = [], 0
    for part in parts:
        if part.ndim == 2:
            specs.append(pl.BlockSpec((rows, step), lambda n: (0, n)))
            number += 1
        else:
            specs.append(pl.BlockSpec((part.shape[0], rows, step), lambda n: (0, 0, n)))
            number += part.shape[0]
    return call(
        pack_body,
        (4,),
        specs,
        pl.BlockSpec((number, rows, step), lambda n: (0, 0, n)),
        shape((number, rows, width), parts[0].dtype),
    )(*parts)


def both_cores(near_ref, far_ref):
    return jnp.concatenate([near_ref[0], far_ref[0]], axis=0)


def project_body(count, x_ref, xc_ref, cos_ref, sin_ref, *refs):
    pieces = refs[:count]
    at_ref, q_ref, kv_ref, g_ref, w_ref, sem_ref = refs[count:]

    @pl.when(pl.program_id(0) == 0)
    def _():
        load_pieces(pieces, (w_ref, sem_ref))
        turned = w_ref[:, 384:].astype(wide_type).T
        g_ref[...] = turned[EDGE - 384 : EDGE - 384 + 2]

    x = both_cores(x_ref, xc_ref).astype(wide_type)
    rows = x.shape[0]
    unit = x * lax.rsqrt(jnp.mean(x * x, axis=-1, keepdims=True) + eps_norm)
    normed = (unit * g_ref[0:1]).astype(low_type)
    at_ref[...] = normed.T
    flat = dot(w_ref[...], normed, 0, 1)
    cos, sin = cos_ref[0], sin_ref[0]

    def rotated(start):
        first = flat[start : start + HALF]
        second = flat[start + HALF : start + HEAD_SIZE]
        return jnp.concatenate(
            [first * cos - second * sin, second * cos + first * sin], axis=0
        ).astype(low_type)

    for head in range(GROUP):
        q_ref[0, :, head * rows : (head + 1) * rows] = rotated(head * HEAD_SIZE)
    kv_ref[0] = jnp.concatenate(
        [rotated(QROWS), flat[QROWS + HEAD_SIZE : EDGE].astype(low_type)], axis=0
    )


def project(near, far, weight, cos, sin):
    tiles, per, width = near.shape
    wide = 2 * per
    return call(
        functools.partial(project_body, weight.count()),
        (tiles,),
        [
            tile_of(1, per, width),
            tile_of(1, per, width),
            tile_of(1, HALF, wide),
            tile_of(1, HALF, wide),
            *weight.specs(),
        ],
        [
            pl.BlockSpec((width, wide), lambda t: (0, t)),
            tile_of(1, HEAD_SIZE, GROUP * wide),
            tile_of(1, BOTH, wide),
            pl.BlockSpec((2, width), lambda t: (0, 0)),
        ],
        [
            shape((width, tiles * wide), low_type),
            shape((tiles, HEAD_SIZE, GROUP * wide), low_type),
            shape((tiles, BOTH, wide), low_type),
            shape((2, width), wide_type),
        ],
        weight.scratch(),
    )(near, far, cos, sin, *weight.values())


def load_keys(kv_refs, kv_ref, sem_ref):
    copies, start = [], 0
    for index, part in enumerate(kv_refs):
        size = part.shape[0]
        copies.append(
            pltpu.make_async_copy(part, kv_ref.at[start : start + size], sem_ref.at[index])
        )
        start += size
    for copy in copies:
        copy.start()
    for copy in copies:
        copy.wait()


def attend_body(count, seen_ref, base_ref, q_ref, pos_ref, start_ref, local_ref, *refs):
    kv_parts, pieces = refs[:4], refs[4 : 4 + count]
    o_ref, ot_ref, lse_ref, near_ref, far_ref = refs[4 + count : 9 + count]
    top_ref, sum_ref, acc_ref, kv_ref, kv_sem, w_ref, sem_ref = refs[9 + count :]
    tile = pl.program_id(0)
    key_tiles = kv_ref.shape[0]

    @pl.when(tile == 0)
    def _():
        load_keys(kv_parts, kv_ref, kv_sem)
        load_pieces(pieces, (w_ref, sem_ref))

    top_ref[...] = jnp.full(top_ref.shape, masked_score, wide_type)
    sum_ref[...] = jnp.zeros(sum_ref.shape, wide_type)
    acc_ref[...] = jnp.zeros(acc_ref.shape, wide_type)

    def step(k, carry):
        @pl.when(seen_ref[tile * key_tiles + k] != 0)
        def _():
            raw = dot(kv_ref[k, :HEAD_SIZE], q_ref[0], 0, 0)
            key_pos = base_ref[k] + local_ref[...]
            allowed = (key_pos <= pos_ref[0]) & (key_pos >= start_ref[0])
            raw = jnp.where(allowed, raw, masked_score)
            top_old = top_ref[...]
            top = jnp.maximum(top_old, jnp.max(raw, axis=0, keepdims=True))
            shrink = jnp.exp2((top_old - top) * EXP_SCALE)
            probs = jnp.where(allowed, jnp.exp2((raw - top) * EXP_SCALE), 0.0)
            sum_ref[...] = sum_ref[...] * shrink + jnp.sum(probs, axis=0, keepdims=True)
            acc_ref[...] = acc_ref[...] * shrink + dot(
                kv_ref[k, HEAD_SIZE:], probs.astype(low_type), 1, 0
            )
            top_ref[...] = top

        return carry

    lax.fori_loop(0, key_tiles, step, 0)
    out = acc_ref[...] / sum_ref[...]
    ot_ref[0] = out
    lse_ref[0] = top_ref[...] * EXP_SCALE + jnp.log2(sum_ref[...])
    rows = out.shape[1] // GROUP
    stacked = jnp.concatenate(
        [out[:, head * rows : (head + 1) * rows] for head in range(GROUP)], axis=0
    )
    attended = stacked.T.astype(low_type)
    o_ref[0] = attended
    branch = dot(attended, w_ref[...], 1, 1)
    near_ref[0] = branch[: rows // 2].astype(low_type)
    far_ref[0] = branch[rows // 2 :].astype(low_type)


def key_scratch(kv):
    number = sum(part.shape[0] for part in kv)
    return [
        pltpu.VMEM((number, *kv[0].shape[1:]), low_type),
        pltpu.SemaphoreType.DMA((len(kv),)),
    ]


def attend(layout, kv, weight):
    seen, base, q, pos, start, local = layout
    tiles, _, columns = q.shape
    wide = kv[0].shape[2]
    width = 2 * len(weight.blocks) * weight.rows
    return call(
        functools.partial(attend_body, weight.count()),
        (tiles,),
        [
            smem_spec(),
            smem_spec(),
            tile_of(1, HEAD_SIZE, columns),
            tile_of(1, 1, columns),
            tile_of(1, 1, columns),
            whole(local),
            *[any_spec()] * 4,
            *weight.specs(),
        ],
        [
            tile_of(1, wide, QROWS),
            tile_of(1, HEAD_SIZE, columns),
            tile_of(1, 1, columns),
            tile_of(1, wide // 2, width),
            tile_of(1, wide // 2, width),
        ],
        [
            shape((tiles, wide, QROWS), low_type),
            shape((tiles, HEAD_SIZE, columns), wide_type),
            shape((tiles, 1, columns), wide_type),
            shape((tiles, wide // 2, width), low_type),
            shape((tiles, wide // 2, width), low_type),
        ],
        [
            pltpu.VMEM((1, columns), wide_type),
            pltpu.VMEM((1, columns), wide_type),
            pltpu.VMEM((HEAD_SIZE, columns), wide_type),
            *key_scratch(kv),
            *weight.scratch(),
        ],
    )(*layout, *kv, *weight.values())


def attend_back_body(
    count, seen_ref, base_ref, q_ref, pos_ref, start_ref, local_ref,
    z_ref, zc_ref, ot_ref, lse_ref, cos_ref, sin_ref, *refs,
):
    kv_parts, pieces = refs[:4], refs[4 : 4 + count]
    dq_ref, *dkv_parts = refs[4 + count : 9 + count]
    acc_ref, dkv_ref, kv_ref, kv_sem, w_ref, sem_ref = refs[9 + count :]
    tile = pl.program_id(0)
    key_tiles = kv_ref.shape[0]

    @pl.when(tile == 0)
    def _():
        load_keys(kv_parts, kv_ref, kv_sem)
        load_pieces(pieces, (w_ref, sem_ref))
        dkv_ref[...] = jnp.zeros(dkv_ref.shape, wide_type)

    rows = q_ref.shape[2] // GROUP
    turned = dot(w_ref[...], both_cores(z_ref, zc_ref), 0, 1).astype(low_type)
    grad_out = jnp.concatenate(
        [turned[head * HEAD_SIZE : (head + 1) * HEAD_SIZE] for head in range(GROUP)], axis=1
    )
    delta = jnp.sum(grad_out.astype(wide_type) * ot_ref[0], axis=0, keepdims=True)
    acc_ref[...] = jnp.zeros(acc_ref.shape, wide_type)

    def step(k, carry):
        @pl.when(seen_ref[tile * key_tiles + k] != 0)
        def _():
            raw = dot(kv_ref[k, :HEAD_SIZE], q_ref[0], 0, 0)
            key_pos = base_ref[k] + local_ref[...]
            allowed = (key_pos <= pos_ref[0]) & (key_pos >= start_ref[0])
            probs = jnp.where(allowed, jnp.exp2(raw * EXP_SCALE - lse_ref[0]), 0.0)
            grad_probs = dot(kv_ref[k, HEAD_SIZE:], grad_out, 0, 0)
            grad_scores = (probs * (grad_probs - delta)).astype(low_type)
            acc_ref[...] += dot(kv_ref[k, :HEAD_SIZE], grad_scores, 1, 0)
            dkv_ref[k, :HEAD_SIZE] += dot(q_ref[0], grad_scores, 1, 1) * SCALE
            dkv_ref[k, HEAD_SIZE:] += dot(grad_out, probs.astype(low_type), 1, 1)

        return carry

    lax.fori_loop(0, key_tiles, step, 0)
    cos, sin = cos_ref[0], sin_ref[0]
    for head in range(GROUP):
        part = acc_ref[:, head * rows : (head + 1) * rows] * SCALE
        first, second = part[:HALF], part[HALF:]
        dq_ref[0, head * HEAD_SIZE : (head + 1) * HEAD_SIZE] = jnp.concatenate(
            [first * cos + second * sin, second * cos - first * sin], axis=0
        ).astype(low_type)

    @pl.when(tile == pl.num_programs(0) - 1)
    def _():
        start = 0
        for part in dkv_parts:
            size = part.shape[0]
            part[...] = dkv_ref[start : start + size].astype(part.dtype)
            start += size


def attend_back(layout, kv, weight, near, far, out_turned, lse, cos, sin):
    seen, base, q, pos, start, local = layout
    tiles, _, columns = q.shape
    wide = kv[0].shape[2]
    width = near.shape[2]
    kinds = (wide_type, low_type, low_type, low_type)
    held = key_scratch(kv)
    return call(
        functools.partial(attend_back_body, weight.count()),
        (tiles,),
        [
            smem_spec(),
            smem_spec(),
            tile_of(1, HEAD_SIZE, columns),
            tile_of(1, 1, columns),
            tile_of(1, 1, columns),
            whole(local),
            tile_of(1, wide // 2, width),
            tile_of(1, wide // 2, width),
            tile_of(1, HEAD_SIZE, columns),
            tile_of(1, 1, columns),
            tile_of(1, HALF, wide),
            tile_of(1, HALF, wide),
            *[any_spec()] * 4,
            *weight.specs(),
        ],
        [tile_of(1, QROWS, wide)] + [whole(part) for part in kv],
        [shape((tiles, QROWS, wide), low_type)]
        + [shape(part.shape, kind) for part, kind in zip(kv, kinds)],
        [
            pltpu.VMEM((HEAD_SIZE, columns), wide_type),
            pltpu.VMEM(held[0].shape, wide_type),
            *held,
            *weight.scratch(),
        ],
    )(*layout, near, far, out_turned, lse, cos, sin, *kv, *weight.values())


def finish_body(late_ref, dq_ref, own_ref, y_ref, a_ref, b_ref, cos_ref, sin_ref, out_ref):
    late = (pl.program_id(0) // 2 == late_ref[0]).astype(wide_type)
    total = own_ref[0] + y_ref[0].astype(wide_type)
    total = total + late * (a_ref[0].astype(wide_type) + b_ref[0].astype(wide_type))
    cos, sin = cos_ref[0], sin_ref[0]
    first, second = total[:HALF], total[HALF:HEAD_SIZE]
    turned = jnp.concatenate(
        [
            dq_ref[0].astype(wide_type),
            first * cos + second * sin,
            second * cos - first * sin,
            total[HEAD_SIZE:],
            jnp.zeros((2, total.shape[1]), wide_type),
        ],
        axis=0,
    )
    out_ref[0] = turned.T.astype(low_type)


def finish(late, dq, own, from_y, from_a, from_b, cos, sin):
    tiles, _, wide = dq.shape
    return call(
        finish_body,
        (tiles,),
        [
            smem_spec(),
            tile_of(1, QROWS, wide),
            tile_of(1, BOTH, wide),
            tile_of(1, BOTH, wide),
            pl.BlockSpec((1, BOTH, wide), lambda t: (t % 2, 0, 0)),
            pl.BlockSpec((1, BOTH, wide), lambda t: (t % 2, 0, 0)),
            tile_of(1, HALF, wide),
            tile_of(1, HALF, wide),
        ],
        tile_of(1, wide, EDGE + 2),
        shape((tiles, wide, EDGE + 2), low_type),
    )(late, dq, own, from_y, from_a, from_b, cos, sin)


def turn_body(near_ref, far_ref, out_ref):
    out_ref[...] = both_cores(near_ref, far_ref).T


def turn(near, far):
    tiles, per, width = near.shape
    return call(
        turn_body,
        (tiles,),
        [tile_of(1, per, width), tile_of(1, per, width)],
        pl.BlockSpec((width, 2 * per), lambda t: (0, t)),
        shape((width, 2 * per * tiles), low_type),
    )(near, far)


def ffn_body(count, near_ref, far_ref, *refs):
    gate_pieces, up_pieces = refs[:count], refs[count : 2 * count]
    at_ref, hid_ref, one_ref, two_ref, gate_ref, gate_sem, up_ref, up_sem = refs[2 * count :]

    @pl.when(pl.program_id(0) == 0)
    def _():
        load_pieces(gate_pieces, (gate_ref, gate_sem))
        load_pieces(up_pieces, (up_ref, up_sem))

    normed = both_cores(near_ref, far_ref)
    at_ref[...] = normed.T
    gate = dot(normed, gate_ref[...], 1, 0)
    upward = dot(normed, up_ref[...], 1, 0)
    sigma = 1.0 / (1.0 + jnp.exp(-gate))
    passed = gate * sigma
    hid_ref[0] = (passed * upward).astype(low_type)
    one_ref[0] = upward * sigma * (1.0 + gate * (1.0 - sigma))
    two_ref[0] = passed


def ffn(near, far, gate_weight, up_weight):
    tiles, per, width = near.shape
    wide = 2 * per
    hidden = gate_weight.columns
    return call(
        functools.partial(ffn_body, gate_weight.count()),
        (tiles,),
        [
            tile_of(1, per, width),
            tile_of(1, per, width),
            *gate_weight.specs(),
            *up_weight.specs(),
        ],
        [
            pl.BlockSpec((width, wide), lambda t: (0, t)),
            tile_of(1, wide, hidden),
            tile_of(1, wide, hidden),
            tile_of(1, wide, hidden),
        ],
        [
            shape((width, tiles * wide), low_type),
            shape((tiles, wide, hidden), low_type),
            shape((tiles, wide, hidden), wide_type),
            shape((tiles, wide, hidden), wide_type),
        ],
        gate_weight.scratch() + up_weight.scratch(),
    )(near, far, *gate_weight.values(), *up_weight.values())


def ffn_back_body(count, near_ref, far_ref, one_ref, two_ref, *refs):
    dgate_ref, dup_ref, w_ref, sem_ref = refs[count:]

    @pl.when(pl.program_id(0) == 0)
    def _():
        load_pieces(refs[:count], (w_ref, sem_ref))

    grad_hidden = dot(both_cores(near_ref, far_ref), w_ref[...], 1, 0)
    dgate_ref[0] = (grad_hidden * one_ref[0]).astype(low_type)
    dup_ref[0] = (grad_hidden * two_ref[0]).astype(low_type)


def ffn_back(near, far, weight, one, two):
    tiles, per, width = near.shape
    wide = 2 * per
    hidden = weight.columns
    part = tile_of(1, wide, hidden)
    return call(
        functools.partial(ffn_back_body, weight.count()),
        (tiles,),
        [tile_of(1, per, width), tile_of(1, per, width), part, part, *weight.specs()],
        [part, part],
        [shape((tiles, wide, hidden), low_type)] * 2,
        weight.scratch(),
    )(near, far, one, two, *weight.values())


def put_blocks(total, out_refs):
    for index, out_ref in enumerate(out_refs):
        out_ref[...] = total[index].astype(out_ref.dtype)


def block_outputs(per, width, step):
    spec = pl.BlockSpec((per, step), lambda n: (0, n))
    kinds = (wide_type, low_type, low_type, low_type)
    return [spec] * 4, [shape((per, width), kind) for kind in kinds]


def combine_body(near_ref, got_ref, *out_refs):
    put_blocks(near_ref[...].astype(wide_type) + got_ref[...].astype(wide_type), out_refs)


def combine(near, got):
    blocks, per, width = near.shape
    step = 512
    spec = pl.BlockSpec((blocks, per, step), lambda n: (0, 0, n))
    out_specs, out_shape = block_outputs(per, width, step)
    return call(combine_body, (width // step,), [spec, spec], out_specs, out_shape)(near, got)


def branch_body(lefts, count, with_got, *refs):
    left_refs, refs = refs[:lefts], refs[lefts:]
    pieces, refs = [refs[i * count : (i + 1) * count] for i in range(lefts)], refs[lefts * count :]
    got_ref, refs = (refs[0], refs[1:]) if with_got else (None, refs)
    outs, scratch = refs[: -2 * lefts], refs[-2 * lefts :]
    step = outs[0].shape[-1]

    @pl.when(pl.program_id(0) == 0)
    def _():
        for index in range(lefts):
            load_pieces(pieces[index], scratch[2 * index : 2 * index + 2])

    start = pl.multiple_of(pl.program_id(0) * step, step)
    total = None
    for index in range(lefts):
        left = left_refs[index][...]
        rows = left.shape[0] * left.shape[2]
        weight = scratch[2 * index][pl.ds(start, step), :]
        term = dot(left.reshape(rows, left.shape[3]), weight, 1, 1)
        total = term if total is None else total + term
    total = total.reshape(4, total.shape[0] // 4, step)
    if got_ref is None:
        outs[0][...] = total.astype(low_type)
    else:
        put_blocks(total + got_ref[...].astype(wide_type), outs)


def branch(pairs, core, got=None):
    step = 512
    specs, lefts, weight_specs, weights, scratch = [], [], [], [], []
    for left, weight in pairs:
        tiles, wide, inner = left.shape
        lefts.append(left.reshape(tiles, 2, wide // 2, inner))
        specs.append(pl.BlockSpec((tiles, 1, wide // 2, inner), lambda n: (0, core, 0, 0)))
        weight_specs += weight.specs()
        weights += weight.values()
        scratch += weight.scratch()
    width = 2 * len(weight.blocks) * weight.rows
    per = wide // 2
    block = pl.BlockSpec((tiles, per, step), lambda n: (0, 0, n))
    if got is None:
        out_specs, out_shape = [block], [shape((tiles, per, width), low_type)]
    else:
        out_specs, out_shape = block_outputs(per, width, step)
    outs = call(
        functools.partial(branch_body, len(pairs), weight.count(), got is not None),
        (width // step,),
        specs + weight_specs + ([] if got is None else [block]),
        out_specs,
        out_shape,
        scratch,
    )(*lefts, *weights, *([] if got is None else [got]))
    return outs[0] if got is None else outs


def weight_body(count, index_ref, first_ref, second_ref, right_ref, *refs):
    left = jnp.concatenate([first_ref[0], second_ref[0]], axis=0)
    total = dot(left, right_ref[...], 1, 0)
    rows = total.shape[0] // 2
    for part in range(2):
        block = total[part * rows : (part + 1) * rows]
        for position in range(count):
            block = block + refs[2 * position + part][0].astype(wide_type)
        refs[-1][part] = block.astype(refs[-1].dtype)


def weight_rows(turned, right, places, addends, kind):
    tokens = turned.shape[1]
    columns = right.shape[-1]
    blocks = lax.axis_size("dp")
    rows = turned.shape[0] // blocks
    number = len(places)
    flat = [jnp.asarray(p, jnp.int32) for p in places]

    def named(offset, part, last):
        return pl.BlockSpec(
            (1, rows, last), lambda i, index: (index[offset + 2 * i + part], 0, 0)
        )

    specs = [
        named(0, 0, tokens),
        named(0, 1, tokens),
        pl.BlockSpec((tokens, columns), lambda i, index: (0, 0)),
    ]
    given = []
    for position, (array, where) in enumerate(addends):
        flat += [jnp.asarray(p, jnp.int32) for p in where]
        for part in range(2):
            specs.append(named((position + 1) * number, part, columns))
            given.append(array)
    left = turned.reshape(blocks, rows, tokens)
    return pl.pallas_call(
        functools.partial(weight_body, len(addends)),
        grid_spec=pltpu.PrefetchScalarGridSpec(
            num_scalar_prefetch=1,
            grid=(number // 2,),
            in_specs=specs,
            out_specs=pl.BlockSpec((2, rows, columns), lambda i, index: (i, 0, 0)),
        ),
        out_shape=shape((number, rows, columns), kind),
        compiler_params=pltpu.CompilerParams(vmem_limit_bytes=VMEM_LIMIT),
        cost_estimate=pl.CostEstimate(flops=10**10, bytes_accessed=0, transcendentals=0),
    )(jnp.stack(flat), left, left, right.reshape(tokens, columns), *given)


def share_first(turned, right):
    _, _, y, _, _ = bits()
    ring = lax.axis_size("dp") // 4
    places = [4 * g + 2 * b + (1 - y) for g in range(ring) for b in range(2)]
    return weight_rows(turned, right, places, [], low_type)


def share_term(turned, right, got, step, travel=None):
    h, l, y, _, _ = bits()
    ring = lax.axis_size("dp") // 4
    group = (h - 1 - step) % ring
    last = step == ring - 1
    order = [l, 1 - l] if last else [0, 1]
    places = [4 * group + 2 * b + y for b in order]
    addends = [(got, [2 * group + b for b in order])]
    if travel is not None:
        addends.append((travel, order))
    return weight_rows(turned, right, places, addends, wide_type if last else low_type)


def share_rest(turned, right, got, term):
    ring = lax.axis_size("dp") // 4
    travel = hop_ring(term)
    for step in range(1, ring - 1):
        travel = hop_ring(share_term(turned, right, got, step, travel))
    return travel


def share_third(turned, right, got, travel):
    ring = lax.axis_size("dp") // 4
    own = share_term(turned, right, got, ring - 1, travel)
    return own[0], own[1].astype(low_type), jnp.sum(jnp.square(own))


def adamw(param, grad, first, second):
    first_new = beta_first * first + (1.0 - beta_first) * grad
    second_new = beta_second * second + (1.0 - beta_second) * grad * grad
    first_hat = first_new / (1.0 - beta_first**STEP)
    second_hat = second_new / (1.0 - beta_second**STEP)
    change = -learn_rate * (first_hat / (jnp.sqrt(second_hat) + adam_eps) + weight_decay * param)
    return (first_new, second_new, change)


def on_device(
    tokens,
    upstream,
    offsets,
    query_weight,
    keyval_weight,
    output_weight,
    gateup_weight,
    down_weight,
    norm_gains,
    first_query,
    first_keyval,
    first_output,
    first_gateup,
    first_down,
    first_gains,
    second_query,
    second_keyval,
    second_output,
    second_gateup,
    second_down,
    second_gains,
):
    h, l, y, xbit, cbit = bits()
    pin = Windows(norm_gains)
    ring = lax.axis_size("dp") // 4
    block_rows = offsets.shape[0]
    per, width = tokens.shape
    wide = 2 * per

    def split(bit, arrays, more=()):
        lower, upper = [], []
        for array in arrays:
            half = array.shape[-1] // 2
            lower.append(array[:, :half].astype(low_type))
            upper.append(array[:, half:].astype(low_type))
        lower = jnp.concatenate([*lower, *more], axis=1)
        upper = jnp.concatenate([*upper, *more], axis=1)
        return choose(bit, lower, upper), choose(bit, upper, lower)

    def paired(own, other):
        return ordered(l, own[None], other[None], 0)

    places = jnp.stack(
        [
            4 * ((h - step) % ring) + 2 * b + (y ^ flip)
            for step in range(ring)
            for flip in range(2)
            for b in range(2)
        ]
    ).astype(jnp.int32)

    def legs(pair, pair_y, rings, rings_y):
        blocks = [pair, pair_y]
        for block, block_y in zip(rings, rings_y):
            blocks += [block, block_y]
        return Pieces(blocks, places)

    def arrived(own, *others):
        for other in others:
            own = own + other.astype(wide_type)
        return own

    def onward(block, corner):
        return (block.astype(wide_type) + corner.astype(wide_type)).astype(low_type)

    gain_columns = norm_gains.astype(low_type).T
    q_own, q_other = split(
        l, [query_weight, keyval_weight[0], keyval_weight[1]], [gain_columns]
    )
    o_own, o_other = split(l, [output_weight])
    q_other, o_other, other_offsets = hop_low(q_other), hop_low(o_other), hop_low(offsets)

    q_other, o_other, other_offsets, bit, own_rows = pin(
        q_other, o_other, other_offsets, l, tokens
    )
    q_pair = paired(q_own, q_other)
    q_ring, q_y = hop_ring(q_pair), hop_y(q_pair)
    tx, tz = hop_x(own_rows), hop_low(own_rows)
    o_pair = paired(o_own, o_other)
    g_own, g_other = halves(bit, gateup_weight, 0)

    def relative(own):
        four = own.reshape(2, 2, per)
        four = choose(xbit, four, four[::-1])
        return choose(cbit, four, four[:, ::-1])

    offset_tiles = jnp.concatenate([relative(offsets), relative(other_offsets)], axis=0)
    offset_tiles = offset_tiles.reshape(4, wide)
    lane = jnp.arange(wide, dtype=jnp.int32)
    local = choose(cbit, lane, lane ^ per)
    mine = jnp.arange(4, dtype=jnp.int32)

    def bases(group_h, group_y, low_bits, x_bits):
        block = 4 * group_h + 2 * low_bits + group_y
        return block * block_rows + x_bits * wide

    low_bits, x_bits = l ^ (mine // 2), xbit ^ (mine % 2)
    own_base = bases(h, y, low_bits, x_bits)
    one = jnp.ones((2,), jnp.int32)
    key_base = jnp.concatenate(
        [
            own_base,
            bases(h, 1 - y, low_bits, x_bits),
            bases(h - 1, y, one, x_bits[:2]),
            bases(h - 1, 1 - y, one, x_bits[:2]),
        ]
    ).astype(jnp.int32)
    query_pos = own_base[:, None] + local[None, :]
    doc_start = query_pos - offset_tiles
    seen = (
        (key_base[None, :] <= own_base[:, None] + wide - 1)
        & (key_base[None, :] + wide - 1 >= jnp.min(doc_start, axis=1, keepdims=True))
    ).astype(jnp.int32).reshape(-1)
    spread = lambda a: jnp.tile(a, (1, GROUP)).reshape(4, 1, GROUP * wide)
    query_lanes, start_lanes = spread(query_pos), spread(doc_start)
    local_column = local.reshape(wide, 1)
    freqs = rope_base ** (-(jnp.arange(HALF).astype(wide_type) * 2.0 / HEAD_SIZE))
    angle = freqs[None, :, None] * offset_tiles.astype(wide_type)[:, None, :]
    cos, sin = jnp.cos(angle), jnp.sin(angle)

    tx, tz, g_other = pin(tx, tz, g_other)
    tf = hop_x(tz)
    g_other = hop_low(g_other)

    tf, q_y, bit, up_own = pin(tf, q_y, bit, upstream)
    near = pack(own_rows, tx, tz, tf)
    far = hop_core(near)
    u_own, u_other = halves(bit, gateup_weight, 1)

    far, q_ring, g_other, u_other, o_pair, up_own, bit = pin(
        far, q_ring, g_other, u_other, o_pair, up_own, bit
    )
    q_far = rest_of_ring(q_ring)
    q_far_y = [hop_y(block) for block in q_far]
    o_ring = hop_ring(o_pair)
    u_other = hop_low(u_other)
    ux = hop_x(up_own)
    g_pair = paired(g_own, g_other)
    d_own, d_other = halves(bit, down_weight)

    d_other, o_pair, *q_far_y = pin(d_other, o_pair, *q_far_y)
    qkv_full = legs(q_pair, q_y, q_far, q_far_y)
    turned_one, q_turned, kv_own, gains = project(near, far, qkv_full, cos, sin)
    d_other, o_y = hop_low(d_other), hop_y(o_pair)

    kv_own, o_y, o_ring, u_other, ux = pin(kv_own, o_y, o_ring, u_other, ux)
    late = choose(l, kv_own[2:], kv_own[:2])
    kv_a, kv_b, kv_y = to_next(late, 0), to_next(late, 1), hop_y(kv_own)
    o_far = rest_of_ring(o_ring)
    o_far_y = [hop_y(block) for block in o_far]
    u_pair = paired(u_own, u_other)

    kv_y, kv_a, kv_b, g_pair, up_own, d_other, *o_far_y = pin(
        kv_y, kv_a, kv_b, g_pair, up_own, d_other, *o_far_y
    )
    g_ring, g_y = hop_ring(g_pair), hop_y(g_pair)
    uz = hop_low(up_own)
    d_pair = paired(d_own, d_other)

    (q_turned,) = pin.apart(q_turned)
    output_full = legs(o_pair, o_y, o_far, o_far_y)
    layout = (seen, key_base, q_turned, query_lanes, start_lanes, local_column)
    kv = (kv_own, kv_y, kv_a, kv_b)
    attended, out_turned, lse, branch_near, branch_far = attend(layout, kv, output_full)
    z_got = hop_core(branch_far)

    z_got, g_y, u_pair = pin(z_got, g_y, u_pair)
    z_own, z_x, z_low, z_corner = combine(branch_near, z_got)
    zc = hop_x(z_corner)
    u_y = hop_y(u_pair)
    inputs = tokens.astype(wide_type)
    inverse_one = lax.rsqrt(jnp.mean(inputs * inputs, axis=-1, keepdims=True) + eps_norm)
    unit_one = inputs * inverse_one

    zc, z_x, g_ring, u_pair, uz = pin(zc, z_x, g_ring, u_pair, uz)
    zz, zx = hop_low(onward(z_low, zc)), hop_x(z_x)
    g_far = rest_of_ring(g_ring)
    u_ring = hop_ring(u_pair)

    zx, zz, u_y, uz = pin(zx, zz, u_y, uz)
    g_far_y = [hop_y(block) for block in g_far]
    middle = inputs + arrived(z_own, zx, zz)
    inverse_two = lax.rsqrt(jnp.mean(middle * middle, axis=-1, keepdims=True) + eps_norm)
    unit_two = middle * inverse_two
    own_two = (unit_two * gains[1]).astype(low_type)
    az, ax = hop_low(own_two), hop_x(own_two)

    ax, az, u_ring, d_pair, uz, *g_far_y = pin(ax, az, u_ring, d_pair, uz, *g_far_y)
    af = hop_x(az)
    u_far = rest_of_ring(u_ring)
    u_far_y = [hop_y(block) for block in u_far]
    d_ring = hop_ring(d_pair)
    gate_full = legs(g_pair, g_y, g_far, g_far_y)

    af, d_pair, uz = pin(af, d_pair, uz)
    near_two = pack(own_two, ax, az, af)
    far_two = hop_core(near_two)
    d_y, uf = hop_y(d_pair), hop_x(uz)

    far_two, *u_far_y = pin(far_two, *u_far_y)
    up_full = legs(u_pair, u_y, u_far, u_far_y)
    turned_two, hidden, first_factor, second_factor = ffn(
        near_two, far_two, gate_full, up_full
    )

    d_ring, d_y, uf, hidden = pin(d_ring, d_y, uf, hidden)
    d_far = rest_of_ring(d_ring)
    d_far_y = [hop_y(block) for block in d_far]
    near_up = pack(up_own, ux, uz, uf)
    far_up = hop_core(near_up)
    turned_up = turn(near_up, far_up)
    down_first = share_first(turned_up, hidden)

    down_first, hidden, *d_far_y = pin(down_first, hidden, *d_far_y)
    down_sent = hop_y(down_first)
    down_full = legs(d_pair, d_y, d_far, d_far_y)
    grad_gate, grad_up = ffn_back(near_up, far_up, down_full, first_factor, second_factor)
    ffn_pairs = [(grad_gate, gate_full), (grad_up, up_full)]
    s_got = hop_core(branch(ffn_pairs, 1))
    gate_first = share_first(turned_two, grad_gate)

    s_got, grad_up, gate_first = pin(s_got, grad_up, gate_first)
    s_own, s_x, s_low, s_corner = branch(ffn_pairs, 0, s_got)
    sc = hop_x(s_corner)

    sc, s_x, grad_up = pin(sc, s_x, grad_up)
    sz, sx = hop_low(onward(s_low, sc)), hop_x(s_x)
    up_first = share_first(turned_two, grad_up)

    sx, sz, down_got, gate_first, up_first, hidden = pin(
        sx, sz, down_sent, gate_first, up_first, hidden
    )
    grad_normed_two = arrived(s_own, sx, sz)
    gain_two = jnp.sum(grad_normed_two * unit_two, axis=0)
    grad_middle = upstream.astype(wide_type) + norm_back(
        grad_normed_two, unit_two, inverse_two, gains[1]
    )
    own_three = grad_middle.astype(low_type)
    bz, bx = hop_low(own_three), hop_x(own_three)
    gate_sent = hop_y(gate_first)
    down_travel = share_rest(
        turned_up, hidden, down_got, share_term(turned_up, hidden, down_got, 0)
    )

    bx, bz = pin(bx, bz)
    bf = hop_x(bz)

    (bf,) = pin(bf)
    near_three = pack(own_three, bx, bz, bf)
    far_three = hop_core(near_three)

    (far_three,) = pin(far_three)
    dq_turned, dkv_own, dkv_y, dkv_a, dkv_b = attend_back(
        layout, kv, output_full, near_three, far_three, out_turned, lse, cos, sin
    )

    dkv_y, dkv_a, dkv_b, gate_got, down_travel, up_first = pin(
        dkv_y, dkv_a, dkv_b, gate_sent, down_travel, up_first
    )
    dkv_a, dkv_b, dkv_y = to_previous(dkv_a, 0), to_previous(dkv_b, 1), hop_y(dkv_y)
    up_sent = hop_y(up_first)
    gate_term = share_term(turned_two, grad_gate, gate_got, 0)

    dkv_y, dkv_a, dkv_b, gate_term, near_three = pin(
        dkv_y, dkv_a, dkv_b, gate_term, near_three
    )
    gate_travel = share_rest(turned_two, grad_gate, gate_got, gate_term)
    dqkv = finish(
        (1 - l).astype(jnp.int32).reshape(1), dq_turned, dkv_own, dkv_y, dkv_a, dkv_b, cos, sin
    )
    attn_pairs = [(dqkv, qkv_full)]
    r_got = hop_core(branch(attn_pairs, 1))
    turned_three = turn(near_three, far_three)
    output_first = share_first(turned_three, attended)

    r_got, dqkv, output_first = pin(r_got, dqkv, output_first)
    output_sent = hop_y(output_first)
    r_own, r_x, r_low, r_corner = branch([(dqkv, qkv_full)], 0, r_got)
    rc = hop_x(r_corner)
    qkv_first = share_first(turned_one, dqkv)

    rc, r_x, up_got, qkv_first, down_travel = pin(rc, r_x, up_sent, qkv_first, down_travel)
    rz, rx = hop_low(onward(r_low, rc)), hop_x(r_x)
    up_travel = share_rest(
        turned_two, grad_up, up_got, share_term(turned_two, grad_up, up_got, 0)
    )

    down_travel, qkv_first = pin.apart(down_travel, qkv_first)
    down_mine, down_theirs, down_square = share_third(turned_up, hidden, down_got, down_travel)

    rx, rz, gate_travel, output_got, down_theirs, qkv_first = pin(
        rx, rz, gate_travel, output_sent, down_theirs, qkv_first
    )
    qkv_sent = hop_y(qkv_first)
    down_other = hop_low(down_theirs)

    hidden, gate_travel, output_got, rx = pin.apart(hidden, gate_travel, output_got, rx)
    f_got = hop_core(branch([(hidden, down_full)], 1))
    output_term = share_term(turned_three, attended, output_got, 0)
    grad_normed_one = arrived(r_own, rx, rz)
    gain_one = jnp.sum(grad_normed_one * unit_one, axis=0)
    grad_tokens = grad_middle + norm_back(grad_normed_one, unit_one, inverse_one, gains[0])
    gate_mine, gate_theirs, gate_square = share_third(
        turned_two, grad_gate, gate_got, gate_travel
    )
    gate_other = hop_low(gate_theirs)

    f_got, qkv_got, output_term, down_other = pin(f_got, qkv_sent, output_term, down_other)
    output_travel = share_rest(turned_three, attended, output_got, output_term)
    qkv_travel = share_rest(
        turned_one, dqkv, qkv_got, share_term(turned_one, dqkv, qkv_got, 0)
    )

    up_travel, gate_other = pin.apart(up_travel, gate_other)
    up_mine, up_theirs, up_square = share_third(turned_two, grad_up, up_got, up_travel)

    up_theirs, hidden, f_got = pin(up_theirs, hidden, f_got)
    up_other = hop_low(up_theirs)
    f_own, f_x, f_low, f_corner = branch([(hidden, down_full)], 0, f_got)
    fc = hop_x(f_corner)

    fc, f_x, output_travel, gain_one = pin(fc, f_x, output_travel, gain_one)
    fz, fx = hop_low(onward(f_low, fc)), hop_x(f_x)

    (output_travel,) = pin.apart(output_travel)
    output_mine, output_theirs, output_square = share_third(
        turned_three, attended, output_got, output_travel
    )
    output_other = hop_low(output_theirs)
    square_row = jnp.full(
        (1, width), (down_square + gate_square + up_square + output_square) / width
    )
    sums = jnp.concatenate([gain_one[None], gain_two[None], square_row], axis=0)

    qkv_travel, sums, up_other = pin(qkv_travel, sums, up_other)
    qkv_mine, qkv_theirs, qkv_square = share_third(turned_one, dqkv, qkv_got, qkv_travel)
    qkv_other = hop_low(qkv_theirs)
    last_row = (jnp.arange(3) == 2).astype(wide_type)[:, None]
    totals = sums + last_row * (qkv_square / width)
    totals = totals + hop_core(totals)

    from_x = hop_x(totals)
    from_x, qkv_other, output_other, fx, fz = pin(from_x, qkv_other, output_other, fx, fz)
    block_out = (middle + arrived(f_own, fx, fz)).astype(low_type)
    totals = sum_rest(totals + from_x)
    gain_total = totals[:2]
    grad_norm = jnp.sqrt(totals[2, 0] * width + jnp.sum(gain_total * gain_total))
    def joined(mine, other, start, stop):
        return ordered(l, mine[:, start:stop], other[:, start:stop].astype(wide_type), 1)

    edge_one = QROWS + HEAD_SIZE
    hidden_part = down_mine.shape[1]
    grad_query = joined(qkv_mine, qkv_other, 0, QROWS)
    grad_keyval = jnp.stack(
        [
            joined(qkv_mine, qkv_other, QROWS, edge_one),
            joined(qkv_mine, qkv_other, edge_one, EDGE),
        ]
    )
    grad_output = joined(output_mine, output_other, 0, QROWS)
    grad_gateup = jnp.stack(
        [
            joined(gate_mine, gate_other, 0, hidden_part),
            joined(up_mine, up_other, 0, hidden_part),
        ]
    )
    grad_down = joined(down_mine, down_other, 0, hidden_part)
    rows_owned = query_weight.shape[0]
    grad_gains = lax.dynamic_slice_in_dim(
        gain_total, lax.axis_index("dp") * rows_owned, rows_owned, 1
    )
    clipping_bound = math.sqrt(
        MODEL_WIDTH
        * (2 * QUERY_HEAD_COUNT * HEAD_SIZE + 2 * KEY_VALUE_HEADS * HEAD_SIZE + 3 * HIDDEN_UNITS)
        + 2 * MODEL_WIDTH
    )
    clip = jnp.minimum(1.0, clipping_bound / (grad_norm + 1e-06))
    params = (query_weight, keyval_weight, output_weight, gateup_weight, down_weight, pin.held)
    firsts = (first_query, first_keyval, first_output, first_gateup, first_down, first_gains)
    seconds = (second_query, second_keyval, second_output, second_gateup, second_down, second_gains)
    grads = (grad_query, grad_keyval, grad_output, grad_gateup, grad_down, grad_gains)
    states = [
        adamw(params[index], grads[index] * clip, firsts[index], seconds[index])
        for index in range(6)
    ]
    return (
        block_out,
        grad_tokens,
        grad_norm,
        *grads,
        *[state[0] for state in states],
        *[state[1] for state in states],
        *[state[2] for state in states],
    )


def solution(mesh):
    weights = (
        P("dp", "mp"),
        P(None, "dp", "mp"),
        P("dp", "mp"),
        P(None, "dp", "mp"),
        P("dp", "mp"),
        P(None, "dp"),
    )
    rows = P(("dp", "mp"), None)
    return jax.shard_map(
        on_device,
        mesh=mesh,
        in_specs=(rows, rows, P("dp"), *weights, *weights, *weights),
        out_specs=(rows, rows, P(), *weights, *weights, *weights, *weights),
        check_vma=False,
    )
```

```python
import functools
import math

import jax
import jax.numpy as jnp
from jax import lax
from jax.experimental import pallas as pl
from jax.experimental.pallas import tpu as pltpu
from jax.sharding import PartitionSpec as P

MODEL_WIDTH = 2560
QUERY_HEAD_COUNT = 32
KEY_VALUE_HEADS = 8
HEAD_SIZE = 80
HIDDEN_UNITS = 7168
STEP = 10

eps_norm = 1e-05
rope_base = 1000000.0
beta_first = 0.9
beta_second = 0.95
learn_rate = 0.02
weight_decay = 0.1
adam_eps = 1e-08
masked_score = -1e30

low_type = jnp.bfloat16
wide_type = jnp.float32

HALF = HEAD_SIZE // 2
GROUP = QUERY_HEAD_COUNT // KEY_VALUE_HEADS
QROWS = GROUP * HEAD_SIZE
BOTH = 2 * HEAD_SIZE
EDGE = QROWS + BOTH
EXP_SCALE = (HEAD_SIZE ** (-0.5)) * math.log2(math.e)
SCALE = HEAD_SIZE ** (-0.5)
AXES = ("dp", "mp")


def hop(block, move):
    dp_size, mp_size = lax.axis_size("dp"), lax.axis_size("mp")
    route = []
    for d in range(dp_size):
        for m in range(mp_size):
            target = move(d, m)
            if target is not None:
                route.append((d * mp_size + m, target[0] * mp_size + target[1]))
    return lax.ppermute(block, AXES, route)


def hop_core(block):
    return hop(block, lambda d, m: (d, m ^ 1))


def hop_x(block):
    return hop(block, lambda d, m: (d, m ^ 2))


def hop_low(block):
    return hop(block, lambda d, m: (d ^ 2, m))


def hop_y(block):
    return hop(block, lambda d, m: (d ^ 1, m))


def hop_ring(block):
    size = lax.axis_size("dp")
    return hop(block, lambda d, m: ((d + 4) % size, m))


def to_next(block, flip):
    size = lax.axis_size("dp")

    def move(d, m):
        if d + 4 >= size or (flip and d % 2 == 0):
            return None
        return (d + 4) ^ flip, m

    return hop(block, move)


def to_previous(block, flip):
    def move(d, m):
        if d < 4 or (flip and d % 2 == 1):
            return None
        return (d - 4) ^ flip, m

    return hop(block, move)


def bits():
    d = lax.axis_index("dp")
    m = lax.axis_index("mp")
    return d // 4, (d // 2) % 2, d % 2, m // 2, m % 2


def choose(bit, if_zero, if_one):
    return jnp.where(bit == 0, if_zero, if_one)


def ordered(bit, mine, other, axis):
    return choose(
        bit,
        jnp.concatenate([mine, other], axis=axis),
        jnp.concatenate([other, mine], axis=axis),
    )


def keep_body(held_ref, out_ref):
    out_ref[...] = held_ref[...]


class Windows:
    def __init__(self, held):
        self.held = held

    def __call__(self, *arrays):
        *given, held = lax.optimization_barrier((*arrays, self.held))
        self.held = pl.pallas_call(
            keep_body,
            out_shape=jax.ShapeDtypeStruct(held.shape, held.dtype),
            cost_estimate=pl.CostEstimate(flops=10**12, bytes_accessed=0, transcendentals=0),
        )(held)
        return given

    def apart(self, *arrays):
        self.held = hop_core(self.held)
        return self(*arrays)


def rest_of_ring(first):
    blocks = [first]
    for _ in range(lax.axis_size("dp") // 4 - 2):
        blocks.append(hop_ring(blocks[-1]))
    return blocks


def sum_rest(value):
    ring = lax.axis_size("dp") // 4
    for step in (hop_low, hop_y):
        value = value + step(value)
    travel = value
    for _ in range(1, ring):
        travel = hop_ring(travel)
        value = value + travel
    return value


def norm_back(incoming, unit_rows, inverse_root, gain):
    scaled = incoming * gain
    return inverse_root * (
        scaled - unit_rows * jnp.mean(scaled * unit_rows, axis=-1, keepdims=True)
    )


VMEM_LIMIT = 56 * 2**20


def call(body, grid, in_specs, out_specs, out_shape, scratch=(), flops=10**10):
    return pl.pallas_call(
        body,
        grid=grid,
        in_specs=in_specs,
        out_specs=out_specs,
        out_shape=out_shape,
        scratch_shapes=list(scratch),
        compiler_params=pltpu.CompilerParams(vmem_limit_bytes=VMEM_LIMIT),
        cost_estimate=pl.CostEstimate(flops=flops, bytes_accessed=0, transcendentals=0),
    )


def shape(dims, kind):
    return jax.ShapeDtypeStruct(dims, kind)


def whole(array):
    zeros = (0,) * array.ndim
    return pl.BlockSpec(array.shape, lambda *_: zeros)


def tile_of(*dims):
    rest = (0,) * (len(dims) - 1)
    return pl.BlockSpec(dims, lambda t: (t, *rest))


def dot(left, right, left_dim, right_dim):
    return lax.dot_general(
        left, right, (((left_dim,), (right_dim,)), ((), ())), preferred_element_type=wide_type
    )


def any_spec():
    return pl.BlockSpec(memory_space=pl.ANY)


def smem_spec():
    return pl.BlockSpec(memory_space=pltpu.SMEM)


class Pieces:
    def __init__(self, blocks, places):
        self.blocks = blocks
        self.places = places
        _, self.rows, self.columns = blocks[0].shape

    def count(self):
        return 1 + len(self.blocks)

    def specs(self):
        return [smem_spec()] + [any_spec()] * len(self.blocks)

    def values(self):
        return [self.places, *self.blocks]

    def scratch(self):
        number = 2 * len(self.blocks)
        return [
            pltpu.VMEM((number * self.rows, self.columns), low_type),
            pltpu.SemaphoreType.DMA((number,)),
        ]


def load_pieces(refs, scratch):
    place_ref, *block_refs = refs
    weight_ref, sem_ref = scratch
    copies = []
    for index, block_ref in enumerate(block_refs):
        rows = block_ref.shape[1]
        for part in range(2):
            number = 2 * index + part
            start = pl.multiple_of(place_ref[number] * rows, rows & -rows)
            copies.append(
                pltpu.make_async_copy(
                    block_ref.at[part], weight_ref.at[pl.ds(start, rows)], sem_ref.at[number]
                )
            )
    for copy in copies:
        copy.start()
    for copy in copies:
        copy.wait()


def halves_body(bit_ref, weight_ref, own_ref, other_ref):
    size = own_ref.shape[1]
    for out_ref, which in ((own_ref, bit_ref[0]), (other_ref, 1 - bit_ref[0])):
        start = pl.multiple_of(which * size, size & -size)
        out_ref[...] = weight_ref[:, pl.ds(start, size)].astype(low_type)


def halves(bit, weight, layer=None):
    rows, columns = weight.shape[-2:]
    step = rows // 5
    if layer is None:
        spec = pl.BlockSpec((step, columns), lambda i: (i, 0))
    else:
        spec = pl.BlockSpec((pl.squeezed, step, columns), lambda i: (layer, i, 0))
    half = pl.BlockSpec((step, columns // 2), lambda i: (i, 0))
    return call(
        halves_body,
        (5,),
        [smem_spec(), spec],
        [half, half],
        [shape((rows, columns // 2), low_type)] * 2,
    )(bit.astype(jnp.int32).reshape(1), weight)


def pack_body(*refs):
    *parts, out_ref = refs
    start = 0
    for part in parts:
        if len(part.shape) == 2:
            out_ref[start] = part[...]
            start += 1
        else:
            out_ref[start : start + part.shape[0]] = part[...]
            start += part.shape[0]


def pack(*parts):
    rows, width = parts[0].shape[-2:]
    step = width // 4
    specs, number = [], 0
    for part in parts:
        if part.ndim == 2:
            specs.append(pl.BlockSpec((rows, step), lambda n: (0, n)))
            number += 1
        else:
            specs.append(pl.BlockSpec((part.shape[0], rows, step), lambda n: (0, 0, n)))
            number += part.shape[0]
    return call(
        pack_body,
        (4,),
        specs,
        pl.BlockSpec((number, rows, step), lambda n: (0, 0, n)),
        shape((number, rows, width), parts[0].dtype),
    )(*parts)


def both_cores(near_ref, far_ref):
    return jnp.concatenate([near_ref[0], far_ref[0]], axis=0)


def project_body(count, x_ref, xc_ref, cos_ref, sin_ref, *refs):
    pieces = refs[:count]
    at_ref, q_ref, kv_ref, g_ref, w_ref, sem_ref = refs[count:]

    @pl.when(pl.program_id(0) == 0)
    def _():
        load_pieces(pieces, (w_ref, sem_ref))
        turned = w_ref[:, 384:].astype(wide_type).T
        g_ref[...] = turned[EDGE - 384 : EDGE - 384 + 2]

    x = both_cores(x_ref, xc_ref).astype(wide_type)
    rows = x.shape[0]
    unit = x * lax.rsqrt(jnp.mean(x * x, axis=-1, keepdims=True) + eps_norm)
    normed = (unit * g_ref[0:1]).astype(low_type)
    at_ref[...] = normed.T
    flat = dot(w_ref[...], normed, 0, 1)
    cos, sin = cos_ref[0], sin_ref[0]

    def rotated(start):
        first = flat[start : start + HALF]
        second = flat[start + HALF : start + HEAD_SIZE]
        return jnp.concatenate(
            [first * cos - second * sin, second * cos + first * sin], axis=0
        ).astype(low_type)

    for head in range(GROUP):
        q_ref[0, :, head * rows : (head + 1) * rows] = rotated(head * HEAD_SIZE)
    kv_ref[0] = jnp.concatenate(
        [rotated(QROWS), flat[QROWS + HEAD_SIZE : EDGE].astype(low_type)], axis=0
    )


def project(near, far, weight, cos, sin):
    tiles, per, width = near.shape
    wide = 2 * per
    return call(
        functools.partial(project_body, weight.count()),
        (tiles,),
        [
            tile_of(1, per, width),
            tile_of(1, per, width),
            tile_of(1, HALF, wide),
            tile_of(1, HALF, wide),
            *weight.specs(),
        ],
        [
            pl.BlockSpec((width, wide), lambda t: (0, t)),
            tile_of(1, HEAD_SIZE, GROUP * wide),
            tile_of(1, BOTH, wide),
            pl.BlockSpec((2, width), lambda t: (0, 0)),
        ],
        [
            shape((width, tiles * wide), low_type),
            shape((tiles, HEAD_SIZE, GROUP * wide), low_type),
            shape((tiles, BOTH, wide), low_type),
            shape((2, width), wide_type),
        ],
        weight.scratch(),
    )(near, far, cos, sin, *weight.values())


def load_keys(kv_refs, kv_ref, sem_ref):
    copies, start = [], 0
    for index, part in enumerate(kv_refs):
        size = part.shape[0]
        copies.append(
            pltpu.make_async_copy(part, kv_ref.at[start : start + size], sem_ref.at[index])
        )
        start += size
    for copy in copies:
        copy.start()
    for copy in copies:
        copy.wait()


def attend_body(count, seen_ref, base_ref, q_ref, pos_ref, start_ref, local_ref, *refs):
    kv_parts, pieces = refs[:4], refs[4 : 4 + count]
    o_ref, ot_ref, lse_ref, near_ref, far_ref = refs[4 + count : 9 + count]
    top_ref, sum_ref, acc_ref, kv_ref, kv_sem, w_ref, sem_ref = refs[9 + count :]
    tile = pl.program_id(0)
    key_tiles = kv_ref.shape[0]

    @pl.when(tile == 0)
    def _():
        load_keys(kv_parts, kv_ref, kv_sem)
        load_pieces(pieces, (w_ref, sem_ref))

    top_ref[...] = jnp.full(top_ref.shape, masked_score, wide_type)
    sum_ref[...] = jnp.zeros(sum_ref.shape, wide_type)
    acc_ref[...] = jnp.zeros(acc_ref.shape, wide_type)

    def step(k, carry):
        @pl.when(seen_ref[tile * key_tiles + k] != 0)
        def _():
            raw = dot(kv_ref[k, :HEAD_SIZE], q_ref[0], 0, 0)
            key_pos = base_ref[k] + local_ref[...]
            allowed = (key_pos <= pos_ref[0]) & (key_pos >= start_ref[0])
            raw = jnp.where(allowed, raw, masked_score)
            top_old = top_ref[...]
            top = jnp.maximum(top_old, jnp.max(raw, axis=0, keepdims=True))
            shrink = jnp.exp2((top_old - top) * EXP_SCALE)
            probs = jnp.where(allowed, jnp.exp2((raw - top) * EXP_SCALE), 0.0)
            sum_ref[...] = sum_ref[...] * shrink + jnp.sum(probs, axis=0, keepdims=True)
            acc_ref[...] = acc_ref[...] * shrink + dot(
                kv_ref[k, HEAD_SIZE:], probs.astype(low_type), 1, 0
            )
            top_ref[...] = top

        return carry

    lax.fori_loop(0, key_tiles, step, 0)
    out = acc_ref[...] / sum_ref[...]
    ot_ref[0] = out
    lse_ref[0] = top_ref[...] * EXP_SCALE + jnp.log2(sum_ref[...])
    rows = out.shape[1] // GROUP
    stacked = jnp.concatenate(
        [out[:, head * rows : (head + 1) * rows] for head in range(GROUP)], axis=0
    )
    attended = stacked.T.astype(low_type)
    o_ref[0] = attended
    branch = dot(attended, w_ref[...], 1, 1)
    near_ref[0] = branch[: rows // 2].astype(low_type)
    far_ref[0] = branch[rows // 2 :].astype(low_type)


def key_scratch(kv):
    number = sum(part.shape[0] for part in kv)
    return [
        pltpu.VMEM((number, *kv[0].shape[1:]), low_type),
        pltpu.SemaphoreType.DMA((len(kv),)),
    ]


def attend(layout, kv, weight):
    seen, base, q, pos, start, local = layout
    tiles, _, columns = q.shape
    wide = kv[0].shape[2]
    width = 2 * len(weight.blocks) * weight.rows
    return call(
        functools.partial(attend_body, weight.count()),
        (tiles,),
        [
            smem_spec(),
            smem_spec(),
            tile_of(1, HEAD_SIZE, columns),
            tile_of(1, 1, columns),
            tile_of(1, 1, columns),
            whole(local),
            *[any_spec()] * 4,
            *weight.specs(),
        ],
        [
            tile_of(1, wide, QROWS),
            tile_of(1, HEAD_SIZE, columns),
            tile_of(1, 1, columns),
            tile_of(1, wide // 2, width),
            tile_of(1, wide // 2, width),
        ],
        [
            shape((tiles, wide, QROWS), low_type),
            shape((tiles, HEAD_SIZE, columns), wide_type),
            shape((tiles, 1, columns), wide_type),
            shape((tiles, wide // 2, width), low_type),
            shape((tiles, wide // 2, width), low_type),
        ],
        [
            pltpu.VMEM((1, columns), wide_type),
            pltpu.VMEM((1, columns), wide_type),
            pltpu.VMEM((HEAD_SIZE, columns), wide_type),
            *key_scratch(kv),
            *weight.scratch(),
        ],
    )(*layout, *kv, *weight.values())


def attend_back_body(
    count, seen_ref, base_ref, q_ref, pos_ref, start_ref, local_ref,
    z_ref, zc_ref, ot_ref, lse_ref, cos_ref, sin_ref, *refs,
):
    kv_parts, pieces = refs[:4], refs[4 : 4 + count]
    dq_ref, *dkv_parts = refs[4 + count : 9 + count]
    acc_ref, dkv_ref, kv_ref, kv_sem, w_ref, sem_ref = refs[9 + count :]
    tile = pl.program_id(0)
    key_tiles = kv_ref.shape[0]

    @pl.when(tile == 0)
    def _():
        load_keys(kv_parts, kv_ref, kv_sem)
        load_pieces(pieces, (w_ref, sem_ref))
        dkv_ref[...] = jnp.zeros(dkv_ref.shape, wide_type)

    rows = q_ref.shape[2] // GROUP
    turned = dot(w_ref[...], both_cores(z_ref, zc_ref), 0, 1).astype(low_type)
    grad_out = jnp.concatenate(
        [turned[head * HEAD_SIZE : (head + 1) * HEAD_SIZE] for head in range(GROUP)], axis=1
    )
    delta = jnp.sum(grad_out.astype(wide_type) * ot_ref[0], axis=0, keepdims=True)
    acc_ref[...] = jnp.zeros(acc_ref.shape, wide_type)

    def step(k, carry):
        @pl.when(seen_ref[tile * key_tiles + k] != 0)
        def _():
            raw = dot(kv_ref[k, :HEAD_SIZE], q_ref[0], 0, 0)
            key_pos = base_ref[k] + local_ref[...]
            allowed = (key_pos <= pos_ref[0]) & (key_pos >= start_ref[0])
            probs = jnp.where(allowed, jnp.exp2(raw * EXP_SCALE - lse_ref[0]), 0.0)
            grad_probs = dot(kv_ref[k, HEAD_SIZE:], grad_out, 0, 0)
            grad_scores = (probs * (grad_probs - delta)).astype(low_type)
            acc_ref[...] += dot(kv_ref[k, :HEAD_SIZE], grad_scores, 1, 0)
            dkv_ref[k, :HEAD_SIZE] += dot(q_ref[0], grad_scores, 1, 1) * SCALE
            dkv_ref[k, HEAD_SIZE:] += dot(grad_out, probs.astype(low_type), 1, 1)

        return carry

    lax.fori_loop(0, key_tiles, step, 0)
    cos, sin = cos_ref[0], sin_ref[0]
    for head in range(GROUP):
        part = acc_ref[:, head * rows : (head + 1) * rows] * SCALE
        first, second = part[:HALF], part[HALF:]
        dq_ref[0, head * HEAD_SIZE : (head + 1) * HEAD_SIZE] = jnp.concatenate(
            [first * cos + second * sin, second * cos - first * sin], axis=0
        ).astype(low_type)

    @pl.when(tile == pl.num_programs(0) - 1)
    def _():
        start = 0
        for part in dkv_parts:
            size = part.shape[0]
            part[...] = dkv_ref[start : start + size].astype(part.dtype)
            start += size


def attend_back(layout, kv, weight, near, far, out_turned, lse, cos, sin):
    seen, base, q, pos, start, local = layout
    tiles, _, columns = q.shape
    wide = kv[0].shape[2]
    width = near.shape[2]
    kinds = (wide_type, low_type, low_type, low_type)
    held = key_scratch(kv)
    return call(
        functools.partial(attend_back_body, weight.count()),
        (tiles,),
        [
            smem_spec(),
            smem_spec(),
            tile_of(1, HEAD_SIZE, columns),
            tile_of(1, 1, columns),
            tile_of(1, 1, columns),
            whole(local),
            tile_of(1, wide // 2, width),
            tile_of(1, wide // 2, width),
            tile_of(1, HEAD_SIZE, columns),
            tile_of(1, 1, columns),
            tile_of(1, HALF, wide),
            tile_of(1, HALF, wide),
            *[any_spec()] * 4,
            *weight.specs(),
        ],
        [tile_of(1, QROWS, wide)] + [whole(part) for part in kv],
        [shape((tiles, QROWS, wide), low_type)]
        + [shape(part.shape, kind) for part, kind in zip(kv, kinds)],
        [
            pltpu.VMEM((HEAD_SIZE, columns), wide_type),
            pltpu.VMEM(held[0].shape, wide_type),
            *held,
            *weight.scratch(),
        ],
    )(*layout, near, far, out_turned, lse, cos, sin, *kv, *weight.values())


def finish_body(late_ref, dq_ref, own_ref, y_ref, a_ref, b_ref, cos_ref, sin_ref, out_ref):
    late = (pl.program_id(0) // 2 == late_ref[0]).astype(wide_type)
    total = own_ref[0] + y_ref[0].astype(wide_type)
    total = total + late * (a_ref[0].astype(wide_type) + b_ref[0].astype(wide_type))
    cos, sin = cos_ref[0], sin_ref[0]
    first, second = total[:HALF], total[HALF:HEAD_SIZE]
    turned = jnp.concatenate(
        [
            dq_ref[0].astype(wide_type),
            first * cos + second * sin,
            second * cos - first * sin,
            total[HEAD_SIZE:],
            jnp.zeros((2, total.shape[1]), wide_type),
        ],
        axis=0,
    )
    out_ref[0] = turned.T.astype(low_type)


def finish(late, dq, own, from_y, from_a, from_b, cos, sin):
    tiles, _, wide = dq.shape
    return call(
        finish_body,
        (tiles,),
        [
            smem_spec(),
            tile_of(1, QROWS, wide),
            tile_of(1, BOTH, wide),
            tile_of(1, BOTH, wide),
            pl.BlockSpec((1, BOTH, wide), lambda t: (t % 2, 0, 0)),
            pl.BlockSpec((1, BOTH, wide), lambda t: (t % 2, 0, 0)),
            tile_of(1, HALF, wide),
            tile_of(1, HALF, wide),
        ],
        tile_of(1, wide, EDGE + 2),
        shape((tiles, wide, EDGE + 2), low_type),
    )(late, dq, own, from_y, from_a, from_b, cos, sin)


def turn_body(near_ref, far_ref, out_ref):
    out_ref[...] = both_cores(near_ref, far_ref).T


def turn(near, far):
    tiles, per, width = near.shape
    return call(
        turn_body,
        (tiles,),
        [tile_of(1, per, width), tile_of(1, per, width)],
        pl.BlockSpec((width, 2 * per), lambda t: (0, t)),
        shape((width, 2 * per * tiles), low_type),
    )(near, far)


def ffn_body(count, near_ref, far_ref, *refs):
    gate_pieces, up_pieces = refs[:count], refs[count : 2 * count]
    at_ref, hid_ref, one_ref, two_ref, gate_ref, gate_sem, up_ref, up_sem = refs[2 * count :]

    @pl.when(pl.program_id(0) == 0)
    def _():
        load_pieces(gate_pieces, (gate_ref, gate_sem))
        load_pieces(up_pieces, (up_ref, up_sem))

    normed = both_cores(near_ref, far_ref)
    at_ref[...] = normed.T
    gate = dot(normed, gate_ref[...], 1, 0)
    upward = dot(normed, up_ref[...], 1, 0)
    sigma = 1.0 / (1.0 + jnp.exp(-gate))
    passed = gate * sigma
    hid_ref[0] = (passed * upward).astype(low_type)
    one_ref[0] = upward * sigma * (1.0 + gate * (1.0 - sigma))
    two_ref[0] = passed


def ffn(near, far, gate_weight, up_weight):
    tiles, per, width = near.shape
    wide = 2 * per
    hidden = gate_weight.columns
    return call(
        functools.partial(ffn_body, gate_weight.count()),
        (tiles,),
        [
            tile_of(1, per, width),
            tile_of(1, per, width),
            *gate_weight.specs(),
            *up_weight.specs(),
        ],
        [
            pl.BlockSpec((width, wide), lambda t: (0, t)),
            tile_of(1, wide, hidden),
            tile_of(1, wide, hidden),
            tile_of(1, wide, hidden),
        ],
        [
            shape((width, tiles * wide), low_type),
            shape((tiles, wide, hidden), low_type),
            shape((tiles, wide, hidden), wide_type),
            shape((tiles, wide, hidden), wide_type),
        ],
        gate_weight.scratch() + up_weight.scratch(),
    )(near, far, *gate_weight.values(), *up_weight.values())


def ffn_back_body(count, near_ref, far_ref, one_ref, two_ref, *refs):
    dgate_ref, dup_ref, w_ref, sem_ref = refs[count:]

    @pl.when(pl.program_id(0) == 0)
    def _():
        load_pieces(refs[:count], (w_ref, sem_ref))

    grad_hidden = dot(both_cores(near_ref, far_ref), w_ref[...], 1, 0)
    dgate_ref[0] = (grad_hidden * one_ref[0]).astype(low_type)
    dup_ref[0] = (grad_hidden * two_ref[0]).astype(low_type)


def ffn_back(near, far, weight, one, two):
    tiles, per, width = near.shape
    wide = 2 * per
    hidden = weight.columns
    part = tile_of(1, wide, hidden)
    return call(
        functools.partial(ffn_back_body, weight.count()),
        (tiles,),
        [tile_of(1, per, width), tile_of(1, per, width), part, part, *weight.specs()],
        [part, part],
        [shape((tiles, wide, hidden), low_type)] * 2,
        weight.scratch(),
    )(near, far, one, two, *weight.values())


def put_blocks(total, out_refs):
    for index, out_ref in enumerate(out_refs):
        out_ref[...] = total[index].astype(out_ref.dtype)


def block_outputs(per, width, step):
    spec = pl.BlockSpec((per, step), lambda n: (0, n))
    kinds = (wide_type, low_type, low_type, low_type)
    return [spec] * 4, [shape((per, width), kind) for kind in kinds]


def combine_body(near_ref, got_ref, *out_refs):
    put_blocks(near_ref[...].astype(wide_type) + got_ref[...].astype(wide_type), out_refs)


def combine(near, got):
    blocks, per, width = near.shape
    step = 512
    spec = pl.BlockSpec((blocks, per, step), lambda n: (0, 0, n))
    out_specs, out_shape = block_outputs(per, width, step)
    return call(combine_body, (width // step,), [spec, spec], out_specs, out_shape)(near, got)


def branch_body(lefts, count, with_got, *refs):
    left_refs, refs = refs[:lefts], refs[lefts:]
    pieces, refs = [refs[i * count : (i + 1) * count] for i in range(lefts)], refs[lefts * count :]
    got_ref, refs = (refs[0], refs[1:]) if with_got else (None, refs)
    outs, scratch = refs[: -2 * lefts], refs[-2 * lefts :]
    step = outs[0].shape[-1]

    @pl.when(pl.program_id(0) == 0)
    def _():
        for index in range(lefts):
            load_pieces(pieces[index], scratch[2 * index : 2 * index + 2])

    start = pl.multiple_of(pl.program_id(0) * step, step)
    total = None
    for index in range(lefts):
        left = left_refs[index][...]
        rows = left.shape[0] * left.shape[2]
        weight = scratch[2 * index][pl.ds(start, step), :]
        term = dot(left.reshape(rows, left.shape[3]), weight, 1, 1)
        total = term if total is None else total + term
    total = total.reshape(4, total.shape[0] // 4, step)
    if got_ref is None:
        outs[0][...] = total.astype(low_type)
    else:
        put_blocks(total + got_ref[...].astype(wide_type), outs)


def branch(pairs, core, got=None):
    step = 512
    specs, lefts, weight_specs, weights, scratch = [], [], [], [], []
    for left, weight in pairs:
        tiles, wide, inner = left.shape
        lefts.append(left.reshape(tiles, 2, wide // 2, inner))
        specs.append(pl.BlockSpec((tiles, 1, wide // 2, inner), lambda n: (0, core, 0, 0)))
        weight_specs += weight.specs()
        weights += weight.values()
        scratch += weight.scratch()
    width = 2 * len(weight.blocks) * weight.rows
    per = wide // 2
    block = pl.BlockSpec((tiles, per, step), lambda n: (0, 0, n))
    if got is None:
        out_specs, out_shape = [block], [shape((tiles, per, width), low_type)]
    else:
        out_specs, out_shape = block_outputs(per, width, step)
    outs = call(
        functools.partial(branch_body, len(pairs), weight.count(), got is not None),
        (width // step,),
        specs + weight_specs + ([] if got is None else [block]),
        out_specs,
        out_shape,
        scratch,
    )(*lefts, *weights, *([] if got is None else [got]))
    return outs[0] if got is None else outs


def weight_body(count, index_ref, first_ref, second_ref, right_ref, *refs):
    left = jnp.concatenate([first_ref[0], second_ref[0]], axis=0)
    total = dot(left, right_ref[...], 1, 0)
    rows = total.shape[0] // 2
    for part in range(2):
        block = total[part * rows : (part + 1) * rows]
        for position in range(count):
            block = block + refs[2 * position + part][0].astype(wide_type)
        refs[-1][part] = block.astype(refs[-1].dtype)


def weight_rows(turned, right, places, addends, kind):
    tokens = turned.shape[1]
    columns = right.shape[-1]
    blocks = lax.axis_size("dp")
    rows = turned.shape[0] // blocks
    number = len(places)
    flat = [jnp.asarray(p, jnp.int32) for p in places]

    def named(offset, part, last):
        return pl.BlockSpec(
            (1, rows, last), lambda i, index: (index[offset + 2 * i + part], 0, 0)
        )

    specs = [
        named(0, 0, tokens),
        named(0, 1, tokens),
        pl.BlockSpec((tokens, columns), lambda i, index: (0, 0)),
    ]
    given = []
    for position, (array, where) in enumerate(addends):
        flat += [jnp.asarray(p, jnp.int32) for p in where]
        for part in range(2):
            specs.append(named((position + 1) * number, part, columns))
            given.append(array)
    left = turned.reshape(blocks, rows, tokens)
    return pl.pallas_call(
        functools.partial(weight_body, len(addends)),
        grid_spec=pltpu.PrefetchScalarGridSpec(
            num_scalar_prefetch=1,
            grid=(number // 2,),
            in_specs=specs,
            out_specs=pl.BlockSpec((2, rows, columns), lambda i, index: (i, 0, 0)),
        ),
        out_shape=shape((number, rows, columns), kind),
        compiler_params=pltpu.CompilerParams(vmem_limit_bytes=VMEM_LIMIT),
        cost_estimate=pl.CostEstimate(flops=10**10, bytes_accessed=0, transcendentals=0),
    )(jnp.stack(flat), left, left, right.reshape(tokens, columns), *given)


def share_first(turned, right):
    _, _, y, _, _ = bits()
    ring = lax.axis_size("dp") // 4
    places = [4 * g + 2 * b + (1 - y) for g in range(ring) for b in range(2)]
    return weight_rows(turned, right, places, [], low_type)


def share_term(turned, right, got, step, travel=None):
    h, l, y, _, _ = bits()
    ring = lax.axis_size("dp") // 4
    group = (h - 1 - step) % ring
    last = step == ring - 1
    order = [l, 1 - l] if last else [0, 1]
    places = [4 * group + 2 * b + y for b in order]
    addends = [(got, [2 * group + b for b in order])]
    if travel is not None:
        addends.append((travel, order))
    return weight_rows(turned, right, places, addends, wide_type if last else low_type)


def share_rest(turned, right, got, term):
    ring = lax.axis_size("dp") // 4
    travel = hop_ring(term)
    for step in range(1, ring - 1):
        travel = hop_ring(share_term(turned, right, got, step, travel))
    return travel


def share_third(turned, right, got, travel):
    ring = lax.axis_size("dp") // 4
    own = share_term(turned, right, got, ring - 1, travel)
    return own[0], own[1].astype(low_type), jnp.sum(jnp.square(own))


def adamw(param, grad, first, second):
    first_new = beta_first * first + (1.0 - beta_first) * grad
    second_new = beta_second * second + (1.0 - beta_second) * grad * grad
    first_hat = first_new / (1.0 - beta_first**STEP)
    second_hat = second_new / (1.0 - beta_second**STEP)
    change = -learn_rate * (first_hat / (jnp.sqrt(second_hat) + adam_eps) + weight_decay * param)
    return (first_new, second_new, change)


def on_device(
    tokens,
    upstream,
    offsets,
    query_weight,
    keyval_weight,
    output_weight,
    gateup_weight,
    down_weight,
    norm_gains,
    first_query,
    first_keyval,
    first_output,
    first_gateup,
    first_down,
    first_gains,
    second_query,
    second_keyval,
    second_output,
    second_gateup,
    second_down,
    second_gains,
):
    h, l, y, xbit, cbit = bits()
    pin = Windows(norm_gains)
    ring = lax.axis_size("dp") // 4
    block_rows = offsets.shape[0]
    per, width = tokens.shape
    wide = 2 * per

    def split(bit, arrays, more=()):
        lower, upper = [], []
        for array in arrays:
            half = array.shape[-1] // 2
            lower.append(array[:, :half].astype(low_type))
            upper.append(array[:, half:].astype(low_type))
        lower = jnp.concatenate([*lower, *more], axis=1)
        upper = jnp.concatenate([*upper, *more], axis=1)
        return choose(bit, lower, upper), choose(bit, upper, lower)

    def paired(own, other):
        return ordered(l, own[None], other[None], 0)

    places = jnp.stack(
        [
            4 * ((h - step) % ring) + 2 * b + (y ^ flip)
            for step in range(ring)
            for flip in range(2)
            for b in range(2)
        ]
    ).astype(jnp.int32)

    def legs(pair, pair_y, rings, rings_y):
        blocks = [pair, pair_y]
        for block, block_y in zip(rings, rings_y):
            blocks += [block, block_y]
        return Pieces(blocks, places)

    def arrived(own, *others):
        for other in others:
            own = own + other.astype(wide_type)
        return own

    def onward(block, corner):
        return (block.astype(wide_type) + corner.astype(wide_type)).astype(low_type)

    gain_columns = norm_gains.astype(low_type).T
    q_own, q_other = split(
        l, [query_weight, keyval_weight[0], keyval_weight[1]], [gain_columns]
    )
    o_own, o_other = split(l, [output_weight])
    q_other, o_other, other_offsets = hop_low(q_other), hop_low(o_other), hop_low(offsets)

    q_other, o_other, other_offsets, bit, own_rows = pin(
        q_other, o_other, other_offsets, l, tokens
    )
    q_pair = paired(q_own, q_other)
    q_ring, q_y = hop_ring(q_pair), hop_y(q_pair)
    tx, tz = hop_x(own_rows), hop_low(own_rows)
    o_pair = paired(o_own, o_other)
    g_own, g_other = halves(bit, gateup_weight, 0)

    def relative(own):
        four = own.reshape(2, 2, per)
        four = choose(xbit, four, four[::-1])
        return choose(cbit, four, four[:, ::-1])

    offset_tiles = jnp.concatenate([relative(offsets), relative(other_offsets)], axis=0)
    offset_tiles = offset_tiles.reshape(4, wide)
    lane = jnp.arange(wide, dtype=jnp.int32)
    local = choose(cbit, lane, lane ^ per)
    mine = jnp.arange(4, dtype=jnp.int32)

    def bases(group_h, group_y, low_bits, x_bits):
        block = 4 * group_h + 2 * low_bits + group_y
        return block * block_rows + x_bits * wide

    low_bits, x_bits = l ^ (mine // 2), xbit ^ (mine % 2)
    own_base = bases(h, y, low_bits, x_bits)
    one = jnp.ones((2,), jnp.int32)
    key_base = jnp.concatenate(
        [
            own_base,
            bases(h, 1 - y, low_bits, x_bits),
            bases(h - 1, y, one, x_bits[:2]),
            bases(h - 1, 1 - y, one, x_bits[:2]),
        ]
    ).astype(jnp.int32)
    query_pos = own_base[:, None] + local[None, :]
    doc_start = query_pos - offset_tiles
    seen = (
        (key_base[None, :] <= own_base[:, None] + wide - 1)
        & (key_base[None, :] + wide - 1 >= jnp.min(doc_start, axis=1, keepdims=True))
    ).astype(jnp.int32).reshape(-1)
    spread = lambda a: jnp.tile(a, (1, GROUP)).reshape(4, 1, GROUP * wide)
    query_lanes, start_lanes = spread(query_pos), spread(doc_start)
    local_column = local.reshape(wide, 1)
    freqs = rope_base ** (-(jnp.arange(HALF).astype(wide_type) * 2.0 / HEAD_SIZE))
    angle = freqs[None, :, None] * offset_tiles.astype(wide_type)[:, None, :]
    cos, sin = jnp.cos(angle), jnp.sin(angle)

    tx, tz, g_other, bit = pin(tx, tz, g_other, bit)
    tf = hop_x(tz)
    g_other = hop_low(g_other)
    u_own, u_other = halves(bit, gateup_weight, 1)

    q_ring, q_y, o_pair = pin.apart(q_ring, q_y, o_pair)
    q_far = rest_of_ring(q_ring)
    q_far_y = [hop_y(block) for block in q_far]
    o_ring = hop_ring(o_pair)

    tf, bit, up_own = pin(tf, bit, upstream)
    near = pack(own_rows, tx, tz, tf)
    far = hop_core(near)
    d_own, d_other = halves(bit, down_weight)

    far, g_other, u_other, up_own, d_other, o_pair, *q_far_y = pin(
        far, g_other, u_other, up_own, d_other, o_pair, *q_far_y
    )
    u_other = hop_low(u_other)
    g_pair = paired(g_own, g_other)

    qkv_full = legs(q_pair, q_y, q_far, q_far_y)
    turned_one, q_turned, kv_own, gains = project(near, far, qkv_full, cos, sin)
    d_other, o_y, ux = hop_low(d_other), hop_y(o_pair), hop_x(up_own)

    kv_own, o_y, o_ring, u_other, ux = pin(kv_own, o_y, o_ring, u_other, ux)
    late = choose(l, kv_own[2:], kv_own[:2])
    kv_a, kv_b, kv_y = to_next(late, 0), to_next(late, 1), hop_y(kv_own)
    o_far = rest_of_ring(o_ring)
    o_far_y = [hop_y(block) for block in o_far]
    u_pair = paired(u_own, u_other)

    kv_y, kv_a, kv_b, g_pair, up_own, d_other, *o_far_y = pin(
        kv_y, kv_a, kv_b, g_pair, up_own, d_other, *o_far_y
    )
    g_ring, g_y = hop_ring(g_pair), hop_y(g_pair)
    uz = hop_low(up_own)
    d_pair = paired(d_own, d_other)

    (q_turned,) = pin.apart(q_turned)
    output_full = legs(o_pair, o_y, o_far, o_far_y)
    layout = (seen, key_base, q_turned, query_lanes, start_lanes, local_column)
    kv = (kv_own, kv_y, kv_a, kv_b)
    attended, out_turned, lse, branch_near, branch_far = attend(layout, kv, output_full)
    z_got = hop_core(branch_far)

    z_got, g_y, u_pair = pin(z_got, g_y, u_pair)
    z_own, z_x, z_low, z_corner = combine(branch_near, z_got)
    zc = hop_x(z_corner)
    u_y = hop_y(u_pair)
    inputs = tokens.astype(wide_type)
    inverse_one = lax.rsqrt(jnp.mean(inputs * inputs, axis=-1, keepdims=True) + eps_norm)
    unit_one = inputs * inverse_one

    zc, z_x, g_ring, u_pair, uz = pin(zc, z_x, g_ring, u_pair, uz)
    zz, zx = hop_low(onward(z_low, zc)), hop_x(z_x)
    g_far = rest_of_ring(g_ring)
    u_ring = hop_ring(u_pair)

    zx, zz, u_y, uz = pin(zx, zz, u_y, uz)
    g_far_y = [hop_y(block) for block in g_far]
    middle = inputs + arrived(z_own, zx, zz)
    inverse_two = lax.rsqrt(jnp.mean(middle * middle, axis=-1, keepdims=True) + eps_norm)
    unit_two = middle * inverse_two
    own_two = (unit_two * gains[1]).astype(low_type)
    az, ax = hop_low(own_two), hop_x(own_two)

    ax, az, u_ring, d_pair, uz, *g_far_y = pin(ax, az, u_ring, d_pair, uz, *g_far_y)
    af = hop_x(az)
    u_far = rest_of_ring(u_ring)
    u_far_y = [hop_y(block) for block in u_far]
    d_ring = hop_ring(d_pair)
    gate_full = legs(g_pair, g_y, g_far, g_far_y)

    af, d_pair, uz = pin(af, d_pair, uz)
    near_two = pack(own_two, ax, az, af)
    far_two = hop_core(near_two)
    d_y, uf = hop_y(d_pair), hop_x(uz)

    far_two, *u_far_y = pin(far_two, *u_far_y)
    up_full = legs(u_pair, u_y, u_far, u_far_y)
    turned_two, hidden, first_factor, second_factor = ffn(
        near_two, far_two, gate_full, up_full
    )

    d_ring, d_y, uf, hidden = pin(d_ring, d_y, uf, hidden)
    d_far = rest_of_ring(d_ring)
    d_far_y = [hop_y(block) for block in d_far]
    near_up = pack(up_own, ux, uz, uf)
    far_up = hop_core(near_up)
    turned_up = turn(near_up, far_up)
    down_first = share_first(turned_up, hidden)

    down_first, hidden, *d_far_y = pin(down_first, hidden, *d_far_y)
    down_sent = hop_y(down_first)
    down_full = legs(d_pair, d_y, d_far, d_far_y)
    grad_gate, grad_up = ffn_back(near_up, far_up, down_full, first_factor, second_factor)
    ffn_pairs = [(grad_gate, gate_full), (grad_up, up_full)]
    s_got = hop_core(branch(ffn_pairs, 1))
    gate_first = share_first(turned_two, grad_gate)

    s_got, grad_up, gate_first = pin(s_got, grad_up, gate_first)
    s_own, s_x, s_low, s_corner = branch(ffn_pairs, 0, s_got)
    sc = hop_x(s_corner)

    sc, s_x, grad_up = pin(sc, s_x, grad_up)
    sz, sx = hop_low(onward(s_low, sc)), hop_x(s_x)
    up_first = share_first(turned_two, grad_up)

    sx, sz, down_got, gate_first, up_first, hidden = pin(
        sx, sz, down_sent, gate_first, up_first, hidden
    )
    grad_normed_two = arrived(s_own, sx, sz)
    gain_two = jnp.sum(grad_normed_two * unit_two, axis=0)
    grad_middle = upstream.astype(wide_type) + norm_back(
        grad_normed_two, unit_two, inverse_two, gains[1]
    )
    own_three = grad_middle.astype(low_type)
    bz, bx = hop_low(own_three), hop_x(own_three)
    gate_sent = hop_y(gate_first)
    down_travel = share_rest(
        turned_up, hidden, down_got, share_term(turned_up, hidden, down_got, 0)
    )

    bx, bz = pin(bx, bz)
    bf = hop_x(bz)

    (bf,) = pin(bf)
    near_three = pack(own_three, bx, bz, bf)
    far_three = hop_core(near_three)

    (far_three,) = pin(far_three)
    dq_turned, dkv_own, dkv_y, dkv_a, dkv_b = attend_back(
        layout, kv, output_full, near_three, far_three, out_turned, lse, cos, sin
    )

    dkv_y, dkv_a, dkv_b, gate_got, down_travel, up_first = pin(
        dkv_y, dkv_a, dkv_b, gate_sent, down_travel, up_first
    )
    dkv_a, dkv_b, dkv_y = to_previous(dkv_a, 0), to_previous(dkv_b, 1), hop_y(dkv_y)
    up_sent = hop_y(up_first)
    gate_term = share_term(turned_two, grad_gate, gate_got, 0)

    dkv_y, dkv_a, dkv_b, gate_term, near_three = pin(
        dkv_y, dkv_a, dkv_b, gate_term, near_three
    )
    gate_travel = share_rest(turned_two, grad_gate, gate_got, gate_term)

    dq_turned, near_three = pin.apart(dq_turned, near_three)
    dqkv = finish(
        (1 - l).astype(jnp.int32).reshape(1), dq_turned, dkv_own, dkv_y, dkv_a, dkv_b, cos, sin
    )
    attn_pairs = [(dqkv, qkv_full)]
    r_got = hop_core(branch(attn_pairs, 1))
    turned_three = turn(near_three, far_three)
    output_first = share_first(turned_three, attended)

    r_got, dqkv, output_first = pin(r_got, dqkv, output_first)
    output_sent = hop_y(output_first)
    r_own, r_x, r_low, r_corner = branch([(dqkv, qkv_full)], 0, r_got)
    rc = hop_x(r_corner)
    qkv_first = share_first(turned_one, dqkv)

    rc, r_x, up_got, qkv_first, down_travel = pin(rc, r_x, up_sent, qkv_first, down_travel)
    rz, rx = hop_low(onward(r_low, rc)), hop_x(r_x)
    up_travel = share_rest(
        turned_two, grad_up, up_got, share_term(turned_two, grad_up, up_got, 0)
    )

    down_travel, qkv_first = pin.apart(down_travel, qkv_first)
    down_mine, down_theirs, down_square = share_third(turned_up, hidden, down_got, down_travel)

    rx, rz, gate_travel, output_got, down_theirs, qkv_first = pin(
        rx, rz, gate_travel, output_sent, down_theirs, qkv_first
    )
    qkv_sent = hop_y(qkv_first)
    down_other = hop_low(down_theirs)

    hidden, gate_travel, output_got, rx = pin.apart(hidden, gate_travel, output_got, rx)
    f_got = hop_core(branch([(hidden, down_full)], 1))
    output_term = share_term(turned_three, attended, output_got, 0)
    grad_normed_one = arrived(r_own, rx, rz)
    gain_one = jnp.sum(grad_normed_one * unit_one, axis=0)
    grad_tokens = grad_middle + norm_back(grad_normed_one, unit_one, inverse_one, gains[0])
    gate_mine, gate_theirs, gate_square = share_third(
        turned_two, grad_gate, gate_got, gate_travel
    )
    gate_other = hop_low(gate_theirs)

    f_got, qkv_got, output_term, down_other = pin(f_got, qkv_sent, output_term, down_other)
    output_travel = share_rest(turned_three, attended, output_got, output_term)
    qkv_travel = share_rest(
        turned_one, dqkv, qkv_got, share_term(turned_one, dqkv, qkv_got, 0)
    )

    up_travel, gate_other = pin.apart(up_travel, gate_other)
    up_mine, up_theirs, up_square = share_third(turned_two, grad_up, up_got, up_travel)

    up_theirs, hidden, f_got = pin(up_theirs, hidden, f_got)
    up_other = hop_low(up_theirs)

    hidden, f_got = pin.apart(hidden, f_got)
    f_own, f_x, f_low, f_corner = branch([(hidden, down_full)], 0, f_got)
    fc = hop_x(f_corner)

    fc, f_x, gain_one = pin(fc, f_x, gain_one)
    fz, fx = hop_low(onward(f_low, fc)), hop_x(f_x)

    (output_travel,) = pin.apart(output_travel)
    output_mine, output_theirs, output_square = share_third(
        turned_three, attended, output_got, output_travel
    )
    output_other = hop_low(output_theirs)
    square_row = jnp.full(
        (1, width), (down_square + gate_square + up_square + output_square) / width
    )
    sums = jnp.concatenate([gain_one[None], gain_two[None], square_row], axis=0)

    qkv_travel, sums, up_other = pin(qkv_travel, sums, up_other)
    qkv_mine, qkv_theirs, qkv_square = share_third(turned_one, dqkv, qkv_got, qkv_travel)
    qkv_other = hop_low(qkv_theirs)
    last_row = (jnp.arange(3) == 2).astype(wide_type)[:, None]
    totals = sums + last_row * (qkv_square / width)
    totals = totals + hop_core(totals)

    from_x = hop_x(totals)
    from_x, qkv_other, output_other, fx, fz = pin(from_x, qkv_other, output_other, fx, fz)
    block_out = (middle + arrived(f_own, fx, fz)).astype(low_type)
    totals = sum_rest(totals + from_x)
    gain_total = totals[:2]
    grad_norm = jnp.sqrt(totals[2, 0] * width + jnp.sum(gain_total * gain_total))
    def joined(mine, other, start, stop):
        return ordered(l, mine[:, start:stop], other[:, start:stop].astype(wide_type), 1)

    edge_one = QROWS + HEAD_SIZE
    hidden_part = down_mine.shape[1]
    grad_query = joined(qkv_mine, qkv_other, 0, QROWS)
    grad_keyval = jnp.stack(
        [
            joined(qkv_mine, qkv_other, QROWS, edge_one).T,
            joined(qkv_mine, qkv_other, edge_one, EDGE).T,
        ]
    )
    grad_output = joined(output_mine, output_other, 0, QROWS)
    grad_gateup = jnp.stack(
        [
            joined(gate_mine, gate_other, 0, hidden_part),
            joined(up_mine, up_other, 0, hidden_part),
        ]
    )
    grad_down = joined(down_mine, down_other, 0, hidden_part)
    rows_owned = query_weight.shape[0]
    grad_gains = lax.dynamic_slice_in_dim(
        gain_total, lax.axis_index("dp") * rows_owned, rows_owned, 1
    )
    clipping_bound = math.sqrt(
        MODEL_WIDTH
        * (2 * QUERY_HEAD_COUNT * HEAD_SIZE + 2 * KEY_VALUE_HEADS * HEAD_SIZE + 3 * HIDDEN_UNITS)
        + 2 * MODEL_WIDTH
    )
    clip = jnp.minimum(1.0, clipping_bound / (grad_norm + 1e-06))
    params = (query_weight, keyval_weight, output_weight, gateup_weight, down_weight, pin.held)
    firsts = (first_query, first_keyval, first_output, first_gateup, first_down, first_gains)
    seconds = (second_query, second_keyval, second_output, second_gateup, second_down, second_gains)
    grads = (grad_query, grad_keyval, grad_output, grad_gateup, grad_down, grad_gains)
    turned = lambda a: jnp.swapaxes(a, 1, 2)
    states = [
        adamw(params[index], grads[index] * clip, firsts[index], seconds[index])
        if index != 1
        else tuple(
            turned(a)
            for a in adamw(
                turned(params[1]), grads[1] * clip, turned(firsts[1]), turned(seconds[1])
            )
        )
        for index in range(6)
    ]
    grads = (grads[0], turned(grads[1]), *grads[2:])
    return (
        block_out,
        grad_tokens,
        grad_norm,
        *grads,
        *[state[0] for state in states],
        *[state[1] for state in states],
        *[state[2] for state in states],
    )


def solution(mesh):
    weights = (
        P("dp", "mp"),
        P(None, "dp", "mp"),
        P("dp", "mp"),
        P(None, "dp", "mp"),
        P("dp", "mp"),
        P(None, "dp"),
    )
    rows = P(("dp", "mp"), None)
    return jax.shard_map(
        on_device,
        mesh=mesh,
        in_specs=(rows, rows, P("dp"), *weights, *weights, *weights),
        out_specs=(rows, rows, P(), *weights, *weights, *weights, *weights),
        check_vma=False,
    )
```

```python
import functools
import math

import jax
import jax.numpy as jnp
from jax import lax
from jax.experimental import pallas as pl
from jax.experimental.pallas import tpu as pltpu
from jax.sharding import PartitionSpec as P

MODEL_WIDTH = 2560
QUERY_HEAD_COUNT = 32
KEY_VALUE_HEADS = 8
HEAD_SIZE = 80
HIDDEN_UNITS = 7168
STEP = 10

eps_norm = 1e-05
rope_base = 1000000.0
beta_first = 0.9
beta_second = 0.95
learn_rate = 0.02
weight_decay = 0.1
adam_eps = 1e-08
masked_score = -1e30

low_type = jnp.bfloat16
wide_type = jnp.float32

HALF = HEAD_SIZE // 2
GROUP = QUERY_HEAD_COUNT // KEY_VALUE_HEADS
QROWS = GROUP * HEAD_SIZE
BOTH = 2 * HEAD_SIZE
EDGE = QROWS + BOTH
EXP_SCALE = (HEAD_SIZE ** (-0.5)) * math.log2(math.e)
SCALE = HEAD_SIZE ** (-0.5)
AXES = ("dp", "mp")


def hop(block, move):
    dp_size, mp_size = lax.axis_size("dp"), lax.axis_size("mp")
    route = []
    for d in range(dp_size):
        for m in range(mp_size):
            target = move(d, m)
            if target is not None:
                route.append((d * mp_size + m, target[0] * mp_size + target[1]))
    return lax.ppermute(block, AXES, route)


def hop_core(block):
    return hop(block, lambda d, m: (d, m ^ 1))


def hop_x(block):
    return hop(block, lambda d, m: (d, m ^ 2))


def hop_low(block):
    return hop(block, lambda d, m: (d ^ 2, m))


def hop_y(block):
    return hop(block, lambda d, m: (d ^ 1, m))


def hop_ring(block):
    size = lax.axis_size("dp")
    return hop(block, lambda d, m: ((d + 4) % size, m))


def to_next(block, flip):
    size = lax.axis_size("dp")

    def move(d, m):
        if d + 4 >= size or (flip and d % 2 == 0):
            return None
        return (d + 4) ^ flip, m

    return hop(block, move)


def to_previous(block, flip):
    def move(d, m):
        if d < 4 or (flip and d % 2 == 1):
            return None
        return (d - 4) ^ flip, m

    return hop(block, move)


def bits():
    d = lax.axis_index("dp")
    m = lax.axis_index("mp")
    return d // 4, (d // 2) % 2, d % 2, m // 2, m % 2


def choose(bit, if_zero, if_one):
    return jnp.where(bit == 0, if_zero, if_one)


def ordered(bit, mine, other, axis):
    return choose(
        bit,
        jnp.concatenate([mine, other], axis=axis),
        jnp.concatenate([other, mine], axis=axis),
    )


def keep_body(held_ref, out_ref):
    out_ref[...] = held_ref[...]


class Windows:
    def __init__(self, held):
        self.held = held

    def __call__(self, *arrays):
        *given, held = lax.optimization_barrier((*arrays, self.held))
        self.held = pl.pallas_call(
            keep_body,
            out_shape=jax.ShapeDtypeStruct(held.shape, held.dtype),
            cost_estimate=pl.CostEstimate(flops=10**12, bytes_accessed=0, transcendentals=0),
        )(held)
        return given

    def apart(self, *arrays):
        self.held = hop_core(self.held)
        return self(*arrays)


def rest_of_ring(first):
    blocks = [first]
    for _ in range(lax.axis_size("dp") // 4 - 2):
        blocks.append(hop_ring(blocks[-1]))
    return blocks


def sum_rest(value):
    value = value + hop_y(value)
    travel = value
    for _ in range(1, lax.axis_size("dp") // 4):
        travel = hop_ring(travel)
        value = value + travel
    return value


def norm_back(incoming, unit_rows, inverse_root, gain):
    scaled = incoming * gain
    return inverse_root * (
        scaled - unit_rows * jnp.mean(scaled * unit_rows, axis=-1, keepdims=True)
    )


VMEM_LIMIT = 56 * 2**20


def call(body, grid, in_specs, out_specs, out_shape, scratch=(), flops=10**10):
    return pl.pallas_call(
        body,
        grid=grid,
        in_specs=in_specs,
        out_specs=out_specs,
        out_shape=out_shape,
        scratch_shapes=list(scratch),
        compiler_params=pltpu.CompilerParams(vmem_limit_bytes=VMEM_LIMIT),
        cost_estimate=pl.CostEstimate(flops=flops, bytes_accessed=0, transcendentals=0),
    )


def shape(dims, kind):
    return jax.ShapeDtypeStruct(dims, kind)


def whole(array):
    zeros = (0,) * array.ndim
    return pl.BlockSpec(array.shape, lambda *_: zeros)


def tile_of(*dims):
    rest = (0,) * (len(dims) - 1)
    return pl.BlockSpec(dims, lambda t: (t, *rest))


def dot(left, right, left_dim, right_dim):
    return lax.dot_general(
        left, right, (((left_dim,), (right_dim,)), ((), ())), preferred_element_type=wide_type
    )


def any_spec():
    return pl.BlockSpec(memory_space=pl.ANY)


def smem_spec():
    return pl.BlockSpec(memory_space=pltpu.SMEM)


class Pieces:
    def __init__(self, blocks, places):
        self.blocks = blocks
        self.places = places
        _, self.rows, self.columns = blocks[0].shape

    def count(self):
        return 1 + len(self.blocks)

    def specs(self):
        return [smem_spec()] + [any_spec()] * len(self.blocks)

    def values(self):
        return [self.places, *self.blocks]

    def scratch(self):
        number = 2 * len(self.blocks)
        return [
            pltpu.VMEM((number * self.rows, self.columns), low_type),
            pltpu.SemaphoreType.DMA((number,)),
        ]


def load_pieces(refs, scratch):
    place_ref, *block_refs = refs
    weight_ref, sem_ref = scratch
    copies = []
    for index, block_ref in enumerate(block_refs):
        rows = block_ref.shape[1]
        for part in range(2):
            number = 2 * index + part
            start = pl.multiple_of(place_ref[number] * rows, rows & -rows)
            copies.append(
                pltpu.make_async_copy(
                    block_ref.at[part], weight_ref.at[pl.ds(start, rows)], sem_ref.at[number]
                )
            )
    for copy in copies:
        copy.start()
    for copy in copies:
        copy.wait()


def halves_body(bit_ref, weight_ref, own_ref, other_ref):
    size = own_ref.shape[1]
    for out_ref, which in ((own_ref, bit_ref[0]), (other_ref, 1 - bit_ref[0])):
        start = pl.multiple_of(which * size, size & -size)
        out_ref[...] = weight_ref[:, pl.ds(start, size)].astype(low_type)


def halves(bit, weight, layer=None):
    rows, columns = weight.shape[-2:]
    step = rows // 5
    if layer is None:
        spec = pl.BlockSpec((step, columns), lambda i: (i, 0))
    else:
        spec = pl.BlockSpec((pl.squeezed, step, columns), lambda i: (layer, i, 0))
    half = pl.BlockSpec((step, columns // 2), lambda i: (i, 0))
    return call(
        halves_body,
        (5,),
        [smem_spec(), spec],
        [half, half],
        [shape((rows, columns // 2), low_type)] * 2,
    )(bit.astype(jnp.int32).reshape(1), weight)


def pack_body(*refs):
    *parts, out_ref = refs
    start = 0
    for part in parts:
        if len(part.shape) == 2:
            out_ref[start] = part[...]
            start += 1
        else:
            out_ref[start : start + part.shape[0]] = part[...]
            start += part.shape[0]


def pack(*parts):
    rows, width = parts[0].shape[-2:]
    step = width // 2
    specs, number = [], 0
    for part in parts:
        if part.ndim == 2:
            specs.append(pl.BlockSpec((rows, step), lambda n: (0, n)))
            number += 1
        else:
            specs.append(pl.BlockSpec((part.shape[0], rows, step), lambda n: (0, 0, n)))
            number += part.shape[0]
    return call(
        pack_body,
        (2,),
        specs,
        pl.BlockSpec((number, rows, step), lambda n: (0, 0, n)),
        shape((number, rows, width), parts[0].dtype),
    )(*parts)


def both_cores(near_ref, far_ref):
    return jnp.concatenate([near_ref[0], far_ref[0]], axis=0)


def project_body(count, x_ref, xc_ref, cos_ref, sin_ref, *refs):
    pieces = refs[:count]
    at_ref, q_ref, kv_ref, g_ref, w_ref, sem_ref = refs[count:]

    @pl.when(pl.program_id(0) == 0)
    def _():
        load_pieces(pieces, (w_ref, sem_ref))
        turned = w_ref[:, 384:].astype(wide_type).T
        g_ref[...] = turned[EDGE - 384 : EDGE - 384 + 2]

    x = both_cores(x_ref, xc_ref).astype(wide_type)
    rows = x.shape[0]
    unit = x * lax.rsqrt(jnp.mean(x * x, axis=-1, keepdims=True) + eps_norm)
    normed = (unit * g_ref[0:1]).astype(low_type)
    at_ref[...] = normed.T
    flat = dot(w_ref[...], normed, 0, 1)
    cos, sin = cos_ref[0], sin_ref[0]

    def rotated(start):
        first = flat[start : start + HALF]
        second = flat[start + HALF : start + HEAD_SIZE]
        return jnp.concatenate(
            [first * cos - second * sin, second * cos + first * sin], axis=0
        ).astype(low_type)

    for head in range(GROUP):
        q_ref[0, :, head * rows : (head + 1) * rows] = rotated(head * HEAD_SIZE)
    kv_ref[0] = jnp.concatenate(
        [rotated(QROWS), flat[QROWS + HEAD_SIZE : EDGE].astype(low_type)], axis=0
    )


def project(near, far, weight, cos, sin):
    tiles, per, width = near.shape
    wide = 2 * per
    return call(
        functools.partial(project_body, weight.count()),
        (tiles,),
        [
            tile_of(1, per, width),
            tile_of(1, per, width),
            tile_of(1, HALF, wide),
            tile_of(1, HALF, wide),
            *weight.specs(),
        ],
        [
            pl.BlockSpec((width, wide), lambda t: (0, t)),
            tile_of(1, HEAD_SIZE, GROUP * wide),
            tile_of(1, BOTH, wide),
            pl.BlockSpec((2, width), lambda t: (0, 0)),
        ],
        [
            shape((width, tiles * wide), low_type),
            shape((tiles, HEAD_SIZE, GROUP * wide), low_type),
            shape((tiles, BOTH, wide), low_type),
            shape((2, width), wide_type),
        ],
        weight.scratch(),
    )(near, far, cos, sin, *weight.values())


def load_keys(kv_refs, kv_ref, sem_ref):
    copies, start = [], 0
    for index, part in enumerate(kv_refs):
        size = part.shape[0]
        copies.append(
            pltpu.make_async_copy(part, kv_ref.at[start : start + size], sem_ref.at[index])
        )
        start += size
    for copy in copies:
        copy.start()
    for copy in copies:
        copy.wait()


def attend_body(count, seen_ref, base_ref, q_ref, pos_ref, start_ref, local_ref, *refs):
    kv_parts, pieces = refs[:4], refs[4 : 4 + count]
    o_ref, ot_ref, lse_ref, near_ref, far_ref = refs[4 + count : 9 + count]
    top_ref, sum_ref, acc_ref, kv_ref, kv_sem, w_ref, sem_ref = refs[9 + count :]
    tile = pl.program_id(0)
    key_tiles = kv_ref.shape[0]

    @pl.when(tile == 0)
    def _():
        load_keys(kv_parts, kv_ref, kv_sem)
        load_pieces(pieces, (w_ref, sem_ref))

    top_ref[...] = jnp.full(top_ref.shape, masked_score, wide_type)
    sum_ref[...] = jnp.zeros(sum_ref.shape, wide_type)
    acc_ref[...] = jnp.zeros(acc_ref.shape, wide_type)

    def step(k, carry):
        @pl.when(seen_ref[tile * key_tiles + k] != 0)
        def _():
            raw = dot(kv_ref[k, :HEAD_SIZE], q_ref[0], 0, 0)
            key_pos = base_ref[k] + local_ref[...]
            allowed = (key_pos <= pos_ref[0]) & (key_pos >= start_ref[0])
            raw = jnp.where(allowed, raw, masked_score)
            top_old = top_ref[...]
            top = jnp.maximum(top_old, jnp.max(raw, axis=0, keepdims=True))
            shrink = jnp.exp2((top_old - top) * EXP_SCALE)
            probs = jnp.where(allowed, jnp.exp2((raw - top) * EXP_SCALE), 0.0)
            sum_ref[...] = sum_ref[...] * shrink + jnp.sum(probs, axis=0, keepdims=True)
            acc_ref[...] = acc_ref[...] * shrink + dot(
                kv_ref[k, HEAD_SIZE:], probs.astype(low_type), 1, 0
            )
            top_ref[...] = top

        return carry

    lax.fori_loop(0, key_tiles, step, 0)
    out = acc_ref[...] / sum_ref[...]
    ot_ref[0] = out
    lse_ref[0] = top_ref[...] * EXP_SCALE + jnp.log2(sum_ref[...])
    rows = out.shape[1] // GROUP
    stacked = jnp.concatenate(
        [out[:, head * rows : (head + 1) * rows] for head in range(GROUP)], axis=0
    )
    attended = stacked.T.astype(low_type)
    o_ref[0] = attended
    branch = dot(attended, w_ref[...], 1, 1)
    near_ref[0] = branch[: rows // 2].astype(low_type)
    far_ref[0] = branch[rows // 2 :].astype(low_type)


def key_scratch(kv):
    number = sum(part.shape[0] for part in kv)
    return [
        pltpu.VMEM((number, *kv[0].shape[1:]), low_type),
        pltpu.SemaphoreType.DMA((len(kv),)),
    ]


def attend(layout, kv, weight):
    seen, base, q, pos, start, local = layout
    tiles, _, columns = q.shape
    wide = kv[0].shape[2]
    width = 2 * len(weight.blocks) * weight.rows
    return call(
        functools.partial(attend_body, weight.count()),
        (tiles,),
        [
            smem_spec(),
            smem_spec(),
            tile_of(1, HEAD_SIZE, columns),
            tile_of(1, 1, columns),
            tile_of(1, 1, columns),
            whole(local),
            *[any_spec()] * 4,
            *weight.specs(),
        ],
        [
            tile_of(1, wide, QROWS),
            tile_of(1, HEAD_SIZE, columns),
            tile_of(1, 1, columns),
            tile_of(1, wide // 2, width),
            tile_of(1, wide // 2, width),
        ],
        [
            shape((tiles, wide, QROWS), low_type),
            shape((tiles, HEAD_SIZE, columns), wide_type),
            shape((tiles, 1, columns), wide_type),
            shape((tiles, wide // 2, width), low_type),
            shape((tiles, wide // 2, width), low_type),
        ],
        [
            pltpu.VMEM((1, columns), wide_type),
            pltpu.VMEM((1, columns), wide_type),
            pltpu.VMEM((HEAD_SIZE, columns), wide_type),
            *key_scratch(kv),
            *weight.scratch(),
        ],
    )(*layout, *kv, *weight.values())


def attend_back_body(
    count, seen_ref, base_ref, q_ref, pos_ref, start_ref, local_ref,
    z_ref, zc_ref, ot_ref, lse_ref, cos_ref, sin_ref, *refs,
):
    kv_parts, pieces = refs[:4], refs[4 : 4 + count]
    dq_ref, *dkv_parts = refs[4 + count : 9 + count]
    acc_ref, dkv_ref, kv_ref, kv_sem, w_ref, sem_ref = refs[9 + count :]
    tile = pl.program_id(0)
    key_tiles = kv_ref.shape[0]

    @pl.when(tile == 0)
    def _():
        load_keys(kv_parts, kv_ref, kv_sem)
        load_pieces(pieces, (w_ref, sem_ref))
        dkv_ref[...] = jnp.zeros(dkv_ref.shape, wide_type)

    rows = q_ref.shape[2] // GROUP
    turned = dot(w_ref[...], both_cores(z_ref, zc_ref), 0, 1).astype(low_type)
    grad_out = jnp.concatenate(
        [turned[head * HEAD_SIZE : (head + 1) * HEAD_SIZE] for head in range(GROUP)], axis=1
    )
    delta = jnp.sum(grad_out.astype(wide_type) * ot_ref[0], axis=0, keepdims=True)
    acc_ref[...] = jnp.zeros(acc_ref.shape, wide_type)

    def step(k, carry):
        @pl.when(seen_ref[tile * key_tiles + k] != 0)
        def _():
            raw = dot(kv_ref[k, :HEAD_SIZE], q_ref[0], 0, 0)
            key_pos = base_ref[k] + local_ref[...]
            allowed = (key_pos <= pos_ref[0]) & (key_pos >= start_ref[0])
            probs = jnp.where(allowed, jnp.exp2(raw * EXP_SCALE - lse_ref[0]), 0.0)
            grad_probs = dot(kv_ref[k, HEAD_SIZE:], grad_out, 0, 0)
            grad_scores = (probs * (grad_probs - delta)).astype(low_type)
            acc_ref[...] += dot(kv_ref[k, :HEAD_SIZE], grad_scores, 1, 0)
            dkv_ref[k, :HEAD_SIZE] += dot(q_ref[0], grad_scores, 1, 1) * SCALE
            dkv_ref[k, HEAD_SIZE:] += dot(grad_out, probs.astype(low_type), 1, 1)

        return carry

    lax.fori_loop(0, key_tiles, step, 0)
    cos, sin = cos_ref[0], sin_ref[0]
    for head in range(GROUP):
        part = acc_ref[:, head * rows : (head + 1) * rows] * SCALE
        first, second = part[:HALF], part[HALF:]
        dq_ref[0, head * HEAD_SIZE : (head + 1) * HEAD_SIZE] = jnp.concatenate(
            [first * cos + second * sin, second * cos - first * sin], axis=0
        ).astype(low_type)

    @pl.when(tile == pl.num_programs(0) - 1)
    def _():
        start = 0
        for part in dkv_parts:
            size = part.shape[0]
            part[...] = dkv_ref[start : start + size].astype(part.dtype)
            start += size


def attend_back(layout, kv, weight, near, far, out_turned, lse, cos, sin):
    seen, base, q, pos, start, local = layout
    tiles, _, columns = q.shape
    wide = kv[0].shape[2]
    width = near.shape[2]
    kinds = (wide_type, low_type, low_type, low_type)
    held = key_scratch(kv)
    return call(
        functools.partial(attend_back_body, weight.count()),
        (tiles,),
        [
            smem_spec(),
            smem_spec(),
            tile_of(1, HEAD_SIZE, columns),
            tile_of(1, 1, columns),
            tile_of(1, 1, columns),
            whole(local),
            tile_of(1, wide // 2, width),
            tile_of(1, wide // 2, width),
            tile_of(1, HEAD_SIZE, columns),
            tile_of(1, 1, columns),
            tile_of(1, HALF, wide),
            tile_of(1, HALF, wide),
            *[any_spec()] * 4,
            *weight.specs(),
        ],
        [tile_of(1, QROWS, wide)] + [whole(part) for part in kv],
        [shape((tiles, QROWS, wide), low_type)]
        + [shape(part.shape, kind) for part, kind in zip(kv, kinds)],
        [
            pltpu.VMEM((HEAD_SIZE, columns), wide_type),
            pltpu.VMEM(held[0].shape, wide_type),
            *held,
            *weight.scratch(),
        ],
    )(*layout, near, far, out_turned, lse, cos, sin, *kv, *weight.values())


def finish_body(late_ref, dq_ref, own_ref, y_ref, a_ref, b_ref, cos_ref, sin_ref, out_ref):
    late = (pl.program_id(0) // 2 == late_ref[0]).astype(wide_type)
    total = own_ref[0] + y_ref[0].astype(wide_type)
    total = total + late * (a_ref[0].astype(wide_type) + b_ref[0].astype(wide_type))
    cos, sin = cos_ref[0], sin_ref[0]
    first, second = total[:HALF], total[HALF:HEAD_SIZE]
    turned = jnp.concatenate(
        [
            dq_ref[0].astype(wide_type),
            first * cos + second * sin,
            second * cos - first * sin,
            total[HEAD_SIZE:],
            jnp.zeros((2, total.shape[1]), wide_type),
        ],
        axis=0,
    )
    out_ref[0] = turned.T.astype(low_type)


def finish(late, dq, own, from_y, from_a, from_b, cos, sin):
    tiles, _, wide = dq.shape
    return call(
        finish_body,
        (tiles,),
        [
            smem_spec(),
            tile_of(1, QROWS, wide),
            tile_of(1, BOTH, wide),
            tile_of(1, BOTH, wide),
            pl.BlockSpec((1, BOTH, wide), lambda t: (t % 2, 0, 0)),
            pl.BlockSpec((1, BOTH, wide), lambda t: (t % 2, 0, 0)),
            tile_of(1, HALF, wide),
            tile_of(1, HALF, wide),
        ],
        tile_of(1, wide, EDGE + 2),
        shape((tiles, wide, EDGE + 2), low_type),
    )(late, dq, own, from_y, from_a, from_b, cos, sin)


def turn_body(near_ref, far_ref, out_ref):
    out_ref[...] = both_cores(near_ref, far_ref).T


def turn(near, far):
    tiles, per, width = near.shape
    return call(
        turn_body,
        (tiles,),
        [tile_of(1, per, width), tile_of(1, per, width)],
        pl.BlockSpec((width, 2 * per), lambda t: (0, t)),
        shape((width, 2 * per * tiles), low_type),
    )(near, far)


def ffn_body(count, near_ref, far_ref, *refs):
    gate_pieces, up_pieces = refs[:count], refs[count : 2 * count]
    at_ref, hid_ref, one_ref, two_ref, gate_ref, gate_sem, up_ref, up_sem = refs[2 * count :]

    @pl.when(pl.program_id(0) == 0)
    def _():
        load_pieces(gate_pieces, (gate_ref, gate_sem))
        load_pieces(up_pieces, (up_ref, up_sem))

    normed = both_cores(near_ref, far_ref)
    at_ref[...] = normed.T
    gate = dot(normed, gate_ref[...], 1, 0)
    upward = dot(normed, up_ref[...], 1, 0)
    sigma = 1.0 / (1.0 + jnp.exp(-gate))
    passed = gate * sigma
    hid_ref[0] = (passed * upward).astype(low_type)
    one_ref[0] = upward * sigma * (1.0 + gate * (1.0 - sigma))
    two_ref[0] = passed


def ffn(near, far, gate_weight, up_weight):
    tiles, per, width = near.shape
    wide = 2 * per
    hidden = gate_weight.columns
    return call(
        functools.partial(ffn_body, gate_weight.count()),
        (tiles,),
        [
            tile_of(1, per, width),
            tile_of(1, per, width),
            *gate_weight.specs(),
            *up_weight.specs(),
        ],
        [
            pl.BlockSpec((width, wide), lambda t: (0, t)),
            tile_of(1, wide, hidden),
            tile_of(1, wide, hidden),
            tile_of(1, wide, hidden),
        ],
        [
            shape((width, tiles * wide), low_type),
            shape((tiles, wide, hidden), low_type),
            shape((tiles, wide, hidden), wide_type),
            shape((tiles, wide, hidden), wide_type),
        ],
        gate_weight.scratch() + up_weight.scratch(),
    )(near, far, *gate_weight.values(), *up_weight.values())


def ffn_back_body(count, near_ref, far_ref, one_ref, two_ref, *refs):
    dgate_ref, dup_ref, w_ref, sem_ref = refs[count:]

    @pl.when(pl.program_id(0) == 0)
    def _():
        load_pieces(refs[:count], (w_ref, sem_ref))

    grad_hidden = dot(both_cores(near_ref, far_ref), w_ref[...], 1, 0)
    dgate_ref[0] = (grad_hidden * one_ref[0]).astype(low_type)
    dup_ref[0] = (grad_hidden * two_ref[0]).astype(low_type)


def ffn_back(near, far, weight, one, two):
    tiles, per, width = near.shape
    wide = 2 * per
    hidden = weight.columns
    part = tile_of(1, wide, hidden)
    return call(
        functools.partial(ffn_back_body, weight.count()),
        (tiles,),
        [tile_of(1, per, width), tile_of(1, per, width), part, part, *weight.specs()],
        [part, part],
        [shape((tiles, wide, hidden), low_type)] * 2,
        weight.scratch(),
    )(near, far, one, two, *weight.values())


def put_blocks(total, out_refs):
    for index, out_ref in enumerate(out_refs):
        out_ref[...] = total[index].astype(out_ref.dtype)


def block_outputs(per, width, step):
    spec = pl.BlockSpec((per, step), lambda n: (0, n))
    kinds = (wide_type, low_type, low_type, low_type)
    return [spec] * 4, [shape((per, width), kind) for kind in kinds]


def combine_body(near_ref, got_ref, *out_refs):
    put_blocks(near_ref[...].astype(wide_type) + got_ref[...].astype(wide_type), out_refs)


def combine(near, got):
    blocks, per, width = near.shape
    step = width // 2
    spec = pl.BlockSpec((blocks, per, step), lambda n: (0, 0, n))
    out_specs, out_shape = block_outputs(per, width, step)
    return call(combine_body, (width // step,), [spec, spec], out_specs, out_shape)(near, got)


def branch_body(lefts, count, with_got, *refs):
    left_refs, refs = refs[:lefts], refs[lefts:]
    pieces, refs = [refs[i * count : (i + 1) * count] for i in range(lefts)], refs[lefts * count :]
    got_ref, refs = (refs[0], refs[1:]) if with_got else (None, refs)
    outs, scratch = refs[: -2 * lefts], refs[-2 * lefts :]
    step = outs[0].shape[-1]

    @pl.when(pl.program_id(0) == 0)
    def _():
        for index in range(lefts):
            load_pieces(pieces[index], scratch[2 * index : 2 * index + 2])

    start = pl.multiple_of(pl.program_id(0) * step, step)
    total = None
    for index in range(lefts):
        left = left_refs[index][...]
        rows = left.shape[0] * left.shape[2]
        weight = scratch[2 * index][pl.ds(start, step), :]
        term = dot(left.reshape(rows, left.shape[3]), weight, 1, 1)
        total = term if total is None else total + term
    total = total.reshape(4, total.shape[0] // 4, step)
    if got_ref is None:
        outs[0][...] = total.astype(low_type)
    else:
        put_blocks(total + got_ref[...].astype(wide_type), outs)


def branch(pairs, core, got=None):
    step = 512
    specs, lefts, weight_specs, weights, scratch = [], [], [], [], []
    for left, weight in pairs:
        tiles, wide, inner = left.shape
        lefts.append(left.reshape(tiles, 2, wide // 2, inner))
        specs.append(pl.BlockSpec((tiles, 1, wide // 2, inner), lambda n: (0, core, 0, 0)))
        weight_specs += weight.specs()
        weights += weight.values()
        scratch += weight.scratch()
    width = 2 * len(weight.blocks) * weight.rows
    per = wide // 2
    block = pl.BlockSpec((tiles, per, step), lambda n: (0, 0, n))
    if got is None:
        out_specs, out_shape = [block], [shape((tiles, per, width), low_type)]
    else:
        out_specs, out_shape = block_outputs(per, width, step)
    outs = call(
        functools.partial(branch_body, len(pairs), weight.count(), got is not None),
        (width // step,),
        specs + weight_specs + ([] if got is None else [block]),
        out_specs,
        out_shape,
        scratch,
    )(*lefts, *weights, *([] if got is None else [got]))
    return outs[0] if got is None else outs


def weight_body(count, index_ref, first_ref, second_ref, right_ref, *refs):
    left = jnp.concatenate([first_ref[0], second_ref[0]], axis=0)
    total = dot(left, right_ref[...], 1, 0)
    rows = total.shape[0] // 2
    for part in range(2):
        block = total[part * rows : (part + 1) * rows]
        for position in range(count):
            block = block + refs[2 * position + part][0].astype(wide_type)
        refs[-1][part] = block.astype(refs[-1].dtype)


def weight_rows(turned, right, places, addends, kind):
    tokens = turned.shape[1]
    columns = right.shape[-1]
    blocks = lax.axis_size("dp")
    rows = turned.shape[0] // blocks
    number = len(places)
    flat = [jnp.asarray(p, jnp.int32) for p in places]

    def named(offset, part, last):
        return pl.BlockSpec(
            (1, rows, last), lambda i, index: (index[offset + 2 * i + part], 0, 0)
        )

    specs = [
        named(0, 0, tokens),
        named(0, 1, tokens),
        pl.BlockSpec((tokens, columns), lambda i, index: (0, 0)),
    ]
    given = []
    for position, (array, where) in enumerate(addends):
        flat += [jnp.asarray(p, jnp.int32) for p in where]
        for part in range(2):
            specs.append(named((position + 1) * number, part, columns))
            given.append(array)
    left = turned.reshape(blocks, rows, tokens)
    return pl.pallas_call(
        functools.partial(weight_body, len(addends)),
        grid_spec=pltpu.PrefetchScalarGridSpec(
            num_scalar_prefetch=1,
            grid=(number // 2,),
            in_specs=specs,
            out_specs=pl.BlockSpec((2, rows, columns), lambda i, index: (i, 0, 0)),
        ),
        out_shape=shape((number, rows, columns), kind),
        compiler_params=pltpu.CompilerParams(vmem_limit_bytes=VMEM_LIMIT),
        cost_estimate=pl.CostEstimate(flops=10**10, bytes_accessed=0, transcendentals=0),
    )(jnp.stack(flat), left, left, right.reshape(tokens, columns), *given)


def share_first(turned, right):
    _, _, y, _, _ = bits()
    ring = lax.axis_size("dp") // 4
    places = [4 * g + 2 * b + (1 - y) for g in range(ring) for b in range(2)]
    return weight_rows(turned, right, places, [], low_type)


def share_term(turned, right, got, step, travel=None):
    h, l, y, _, _ = bits()
    ring = lax.axis_size("dp") // 4
    group = (h - 1 - step) % ring
    last = step == ring - 1
    order = [l, 1 - l] if last else [0, 1]
    places = [4 * group + 2 * b + y for b in order]
    addends = [(got, [2 * group + b for b in order])]
    if travel is not None:
        addends.append((travel, order))
    return weight_rows(turned, right, places, addends, wide_type if last else low_type)


def share_rest(turned, right, got, term):
    ring = lax.axis_size("dp") // 4
    travel = hop_ring(term)
    for step in range(1, ring - 1):
        travel = hop_ring(share_term(turned, right, got, step, travel))
    return travel


def share_third(turned, right, got, travel):
    ring = lax.axis_size("dp") // 4
    own = share_term(turned, right, got, ring - 1, travel)
    return own[0], own[1].astype(low_type), jnp.sum(jnp.square(own))


def adamw(param, grad, first, second):
    first_new = beta_first * first + (1.0 - beta_first) * grad
    second_new = beta_second * second + (1.0 - beta_second) * grad * grad
    first_hat = first_new / (1.0 - beta_first**STEP)
    second_hat = second_new / (1.0 - beta_second**STEP)
    change = -learn_rate * (first_hat / (jnp.sqrt(second_hat) + adam_eps) + weight_decay * param)
    return (first_new, second_new, change)


def on_device(
    tokens,
    upstream,
    offsets,
    query_weight,
    keyval_weight,
    output_weight,
    gateup_weight,
    down_weight,
    norm_gains,
    first_query,
    first_keyval,
    first_output,
    first_gateup,
    first_down,
    first_gains,
    second_query,
    second_keyval,
    second_output,
    second_gateup,
    second_down,
    second_gains,
):
    h, l, y, xbit, cbit = bits()
    pin = Windows(norm_gains)
    ring = lax.axis_size("dp") // 4
    block_rows = offsets.shape[0]
    per, width = tokens.shape
    wide = 2 * per

    def split(bit, arrays, more=()):
        lower, upper = [], []
        for array in arrays:
            half = array.shape[-1] // 2
            lower.append(array[:, :half].astype(low_type))
            upper.append(array[:, half:].astype(low_type))
        lower = jnp.concatenate([*lower, *more], axis=1)
        upper = jnp.concatenate([*upper, *more], axis=1)
        return choose(bit, lower, upper), choose(bit, upper, lower)

    def paired(own, other):
        return ordered(l, own[None], other[None], 0)

    places = jnp.stack(
        [
            4 * ((h - step) % ring) + 2 * b + (y ^ flip)
            for step in range(ring)
            for flip in range(2)
            for b in range(2)
        ]
    ).astype(jnp.int32)

    def legs(pair, pair_y, rings, rings_y):
        blocks = [pair, pair_y]
        for block, block_y in zip(rings, rings_y):
            blocks += [block, block_y]
        return Pieces(blocks, places)

    def arrived(own, *others):
        for other in others:
            own = own + other.astype(wide_type)
        return own

    def onward(block, corner):
        return (block.astype(wide_type) + corner.astype(wide_type)).astype(low_type)

    gain_columns = norm_gains.astype(low_type).T
    q_own, q_other = split(
        l, [query_weight, keyval_weight[0], keyval_weight[1]], [gain_columns]
    )
    o_own, o_other = split(l, [output_weight])
    q_other, o_other, other_offsets = hop_low(q_other), hop_low(o_other), hop_low(offsets)

    q_other, o_other, other_offsets, bit, own_rows = pin(
        q_other, o_other, other_offsets, l, tokens
    )
    q_pair = paired(q_own, q_other)
    q_ring, q_y = hop_ring(q_pair), hop_y(q_pair)
    tx, tz = hop_x(own_rows), hop_low(own_rows)
    o_pair = paired(o_own, o_other)
    g_own, g_other = halves(bit, gateup_weight, 0)

    def relative(own):
        four = own.reshape(2, 2, per)
        four = choose(xbit, four, four[::-1])
        return choose(cbit, four, four[:, ::-1])

    offset_tiles = jnp.concatenate([relative(offsets), relative(other_offsets)], axis=0)
    offset_tiles = offset_tiles.reshape(4, wide)
    lane = jnp.arange(wide, dtype=jnp.int32)
    local = choose(cbit, lane, lane ^ per)
    mine = jnp.arange(4, dtype=jnp.int32)

    def bases(group_h, group_y, low_bits, x_bits):
        block = 4 * group_h + 2 * low_bits + group_y
        return block * block_rows + x_bits * wide

    low_bits, x_bits = l ^ (mine // 2), xbit ^ (mine % 2)
    own_base = bases(h, y, low_bits, x_bits)
    one = jnp.ones((2,), jnp.int32)
    key_base = jnp.concatenate(
        [
            own_base,
            bases(h, 1 - y, low_bits, x_bits),
            bases(h - 1, y, one, x_bits[:2]),
            bases(h - 1, 1 - y, one, x_bits[:2]),
        ]
    ).astype(jnp.int32)
    query_pos = own_base[:, None] + local[None, :]
    doc_start = query_pos - offset_tiles
    seen = (
        (key_base[None, :] <= own_base[:, None] + wide - 1)
        & (key_base[None, :] + wide - 1 >= jnp.min(doc_start, axis=1, keepdims=True))
    ).astype(jnp.int32).reshape(-1)
    spread = lambda a: jnp.tile(a, (1, GROUP)).reshape(4, 1, GROUP * wide)
    query_lanes, start_lanes = spread(query_pos), spread(doc_start)
    local_column = local.reshape(wide, 1)
    freqs = rope_base ** (-(jnp.arange(HALF).astype(wide_type) * 2.0 / HEAD_SIZE))
    angle = freqs[None, :, None] * offset_tiles.astype(wide_type)[:, None, :]
    cos, sin = jnp.cos(angle), jnp.sin(angle)

    tx, tz, g_other, bit = pin(tx, tz, g_other, bit)
    tf = hop_x(tz)
    g_other = hop_low(g_other)
    u_own, u_other = halves(bit, gateup_weight, 1)

    q_ring, q_y, o_pair = pin.apart(q_ring, q_y, o_pair)
    q_far = rest_of_ring(q_ring)
    q_far_y = [hop_y(block) for block in q_far]
    o_ring = hop_ring(o_pair)

    tf, bit, up_own = pin(tf, bit, upstream)
    near = pack(own_rows, tx, tz, tf)
    far = hop_core(near)
    d_own, d_other = halves(bit, down_weight)

    far, g_other, u_other, up_own, d_other, o_pair, *q_far_y = pin(
        far, g_other, u_other, up_own, d_other, o_pair, *q_far_y
    )
    u_other = hop_low(u_other)
    g_pair = paired(g_own, g_other)

    qkv_full = legs(q_pair, q_y, q_far, q_far_y)
    turned_one, q_turned, kv_own, gains = project(near, far, qkv_full, cos, sin)
    d_other, o_y, ux = hop_low(d_other), hop_y(o_pair), hop_x(up_own)

    kv_own, o_y, o_ring, u_other, ux = pin(kv_own, o_y, o_ring, u_other, ux)
    late = choose(l, kv_own[2:], kv_own[:2])
    kv_a, kv_b, kv_y = to_next(late, 0), to_next(late, 1), hop_y(kv_own)
    o_far = rest_of_ring(o_ring)
    o_far_y = [hop_y(block) for block in o_far]
    u_pair = paired(u_own, u_other)

    kv_y, kv_a, kv_b, g_pair, up_own, d_other, *o_far_y = pin(
        kv_y, kv_a, kv_b, g_pair, up_own, d_other, *o_far_y
    )
    g_ring, g_y = hop_ring(g_pair), hop_y(g_pair)
    uz = hop_low(up_own)
    d_pair = paired(d_own, d_other)

    (q_turned,) = pin.apart(q_turned)
    output_full = legs(o_pair, o_y, o_far, o_far_y)
    layout = (seen, key_base, q_turned, query_lanes, start_lanes, local_column)
    kv = (kv_own, kv_y, kv_a, kv_b)
    attended, out_turned, lse, branch_near, branch_far = attend(layout, kv, output_full)
    z_got = hop_core(branch_far)

    z_got, g_y, u_pair = pin(z_got, g_y, u_pair)
    z_own, z_x, z_low, z_corner = combine(branch_near, z_got)
    zc = hop_x(z_corner)
    u_y = hop_y(u_pair)
    inputs = tokens.astype(wide_type)
    inverse_one = lax.rsqrt(jnp.mean(inputs * inputs, axis=-1, keepdims=True) + eps_norm)
    unit_one = inputs * inverse_one

    zc, z_x, g_ring, u_pair, uz = pin(zc, z_x, g_ring, u_pair, uz)
    zz, zx = hop_low(onward(z_low, zc)), hop_x(z_x)
    g_far = rest_of_ring(g_ring)
    u_ring = hop_ring(u_pair)

    zx, zz, u_y, uz = pin(zx, zz, u_y, uz)
    g_far_y = [hop_y(block) for block in g_far]
    middle = inputs + arrived(z_own, zx, zz)
    inverse_two = lax.rsqrt(jnp.mean(middle * middle, axis=-1, keepdims=True) + eps_norm)
    unit_two = middle * inverse_two
    own_two = (unit_two * gains[1]).astype(low_type)
    az, ax = hop_low(own_two), hop_x(own_two)

    ax, az, u_ring, d_pair, uz, *g_far_y = pin(ax, az, u_ring, d_pair, uz, *g_far_y)
    af = hop_x(az)
    u_far = rest_of_ring(u_ring)
    u_far_y = [hop_y(block) for block in u_far]
    d_ring = hop_ring(d_pair)
    gate_full = legs(g_pair, g_y, g_far, g_far_y)

    af, d_pair, uz = pin(af, d_pair, uz)
    near_two = pack(own_two, ax, az, af)
    far_two = hop_core(near_two)
    d_y, uf = hop_y(d_pair), hop_x(uz)

    far_two, *u_far_y = pin(far_two, *u_far_y)
    up_full = legs(u_pair, u_y, u_far, u_far_y)
    turned_two, hidden, first_factor, second_factor = ffn(
        near_two, far_two, gate_full, up_full
    )

    d_ring, d_y, uf, hidden = pin(d_ring, d_y, uf, hidden)
    d_far = rest_of_ring(d_ring)
    d_far_y = [hop_y(block) for block in d_far]
    near_up = pack(up_own, ux, uz, uf)
    far_up = hop_core(near_up)
    turned_up = turn(near_up, far_up)
    down_first = share_first(turned_up, hidden)

    down_first, hidden, *d_far_y = pin(down_first, hidden, *d_far_y)
    down_sent = hop_y(down_first)
    down_full = legs(d_pair, d_y, d_far, d_far_y)
    grad_gate, grad_up = ffn_back(near_up, far_up, down_full, first_factor, second_factor)
    ffn_pairs = [(grad_gate, gate_full), (grad_up, up_full)]
    s_got = hop_core(branch(ffn_pairs, 1))
    gate_first = share_first(turned_two, grad_gate)

    s_got, grad_up, gate_first = pin(s_got, grad_up, gate_first)
    s_own, s_x, s_low, s_corner = branch(ffn_pairs, 0, s_got)
    sc = hop_x(s_corner)

    sc, s_x, grad_up = pin(sc, s_x, grad_up)
    sz, sx = hop_low(onward(s_low, sc)), hop_x(s_x)
    up_first = share_first(turned_two, grad_up)

    sx, sz, down_got, gate_first, up_first, hidden = pin(
        sx, sz, down_sent, gate_first, up_first, hidden
    )
    grad_normed_two = arrived(s_own, sx, sz)
    gain_two = jnp.sum(grad_normed_two * unit_two, axis=0)
    grad_middle = upstream.astype(wide_type) + norm_back(
        grad_normed_two, unit_two, inverse_two, gains[1]
    )
    own_three = grad_middle.astype(low_type)
    bz, bx = hop_low(own_three), hop_x(own_three)
    gate_sent = hop_y(gate_first)
    down_travel = share_rest(
        turned_up, hidden, down_got, share_term(turned_up, hidden, down_got, 0)
    )

    bx, bz = pin(bx, bz)
    bf = hop_x(bz)

    (bf,) = pin(bf)
    near_three = pack(own_three, bx, bz, bf)
    far_three = hop_core(near_three)

    (far_three,) = pin(far_three)
    dq_turned, dkv_own, dkv_y, dkv_a, dkv_b = attend_back(
        layout, kv, output_full, near_three, far_three, out_turned, lse, cos, sin
    )

    dkv_y, dkv_a, dkv_b, gate_got, down_travel, up_first = pin(
        dkv_y, dkv_a, dkv_b, gate_sent, down_travel, up_first
    )
    dkv_a, dkv_b, dkv_y = to_previous(dkv_a, 0), to_previous(dkv_b, 1), hop_y(dkv_y)
    up_sent = hop_y(up_first)
    gate_term = share_term(turned_two, grad_gate, gate_got, 0)

    dkv_y, dkv_a, dkv_b, gate_term, near_three = pin(
        dkv_y, dkv_a, dkv_b, gate_term, near_three
    )
    gate_travel = share_rest(turned_two, grad_gate, gate_got, gate_term)

    dq_turned, near_three = pin.apart(dq_turned, near_three)
    dqkv = finish(
        (1 - l).astype(jnp.int32).reshape(1), dq_turned, dkv_own, dkv_y, dkv_a, dkv_b, cos, sin
    )
    attn_pairs = [(dqkv, qkv_full)]
    r_got = hop_core(branch(attn_pairs, 1))
    turned_three = turn(near_three, far_three)
    output_first = share_first(turned_three, attended)

    r_got, dqkv, output_first = pin(r_got, dqkv, output_first)
    output_sent = hop_y(output_first)
    r_own, r_x, r_low, r_corner = branch([(dqkv, qkv_full)], 0, r_got)
    rc = hop_x(r_corner)
    qkv_first = share_first(turned_one, dqkv)

    rc, r_x, up_got, qkv_first, down_travel = pin(rc, r_x, up_sent, qkv_first, down_travel)
    rz, rx = hop_low(onward(r_low, rc)), hop_x(r_x)
    up_travel = share_rest(
        turned_two, grad_up, up_got, share_term(turned_two, grad_up, up_got, 0)
    )

    down_travel, qkv_first = pin.apart(down_travel, qkv_first)
    down_mine, down_theirs, down_square = share_third(turned_up, hidden, down_got, down_travel)

    rx, rz, gate_travel, output_got, down_theirs, qkv_first = pin(
        rx, rz, gate_travel, output_sent, down_theirs, qkv_first
    )
    qkv_sent = hop_y(qkv_first)
    down_other = hop_low(down_theirs)

    hidden, gate_travel, output_got, rx = pin.apart(hidden, gate_travel, output_got, rx)
    f_got = hop_core(branch([(hidden, down_full)], 1))
    output_term = share_term(turned_three, attended, output_got, 0)
    grad_normed_one = arrived(r_own, rx, rz)
    gain_one = jnp.sum(grad_normed_one * unit_one, axis=0)
    grad_tokens = grad_middle + norm_back(grad_normed_one, unit_one, inverse_one, gains[0])
    gate_mine, gate_theirs, gate_square = share_third(
        turned_two, grad_gate, gate_got, gate_travel
    )
    gate_other = hop_low(gate_theirs)

    f_got, qkv_got, output_term, down_other = pin(f_got, qkv_sent, output_term, down_other)
    output_travel = share_rest(turned_three, attended, output_got, output_term)
    qkv_travel = share_rest(
        turned_one, dqkv, qkv_got, share_term(turned_one, dqkv, qkv_got, 0)
    )

    up_travel, gate_other = pin.apart(up_travel, gate_other)
    up_mine, up_theirs, up_square = share_third(turned_two, grad_up, up_got, up_travel)

    up_theirs, hidden, f_got = pin(up_theirs, hidden, f_got)
    up_other = hop_low(up_theirs)

    hidden, f_got = pin.apart(hidden, f_got)
    f_own, f_x, f_low, f_corner = branch([(hidden, down_full)], 0, f_got)
    fc = hop_x(f_corner)

    fc, f_x, gain_one = pin(fc, f_x, gain_one)
    fz, fx = hop_low(onward(f_low, fc)), hop_x(f_x)

    (output_travel,) = pin.apart(output_travel)
    output_mine, output_theirs, output_square = share_third(
        turned_three, attended, output_got, output_travel
    )
    output_other = hop_low(output_theirs)
    square_row = jnp.full(
        (1, width), (down_square + gate_square + up_square + output_square) / width
    )
    sums = jnp.concatenate([gain_one[None], gain_two[None], square_row], axis=0)

    qkv_travel, sums, up_other = pin(qkv_travel, sums, up_other)
    qkv_mine, qkv_theirs, qkv_square = share_third(turned_one, dqkv, qkv_got, qkv_travel)
    qkv_other = hop_low(qkv_theirs)
    last_row = (jnp.arange(3) == 2).astype(wide_type)[:, None]
    totals = sums + last_row * (qkv_square / width)
    totals = totals + hop_core(totals)

    totals = sum_rest(totals + hop_x(totals))
    totals, qkv_other, output_other, fx, fz = pin(totals, qkv_other, output_other, fx, fz)
    block_out = (middle + arrived(f_own, fx, fz)).astype(low_type)
    totals = totals + hop_low(totals)
    gain_total = totals[:2]
    grad_norm = jnp.sqrt(totals[2, 0] * width + jnp.sum(gain_total * gain_total))
    def joined(mine, other, start, stop):
        return ordered(l, mine[:, start:stop], other[:, start:stop].astype(wide_type), 1)

    edge_one = QROWS + HEAD_SIZE
    hidden_part = down_mine.shape[1]
    grad_query = joined(qkv_mine, qkv_other, 0, QROWS)
    grad_keyval = jnp.stack(
        [
            joined(qkv_mine, qkv_other, QROWS, edge_one).T,
            joined(qkv_mine, qkv_other, edge_one, EDGE).T,
        ]
    )
    grad_output = joined(output_mine, output_other, 0, QROWS)
    grad_gateup = jnp.stack(
        [
            joined(gate_mine, gate_other, 0, hidden_part),
            joined(up_mine, up_other, 0, hidden_part),
        ]
    )
    grad_down = joined(down_mine, down_other, 0, hidden_part)
    rows_owned = query_weight.shape[0]
    grad_gains = lax.dynamic_slice_in_dim(
        gain_total, lax.axis_index("dp") * rows_owned, rows_owned, 1
    )
    clipping_bound = math.sqrt(
        MODEL_WIDTH
        * (2 * QUERY_HEAD_COUNT * HEAD_SIZE + 2 * KEY_VALUE_HEADS * HEAD_SIZE + 3 * HIDDEN_UNITS)
        + 2 * MODEL_WIDTH
    )
    clip = jnp.minimum(1.0, clipping_bound / (grad_norm + 1e-06))
    params = (query_weight, keyval_weight, output_weight, gateup_weight, down_weight, pin.held)
    firsts = (first_query, first_keyval, first_output, first_gateup, first_down, first_gains)
    seconds = (second_query, second_keyval, second_output, second_gateup, second_down, second_gains)
    grads = (grad_query, grad_keyval, grad_output, grad_gateup, grad_down, grad_gains)
    turned = lambda a: jnp.swapaxes(a, 1, 2)
    states = [
        adamw(params[index], grads[index] * clip, firsts[index], seconds[index])
        if index != 1
        else tuple(
            turned(a)
            for a in adamw(
                turned(params[1]), grads[1] * clip, turned(firsts[1]), turned(seconds[1])
            )
        )
        for index in range(6)
    ]
    grads = (grads[0], turned(grads[1]), *grads[2:])
    return (
        block_out,
        grad_tokens,
        grad_norm,
        *grads,
        *[state[0] for state in states],
        *[state[1] for state in states],
        *[state[2] for state in states],
    )


def solution(mesh):
    weights = (
        P("dp", "mp"),
        P(None, "dp", "mp"),
        P("dp", "mp"),
        P(None, "dp", "mp"),
        P("dp", "mp"),
        P(None, "dp"),
    )
    rows = P(("dp", "mp"), None)
    return jax.shard_map(
        on_device,
        mesh=mesh,
        in_specs=(rows, rows, P("dp"), *weights, *weights, *weights),
        out_specs=(rows, rows, P(), *weights, *weights, *weights, *weights),
        check_vma=False,
    )
```

```python
import functools
import math

import jax
import jax.numpy as jnp
from jax import lax
from jax.experimental import pallas as pl
from jax.experimental.pallas import tpu as pltpu
from jax.sharding import PartitionSpec as P

MODEL_WIDTH = 2560
QUERY_HEAD_COUNT = 32
KEY_VALUE_HEADS = 8
HEAD_SIZE = 80
HIDDEN_UNITS = 7168
STEP = 10

eps_norm = 1e-05
rope_base = 1000000.0
beta_first = 0.9
beta_second = 0.95
learn_rate = 0.02
weight_decay = 0.1
adam_eps = 1e-08
masked_score = -1e30

low_type = jnp.bfloat16
wide_type = jnp.float32

HALF = HEAD_SIZE // 2
GROUP = QUERY_HEAD_COUNT // KEY_VALUE_HEADS
QROWS = GROUP * HEAD_SIZE
BOTH = 2 * HEAD_SIZE
EDGE = QROWS + BOTH
EXP_SCALE = (HEAD_SIZE ** (-0.5)) * math.log2(math.e)
SCALE = HEAD_SIZE ** (-0.5)
AXES = ("dp", "mp")


def hop(block, move):
    dp_size, mp_size = lax.axis_size("dp"), lax.axis_size("mp")
    route = []
    for d in range(dp_size):
        for m in range(mp_size):
            target = move(d, m)
            if target is not None:
                route.append((d * mp_size + m, target[0] * mp_size + target[1]))
    return lax.ppermute(block, AXES, route)


def hop_core(block):
    return hop(block, lambda d, m: (d, m ^ 1))


def hop_x(block):
    return hop(block, lambda d, m: (d, m ^ 2))


def hop_low(block):
    return hop(block, lambda d, m: (d ^ 2, m))


def hop_y(block):
    return hop(block, lambda d, m: (d ^ 1, m))


def hop_ring(block):
    size = lax.axis_size("dp")
    return hop(block, lambda d, m: ((d + 4) % size, m))


def to_next(block, flip):
    size = lax.axis_size("dp")

    def move(d, m):
        if d + 4 >= size or (flip and d % 2 == 0):
            return None
        return (d + 4) ^ flip, m

    return hop(block, move)


def to_previous(block, flip):
    def move(d, m):
        if d < 4 or (flip and d % 2 == 1):
            return None
        return (d - 4) ^ flip, m

    return hop(block, move)


def bits():
    d = lax.axis_index("dp")
    m = lax.axis_index("mp")
    return d // 4, (d // 2) % 2, d % 2, m // 2, m % 2


def choose(bit, if_zero, if_one):
    return jnp.where(bit == 0, if_zero, if_one)


def ordered(bit, mine, other, axis):
    return choose(
        bit,
        jnp.concatenate([mine, other], axis=axis),
        jnp.concatenate([other, mine], axis=axis),
    )


def keep_body(held_ref, out_ref):
    out_ref[...] = held_ref[...]


class Windows:
    def __init__(self, held):
        self.held = held

    def __call__(self, *arrays):
        *given, held = lax.optimization_barrier((*arrays, self.held))
        self.held = pl.pallas_call(
            keep_body,
            out_shape=jax.ShapeDtypeStruct(held.shape, held.dtype),
            cost_estimate=pl.CostEstimate(flops=10**12, bytes_accessed=0, transcendentals=0),
        )(held)
        return given

    def apart(self, *arrays):
        self.held = hop_core(self.held)
        return self(*arrays)


def rest_of_ring(first):
    blocks = [first]
    for _ in range(lax.axis_size("dp") // 4 - 2):
        blocks.append(hop_ring(blocks[-1]))
    return blocks


def sum_rest(value):
    value = value + hop_y(value)
    travel = value
    for _ in range(1, lax.axis_size("dp") // 4):
        travel = hop_ring(travel)
        value = value + travel
    return value


def norm_back(incoming, unit_rows, inverse_root, gain):
    scaled = incoming * gain
    return inverse_root * (
        scaled - unit_rows * jnp.mean(scaled * unit_rows, axis=-1, keepdims=True)
    )


VMEM_LIMIT = 56 * 2**20


def call(body, grid, in_specs, out_specs, out_shape, scratch=(), flops=10**10):
    return pl.pallas_call(
        body,
        grid=grid,
        in_specs=in_specs,
        out_specs=out_specs,
        out_shape=out_shape,
        scratch_shapes=list(scratch),
        compiler_params=pltpu.CompilerParams(vmem_limit_bytes=VMEM_LIMIT),
        cost_estimate=pl.CostEstimate(flops=flops, bytes_accessed=0, transcendentals=0),
    )


def shape(dims, kind):
    return jax.ShapeDtypeStruct(dims, kind)


def whole(array):
    zeros = (0,) * array.ndim
    return pl.BlockSpec(array.shape, lambda *_: zeros)


def tile_of(*dims):
    rest = (0,) * (len(dims) - 1)
    return pl.BlockSpec(dims, lambda t: (t, *rest))


def dot(left, right, left_dim, right_dim):
    return lax.dot_general(
        left, right, (((left_dim,), (right_dim,)), ((), ())), preferred_element_type=wide_type
    )


def any_spec():
    return pl.BlockSpec(memory_space=pl.ANY)


def smem_spec():
    return pl.BlockSpec(memory_space=pltpu.SMEM)


class Pieces:
    def __init__(self, blocks, places):
        self.blocks = blocks
        self.places = places
        _, self.rows, self.columns = blocks[0].shape

    def count(self):
        return 1 + len(self.blocks)

    def specs(self):
        return [smem_spec()] + [any_spec()] * len(self.blocks)

    def values(self):
        return [self.places, *self.blocks]

    def scratch(self):
        number = 2 * len(self.blocks)
        return [
            pltpu.VMEM((number * self.rows, self.columns), low_type),
            pltpu.SemaphoreType.DMA((number,)),
        ]


def load_pieces(refs, scratch):
    place_ref, *block_refs = refs
    weight_ref, sem_ref = scratch
    copies = []
    for index, block_ref in enumerate(block_refs):
        rows = block_ref.shape[1]
        for part in range(2):
            number = 2 * index + part
            start = pl.multiple_of(place_ref[number] * rows, rows & -rows)
            copies.append(
                pltpu.make_async_copy(
                    block_ref.at[part], weight_ref.at[pl.ds(start, rows)], sem_ref.at[number]
                )
            )
    for copy in copies:
        copy.start()
    for copy in copies:
        copy.wait()


def halves_body(bit_ref, weight_ref, own_ref, other_ref):
    size = own_ref.shape[1]
    for out_ref, which in ((own_ref, bit_ref[0]), (other_ref, 1 - bit_ref[0])):
        start = pl.multiple_of(which * size, size & -size)
        out_ref[...] = weight_ref[:, pl.ds(start, size)].astype(low_type)


def halves(bit, weight, layer=None):
    rows, columns = weight.shape[-2:]
    step = rows // 5
    if layer is None:
        spec = pl.BlockSpec((step, columns), lambda i: (i, 0))
    else:
        spec = pl.BlockSpec((pl.squeezed, step, columns), lambda i: (layer, i, 0))
    half = pl.BlockSpec((step, columns // 2), lambda i: (i, 0))
    return call(
        halves_body,
        (5,),
        [smem_spec(), spec],
        [half, half],
        [shape((rows, columns // 2), low_type)] * 2,
    )(bit.astype(jnp.int32).reshape(1), weight)


def pack_body(*refs):
    *parts, out_ref = refs
    start = 0
    for part in parts:
        if len(part.shape) == 2:
            out_ref[start] = part[...]
            start += 1
        else:
            out_ref[start : start + part.shape[0]] = part[...]
            start += part.shape[0]


def pack(*parts):
    rows, width = parts[0].shape[-2:]
    step = width // 2
    specs, number = [], 0
    for part in parts:
        if part.ndim == 2:
            specs.append(pl.BlockSpec((rows, step), lambda n: (0, n)))
            number += 1
        else:
            specs.append(pl.BlockSpec((part.shape[0], rows, step), lambda n: (0, 0, n)))
            number += part.shape[0]
    return call(
        pack_body,
        (2,),
        specs,
        pl.BlockSpec((number, rows, step), lambda n: (0, 0, n)),
        shape((number, rows, width), parts[0].dtype),
    )(*parts)


def both_cores(near_ref, far_ref):
    return jnp.concatenate([near_ref[0], far_ref[0]], axis=0)


def project_body(count, x_ref, xc_ref, cos_ref, sin_ref, *refs):
    pieces = refs[:count]
    at_ref, q_ref, kv_ref, g_ref, w_ref, sem_ref = refs[count:]

    @pl.when(pl.program_id(0) == 0)
    def _():
        load_pieces(pieces, (w_ref, sem_ref))
        turned = w_ref[:, 384:].astype(wide_type).T
        g_ref[...] = turned[EDGE - 384 : EDGE - 384 + 2]

    x = both_cores(x_ref, xc_ref).astype(wide_type)
    rows = x.shape[0]
    unit = x * lax.rsqrt(jnp.mean(x * x, axis=-1, keepdims=True) + eps_norm)
    normed = (unit * g_ref[0:1]).astype(low_type)
    at_ref[...] = normed.T
    flat = dot(w_ref[...], normed, 0, 1)
    cos, sin = cos_ref[0], sin_ref[0]

    def rotated(start):
        first = flat[start : start + HALF]
        second = flat[start + HALF : start + HEAD_SIZE]
        return jnp.concatenate(
            [first * cos - second * sin, second * cos + first * sin], axis=0
        ).astype(low_type)

    for head in range(GROUP):
        q_ref[0, :, head * rows : (head + 1) * rows] = rotated(head * HEAD_SIZE)
    kv_ref[0] = jnp.concatenate(
        [rotated(QROWS), flat[QROWS + HEAD_SIZE : EDGE].astype(low_type)], axis=0
    )


def project(near, far, weight, cos, sin):
    tiles, per, width = near.shape
    wide = 2 * per
    return call(
        functools.partial(project_body, weight.count()),
        (tiles,),
        [
            tile_of(1, per, width),
            tile_of(1, per, width),
            tile_of(1, HALF, wide),
            tile_of(1, HALF, wide),
            *weight.specs(),
        ],
        [
            pl.BlockSpec((width, wide), lambda t: (0, t)),
            tile_of(1, HEAD_SIZE, GROUP * wide),
            tile_of(1, BOTH, wide),
            pl.BlockSpec((2, width), lambda t: (0, 0)),
        ],
        [
            shape((width, tiles * wide), low_type),
            shape((tiles, HEAD_SIZE, GROUP * wide), low_type),
            shape((tiles, BOTH, wide), low_type),
            shape((2, width), wide_type),
        ],
        weight.scratch(),
    )(near, far, cos, sin, *weight.values())


def load_keys(kv_refs, kv_ref, sem_ref):
    copies, start = [], 0
    for index, part in enumerate(kv_refs):
        size = part.shape[0]
        copies.append(
            pltpu.make_async_copy(part, kv_ref.at[start : start + size], sem_ref.at[index])
        )
        start += size
    for copy in copies:
        copy.start()
    for copy in copies:
        copy.wait()


def attend_body(count, seen_ref, base_ref, q_ref, pos_ref, start_ref, local_ref, *refs):
    kv_parts, pieces = refs[:4], refs[4 : 4 + count]
    o_ref, ot_ref, lse_ref, near_ref, far_ref = refs[4 + count : 9 + count]
    top_ref, sum_ref, acc_ref, kv_ref, kv_sem, w_ref, sem_ref = refs[9 + count :]
    tile = pl.program_id(0)
    key_tiles = kv_ref.shape[0]

    @pl.when(tile == 0)
    def _():
        load_keys(kv_parts, kv_ref, kv_sem)
        load_pieces(pieces, (w_ref, sem_ref))

    top_ref[...] = jnp.full(top_ref.shape, masked_score, wide_type)
    sum_ref[...] = jnp.zeros(sum_ref.shape, wide_type)
    acc_ref[...] = jnp.zeros(acc_ref.shape, wide_type)

    def step(k, carry):
        @pl.when(seen_ref[tile * key_tiles + k] != 0)
        def _():
            raw = dot(kv_ref[k, :HEAD_SIZE], q_ref[0], 0, 0)
            key_pos = base_ref[k] + local_ref[...]
            allowed = (key_pos <= pos_ref[0]) & (key_pos >= start_ref[0])
            raw = jnp.where(allowed, raw, masked_score)
            top_old = top_ref[...]
            top = jnp.maximum(top_old, jnp.max(raw, axis=0, keepdims=True))
            shrink = jnp.exp2((top_old - top) * EXP_SCALE)
            probs = jnp.where(allowed, jnp.exp2((raw - top) * EXP_SCALE), 0.0)
            sum_ref[...] = sum_ref[...] * shrink + jnp.sum(probs, axis=0, keepdims=True)
            acc_ref[...] = acc_ref[...] * shrink + dot(
                kv_ref[k, HEAD_SIZE:], probs.astype(low_type), 1, 0
            )
            top_ref[...] = top

        return carry

    lax.fori_loop(0, key_tiles, step, 0)
    out = acc_ref[...] / sum_ref[...]
    ot_ref[0] = out
    lse_ref[0] = top_ref[...] * EXP_SCALE + jnp.log2(sum_ref[...])
    rows = out.shape[1] // GROUP
    stacked = jnp.concatenate(
        [out[:, head * rows : (head + 1) * rows] for head in range(GROUP)], axis=0
    )
    attended = stacked.T.astype(low_type)
    o_ref[0] = attended
    branch = dot(attended, w_ref[...], 1, 1)
    near_ref[0] = branch[: rows // 2].astype(low_type)
    far_ref[0] = branch[rows // 2 :].astype(low_type)


def key_scratch(kv):
    number = sum(part.shape[0] for part in kv)
    return [
        pltpu.VMEM((number, *kv[0].shape[1:]), low_type),
        pltpu.SemaphoreType.DMA((len(kv),)),
    ]


def attend(layout, kv, weight):
    seen, base, q, pos, start, local = layout
    tiles, _, columns = q.shape
    wide = kv[0].shape[2]
    width = 2 * len(weight.blocks) * weight.rows
    return call(
        functools.partial(attend_body, weight.count()),
        (tiles,),
        [
            smem_spec(),
            smem_spec(),
            tile_of(1, HEAD_SIZE, columns),
            tile_of(1, 1, columns),
            tile_of(1, 1, columns),
            whole(local),
            *[any_spec()] * 4,
            *weight.specs(),
        ],
        [
            tile_of(1, wide, QROWS),
            tile_of(1, HEAD_SIZE, columns),
            tile_of(1, 1, columns),
            tile_of(1, wide // 2, width),
            tile_of(1, wide // 2, width),
        ],
        [
            shape((tiles, wide, QROWS), low_type),
            shape((tiles, HEAD_SIZE, columns), wide_type),
            shape((tiles, 1, columns), wide_type),
            shape((tiles, wide // 2, width), low_type),
            shape((tiles, wide // 2, width), low_type),
        ],
        [
            pltpu.VMEM((1, columns), wide_type),
            pltpu.VMEM((1, columns), wide_type),
            pltpu.VMEM((HEAD_SIZE, columns), wide_type),
            *key_scratch(kv),
            *weight.scratch(),
        ],
    )(*layout, *kv, *weight.values())


def attend_back_body(
    count, seen_ref, base_ref, q_ref, pos_ref, start_ref, local_ref,
    z_ref, zc_ref, ot_ref, lse_ref, cos_ref, sin_ref, *refs,
):
    kv_parts, pieces = refs[:4], refs[4 : 4 + count]
    dq_ref, *dkv_parts = refs[4 + count : 9 + count]
    acc_ref, dkv_ref, kv_ref, kv_sem, w_ref, sem_ref = refs[9 + count :]
    tile = pl.program_id(0)
    key_tiles = kv_ref.shape[0]

    @pl.when(tile == 0)
    def _():
        load_keys(kv_parts, kv_ref, kv_sem)
        load_pieces(pieces, (w_ref, sem_ref))
        dkv_ref[...] = jnp.zeros(dkv_ref.shape, wide_type)

    rows = q_ref.shape[2] // GROUP
    turned = dot(w_ref[...], both_cores(z_ref, zc_ref), 0, 1).astype(low_type)
    grad_out = jnp.concatenate(
        [turned[head * HEAD_SIZE : (head + 1) * HEAD_SIZE] for head in range(GROUP)], axis=1
    )
    delta = jnp.sum(grad_out.astype(wide_type) * ot_ref[0], axis=0, keepdims=True)
    acc_ref[...] = jnp.zeros(acc_ref.shape, wide_type)

    def step(k, carry):
        @pl.when(seen_ref[tile * key_tiles + k] != 0)
        def _():
            raw = dot(kv_ref[k, :HEAD_SIZE], q_ref[0], 0, 0)
            key_pos = base_ref[k] + local_ref[...]
            allowed = (key_pos <= pos_ref[0]) & (key_pos >= start_ref[0])
            probs = jnp.where(allowed, jnp.exp2(raw * EXP_SCALE - lse_ref[0]), 0.0)
            grad_probs = dot(kv_ref[k, HEAD_SIZE:], grad_out, 0, 0)
            grad_scores = (probs * (grad_probs - delta)).astype(low_type)
            acc_ref[...] += dot(kv_ref[k, :HEAD_SIZE], grad_scores, 1, 0)
            dkv_ref[k, :HEAD_SIZE] += dot(q_ref[0], grad_scores, 1, 1) * SCALE
            dkv_ref[k, HEAD_SIZE:] += dot(grad_out, probs.astype(low_type), 1, 1)

        return carry

    lax.fori_loop(0, key_tiles, step, 0)
    cos, sin = cos_ref[0], sin_ref[0]
    for head in range(GROUP):
        part = acc_ref[:, head * rows : (head + 1) * rows] * SCALE
        first, second = part[:HALF], part[HALF:]
        dq_ref[0, head * HEAD_SIZE : (head + 1) * HEAD_SIZE] = jnp.concatenate(
            [first * cos + second * sin, second * cos - first * sin], axis=0
        ).astype(low_type)

    @pl.when(tile == pl.num_programs(0) - 1)
    def _():
        start = 0
        for part in dkv_parts:
            size = part.shape[0]
            part[...] = dkv_ref[start : start + size].astype(part.dtype)
            start += size


def attend_back(layout, kv, weight, near, far, out_turned, lse, cos, sin):
    seen, base, q, pos, start, local = layout
    tiles, _, columns = q.shape
    wide = kv[0].shape[2]
    width = near.shape[2]
    kinds = (wide_type, low_type, low_type, low_type)
    held = key_scratch(kv)
    return call(
        functools.partial(attend_back_body, weight.count()),
        (tiles,),
        [
            smem_spec(),
            smem_spec(),
            tile_of(1, HEAD_SIZE, columns),
            tile_of(1, 1, columns),
            tile_of(1, 1, columns),
            whole(local),
            tile_of(1, wide // 2, width),
            tile_of(1, wide // 2, width),
            tile_of(1, HEAD_SIZE, columns),
            tile_of(1, 1, columns),
            tile_of(1, HALF, wide),
            tile_of(1, HALF, wide),
            *[any_spec()] * 4,
            *weight.specs(),
        ],
        [tile_of(1, QROWS, wide)] + [whole(part) for part in kv],
        [shape((tiles, QROWS, wide), low_type)]
        + [shape(part.shape, kind) for part, kind in zip(kv, kinds)],
        [
            pltpu.VMEM((HEAD_SIZE, columns), wide_type),
            pltpu.VMEM(held[0].shape, wide_type),
            *held,
            *weight.scratch(),
        ],
    )(*layout, near, far, out_turned, lse, cos, sin, *kv, *weight.values())


def finish_body(late_ref, dq_ref, own_ref, y_ref, a_ref, b_ref, cos_ref, sin_ref, out_ref):
    late = (pl.program_id(0) // 2 == late_ref[0]).astype(wide_type)
    total = own_ref[0] + y_ref[0].astype(wide_type)
    total = total + late * (a_ref[0].astype(wide_type) + b_ref[0].astype(wide_type))
    cos, sin = cos_ref[0], sin_ref[0]
    first, second = total[:HALF], total[HALF:HEAD_SIZE]
    turned = jnp.concatenate(
        [
            dq_ref[0].astype(wide_type),
            first * cos + second * sin,
            second * cos - first * sin,
            total[HEAD_SIZE:],
            jnp.zeros((2, total.shape[1]), wide_type),
        ],
        axis=0,
    )
    out_ref[0] = turned.T.astype(low_type)


def finish(late, dq, own, from_y, from_a, from_b, cos, sin):
    tiles, _, wide = dq.shape
    return call(
        finish_body,
        (tiles,),
        [
            smem_spec(),
            tile_of(1, QROWS, wide),
            tile_of(1, BOTH, wide),
            tile_of(1, BOTH, wide),
            pl.BlockSpec((1, BOTH, wide), lambda t: (t % 2, 0, 0)),
            pl.BlockSpec((1, BOTH, wide), lambda t: (t % 2, 0, 0)),
            tile_of(1, HALF, wide),
            tile_of(1, HALF, wide),
        ],
        tile_of(1, wide, EDGE + 2),
        shape((tiles, wide, EDGE + 2), low_type),
    )(late, dq, own, from_y, from_a, from_b, cos, sin)


def turn_body(near_ref, far_ref, out_ref):
    out_ref[...] = both_cores(near_ref, far_ref).T


def turn(near, far):
    tiles, per, width = near.shape
    return call(
        turn_body,
        (tiles,),
        [tile_of(1, per, width), tile_of(1, per, width)],
        pl.BlockSpec((width, 2 * per), lambda t: (0, t)),
        shape((width, 2 * per * tiles), low_type),
    )(near, far)


def ffn_body(count, near_ref, far_ref, *refs):
    gate_pieces, up_pieces = refs[:count], refs[count : 2 * count]
    at_ref, hid_ref, one_ref, two_ref, gate_ref, gate_sem, up_ref, up_sem = refs[2 * count :]

    @pl.when(pl.program_id(0) == 0)
    def _():
        load_pieces(gate_pieces, (gate_ref, gate_sem))
        load_pieces(up_pieces, (up_ref, up_sem))

    normed = both_cores(near_ref, far_ref)
    at_ref[...] = normed.T
    gate = dot(normed, gate_ref[...], 1, 0)
    upward = dot(normed, up_ref[...], 1, 0)
    sigma = 1.0 / (1.0 + jnp.exp(-gate))
    passed = gate * sigma
    hid_ref[0] = (passed * upward).astype(low_type)
    one_ref[0] = upward * sigma * (1.0 + gate * (1.0 - sigma))
    two_ref[0] = passed


def ffn(near, far, gate_weight, up_weight):
    tiles, per, width = near.shape
    wide = 2 * per
    hidden = gate_weight.columns
    return call(
        functools.partial(ffn_body, gate_weight.count()),
        (tiles,),
        [
            tile_of(1, per, width),
            tile_of(1, per, width),
            *gate_weight.specs(),
            *up_weight.specs(),
        ],
        [
            pl.BlockSpec((width, wide), lambda t: (0, t)),
            tile_of(1, wide, hidden),
            tile_of(1, wide, hidden),
            tile_of(1, wide, hidden),
        ],
        [
            shape((width, tiles * wide), low_type),
            shape((tiles, wide, hidden), low_type),
            shape((tiles, wide, hidden), wide_type),
            shape((tiles, wide, hidden), wide_type),
        ],
        gate_weight.scratch() + up_weight.scratch(),
    )(near, far, *gate_weight.values(), *up_weight.values())


def ffn_back_body(count, near_ref, far_ref, one_ref, two_ref, *refs):
    dgate_ref, dup_ref, w_ref, sem_ref = refs[count:]

    @pl.when(pl.program_id(0) == 0)
    def _():
        load_pieces(refs[:count], (w_ref, sem_ref))

    grad_hidden = dot(both_cores(near_ref, far_ref), w_ref[...], 1, 0)
    dgate_ref[0] = (grad_hidden * one_ref[0]).astype(low_type)
    dup_ref[0] = (grad_hidden * two_ref[0]).astype(low_type)


def ffn_back(near, far, weight, one, two):
    tiles, per, width = near.shape
    wide = 2 * per
    hidden = weight.columns
    part = tile_of(1, wide, hidden)
    return call(
        functools.partial(ffn_back_body, weight.count()),
        (tiles,),
        [tile_of(1, per, width), tile_of(1, per, width), part, part, *weight.specs()],
        [part, part],
        [shape((tiles, wide, hidden), low_type)] * 2,
        weight.scratch(),
    )(near, far, one, two, *weight.values())


def put_blocks(total, out_refs):
    for index, out_ref in enumerate(out_refs):
        out_ref[...] = total[index].astype(out_ref.dtype)


def block_outputs(per, width, step):
    spec = pl.BlockSpec((per, step), lambda n: (0, n))
    kinds = (wide_type, low_type, low_type, low_type)
    return [spec] * 4, [shape((per, width), kind) for kind in kinds]


def combine_body(near_ref, got_ref, *out_refs):
    put_blocks(near_ref[...].astype(wide_type) + got_ref[...].astype(wide_type), out_refs)


def combine(near, got):
    blocks, per, width = near.shape
    step = width // 2
    spec = pl.BlockSpec((blocks, per, step), lambda n: (0, 0, n))
    out_specs, out_shape = block_outputs(per, width, step)
    return call(combine_body, (width // step,), [spec, spec], out_specs, out_shape)(near, got)


def branch_body(lefts, count, with_got, *refs):
    left_refs, refs = refs[:lefts], refs[lefts:]
    pieces, refs = [refs[i * count : (i + 1) * count] for i in range(lefts)], refs[lefts * count :]
    got_ref, refs = (refs[0], refs[1:]) if with_got else (None, refs)
    outs, scratch = refs[: -2 * lefts], refs[-2 * lefts :]
    step = outs[0].shape[-1]

    @pl.when(pl.program_id(0) == 0)
    def _():
        for index in range(lefts):
            load_pieces(pieces[index], scratch[2 * index : 2 * index + 2])

    start = pl.multiple_of(pl.program_id(0) * step, step)
    total = None
    for index in range(lefts):
        left = left_refs[index][...]
        rows = left.shape[0] * left.shape[2]
        weight = scratch[2 * index][pl.ds(start, step), :]
        term = dot(left.reshape(rows, left.shape[3]), weight, 1, 1)
        total = term if total is None else total + term
    total = total.reshape(4, total.shape[0] // 4, step)
    if got_ref is None:
        outs[0][...] = total.astype(low_type)
    else:
        put_blocks(total + got_ref[...].astype(wide_type), outs)


def branch(pairs, core, got=None):
    step = 640
    specs, lefts, weight_specs, weights, scratch = [], [], [], [], []
    for left, weight in pairs:
        tiles, wide, inner = left.shape
        lefts.append(left.reshape(tiles, 2, wide // 2, inner))
        specs.append(pl.BlockSpec((tiles, 1, wide // 2, inner), lambda n: (0, core, 0, 0)))
        weight_specs += weight.specs()
        weights += weight.values()
        scratch += weight.scratch()
    width = 2 * len(weight.blocks) * weight.rows
    per = wide // 2
    block = pl.BlockSpec((tiles, per, step), lambda n: (0, 0, n))
    if got is None:
        out_specs, out_shape = [block], [shape((tiles, per, width), low_type)]
    else:
        out_specs, out_shape = block_outputs(per, width, step)
    outs = call(
        functools.partial(branch_body, len(pairs), weight.count(), got is not None),
        (width // step,),
        specs + weight_specs + ([] if got is None else [block]),
        out_specs,
        out_shape,
        scratch,
    )(*lefts, *weights, *([] if got is None else [got]))
    return outs[0] if got is None else outs


def weight_body(count, index_ref, first_ref, second_ref, right_ref, *refs):
    left = jnp.concatenate([first_ref[0], second_ref[0]], axis=0)
    total = dot(left, right_ref[...], 1, 0)
    rows = total.shape[0] // 2
    for part in range(2):
        block = total[part * rows : (part + 1) * rows]
        for position in range(count):
            block = block + refs[2 * position + part][0].astype(wide_type)
        refs[-1][part] = block.astype(refs[-1].dtype)


def weight_rows(turned, right, places, addends, kind):
    tokens = turned.shape[1]
    columns = right.shape[-1]
    blocks = lax.axis_size("dp")
    rows = turned.shape[0] // blocks
    number = len(places)
    flat = [jnp.asarray(p, jnp.int32) for p in places]

    def named(offset, part, last):
        return pl.BlockSpec(
            (1, rows, last), lambda i, index: (index[offset + 2 * i + part], 0, 0)
        )

    specs = [
        named(0, 0, tokens),
        named(0, 1, tokens),
        pl.BlockSpec((tokens, columns), lambda i, index: (0, 0)),
    ]
    given = []
    for position, (array, where) in enumerate(addends):
        flat += [jnp.asarray(p, jnp.int32) for p in where]
        for part in range(2):
            specs.append(named((position + 1) * number, part, columns))
            given.append(array)
    left = turned.reshape(blocks, rows, tokens)
    return pl.pallas_call(
        functools.partial(weight_body, len(addends)),
        grid_spec=pltpu.PrefetchScalarGridSpec(
            num_scalar_prefetch=1,
            grid=(number // 2,),
            in_specs=specs,
            out_specs=pl.BlockSpec((2, rows, columns), lambda i, index: (i, 0, 0)),
        ),
        out_shape=shape((number, rows, columns), kind),
        compiler_params=pltpu.CompilerParams(vmem_limit_bytes=VMEM_LIMIT),
        cost_estimate=pl.CostEstimate(flops=10**10, bytes_accessed=0, transcendentals=0),
    )(jnp.stack(flat), left, left, right.reshape(tokens, columns), *given)


def share_first(turned, right):
    _, _, y, _, _ = bits()
    ring = lax.axis_size("dp") // 4
    places = [4 * g + 2 * b + (1 - y) for g in range(ring) for b in range(2)]
    return weight_rows(turned, right, places, [], low_type)


def share_term(turned, right, got, step, travel=None):
    h, l, y, _, _ = bits()
    ring = lax.axis_size("dp") // 4
    group = (h - 1 - step) % ring
    last = step == ring - 1
    order = [l, 1 - l] if last else [0, 1]
    places = [4 * group + 2 * b + y for b in order]
    addends = [(got, [2 * group + b for b in order])]
    if travel is not None:
        addends.append((travel, order))
    return weight_rows(turned, right, places, addends, wide_type if last else low_type)


def share_rest(turned, right, got, term):
    ring = lax.axis_size("dp") // 4
    travel = hop_ring(term)
    for step in range(1, ring - 1):
        travel = hop_ring(share_term(turned, right, got, step, travel))
    return travel


def share_third(turned, right, got, travel):
    ring = lax.axis_size("dp") // 4
    own = share_term(turned, right, got, ring - 1, travel)
    return own[0], own[1].astype(low_type), jnp.sum(jnp.square(own))


def adamw(param, grad, first, second):
    first_new = beta_first * first + (1.0 - beta_first) * grad
    second_new = beta_second * second + (1.0 - beta_second) * grad * grad
    first_hat = first_new / (1.0 - beta_first**STEP)
    second_hat = second_new / (1.0 - beta_second**STEP)
    change = -learn_rate * (first_hat / (jnp.sqrt(second_hat) + adam_eps) + weight_decay * param)
    return (first_new, second_new, change)


def on_device(
    tokens,
    upstream,
    offsets,
    query_weight,
    keyval_weight,
    output_weight,
    gateup_weight,
    down_weight,
    norm_gains,
    first_query,
    first_keyval,
    first_output,
    first_gateup,
    first_down,
    first_gains,
    second_query,
    second_keyval,
    second_output,
    second_gateup,
    second_down,
    second_gains,
):
    h, l, y, xbit, cbit = bits()
    pin = Windows(norm_gains)
    ring = lax.axis_size("dp") // 4
    block_rows = offsets.shape[0]
    per, width = tokens.shape
    wide = 2 * per

    def split(bit, arrays, more=()):
        lower, upper = [], []
        for array in arrays:
            half = array.shape[-1] // 2
            lower.append(array[:, :half].astype(low_type))
            upper.append(array[:, half:].astype(low_type))
        lower = jnp.concatenate([*lower, *more], axis=1)
        upper = jnp.concatenate([*upper, *more], axis=1)
        return choose(bit, lower, upper), choose(bit, upper, lower)

    def paired(own, other):
        return ordered(l, own[None], other[None], 0)

    places = jnp.stack(
        [
            4 * ((h - step) % ring) + 2 * b + (y ^ flip)
            for step in range(ring)
            for flip in range(2)
            for b in range(2)
        ]
    ).astype(jnp.int32)

    def legs(pair, pair_y, rings, rings_y):
        blocks = [pair, pair_y]
        for block, block_y in zip(rings, rings_y):
            blocks += [block, block_y]
        return Pieces(blocks, places)

    def arrived(own, *others):
        for other in others:
            own = own + other.astype(wide_type)
        return own

    def onward(block, corner):
        return (block.astype(wide_type) + corner.astype(wide_type)).astype(low_type)

    gain_columns = norm_gains.astype(low_type).T
    q_own, q_other = split(
        l, [query_weight, keyval_weight[0], keyval_weight[1]], [gain_columns]
    )
    o_own, o_other = split(l, [output_weight])
    q_other, o_other, other_offsets = hop_low(q_other), hop_low(o_other), hop_low(offsets)

    q_other, o_other, other_offsets, bit, own_rows = pin(
        q_other, o_other, other_offsets, l, tokens
    )
    q_pair = paired(q_own, q_other)
    q_ring, q_y = hop_ring(q_pair), hop_y(q_pair)
    tx, tz = hop_x(own_rows), hop_low(own_rows)
    o_pair = paired(o_own, o_other)
    g_own, g_other = halves(bit, gateup_weight, 0)

    def relative(own):
        four = own.reshape(2, 2, per)
        four = choose(xbit, four, four[::-1])
        return choose(cbit, four, four[:, ::-1])

    offset_tiles = jnp.concatenate([relative(offsets), relative(other_offsets)], axis=0)
    offset_tiles = offset_tiles.reshape(4, wide)
    lane = jnp.arange(wide, dtype=jnp.int32)
    local = choose(cbit, lane, lane ^ per)
    mine = jnp.arange(4, dtype=jnp.int32)

    def bases(group_h, group_y, low_bits, x_bits):
        block = 4 * group_h + 2 * low_bits + group_y
        return block * block_rows + x_bits * wide

    low_bits, x_bits = l ^ (mine // 2), xbit ^ (mine % 2)
    own_base = bases(h, y, low_bits, x_bits)
    one = jnp.ones((2,), jnp.int32)
    key_base = jnp.concatenate(
        [
            own_base,
            bases(h, 1 - y, low_bits, x_bits),
            bases(h - 1, y, one, x_bits[:2]),
            bases(h - 1, 1 - y, one, x_bits[:2]),
        ]
    ).astype(jnp.int32)
    query_pos = own_base[:, None] + local[None, :]
    doc_start = query_pos - offset_tiles
    seen = (
        (key_base[None, :] <= own_base[:, None] + wide - 1)
        & (key_base[None, :] + wide - 1 >= jnp.min(doc_start, axis=1, keepdims=True))
    ).astype(jnp.int32).reshape(-1)
    spread = lambda a: jnp.tile(a, (1, GROUP)).reshape(4, 1, GROUP * wide)
    query_lanes, start_lanes = spread(query_pos), spread(doc_start)
    local_column = local.reshape(wide, 1)
    freqs = rope_base ** (-(jnp.arange(HALF).astype(wide_type) * 2.0 / HEAD_SIZE))
    angle = freqs[None, :, None] * offset_tiles.astype(wide_type)[:, None, :]
    cos, sin = jnp.cos(angle), jnp.sin(angle)

    tx, tz, g_other, bit = pin(tx, tz, g_other, bit)
    tf = hop_x(tz)
    g_other = hop_low(g_other)
    u_own, u_other = halves(bit, gateup_weight, 1)

    q_ring, q_y, o_pair = pin.apart(q_ring, q_y, o_pair)
    q_far = rest_of_ring(q_ring)
    q_far_y = [hop_y(block) for block in q_far]
    o_ring = hop_ring(o_pair)

    tf, bit, up_own = pin(tf, bit, upstream)
    near = pack(own_rows, tx, tz, tf)
    far = hop_core(near)
    d_own, d_other = halves(bit, down_weight)

    far, g_other, u_other, up_own, d_other, o_pair, *q_far_y = pin(
        far, g_other, u_other, up_own, d_other, o_pair, *q_far_y
    )
    u_other = hop_low(u_other)
    g_pair = paired(g_own, g_other)

    qkv_full = legs(q_pair, q_y, q_far, q_far_y)
    turned_one, q_turned, kv_own, gains = project(near, far, qkv_full, cos, sin)
    d_other, o_y, ux = hop_low(d_other), hop_y(o_pair), hop_x(up_own)

    kv_own, o_y, o_ring, u_other, ux = pin(kv_own, o_y, o_ring, u_other, ux)
    late = choose(l, kv_own[2:], kv_own[:2])
    kv_a, kv_b, kv_y = to_next(late, 0), to_next(late, 1), hop_y(kv_own)
    o_far = rest_of_ring(o_ring)
    o_far_y = [hop_y(block) for block in o_far]
    u_pair = paired(u_own, u_other)

    kv_y, kv_a, kv_b, g_pair, up_own, d_other, *o_far_y = pin(
        kv_y, kv_a, kv_b, g_pair, up_own, d_other, *o_far_y
    )
    g_ring, g_y = hop_ring(g_pair), hop_y(g_pair)
    uz = hop_low(up_own)
    d_pair = paired(d_own, d_other)

    (q_turned,) = pin.apart(q_turned)
    output_full = legs(o_pair, o_y, o_far, o_far_y)
    layout = (seen, key_base, q_turned, query_lanes, start_lanes, local_column)
    kv = (kv_own, kv_y, kv_a, kv_b)
    attended, out_turned, lse, branch_near, branch_far = attend(layout, kv, output_full)
    z_got = hop_core(branch_far)

    z_got, g_y, u_pair = pin(z_got, g_y, u_pair)
    z_own, z_x, z_low, z_corner = combine(branch_near, z_got)
    zc = hop_x(z_corner)
    u_y = hop_y(u_pair)
    inputs = tokens.astype(wide_type)
    inverse_one = lax.rsqrt(jnp.mean(inputs * inputs, axis=-1, keepdims=True) + eps_norm)
    unit_one = inputs * inverse_one

    zc, z_x, g_ring, u_pair, uz = pin(zc, z_x, g_ring, u_pair, uz)
    zz, zx = hop_low(onward(z_low, zc)), hop_x(z_x)
    g_far = rest_of_ring(g_ring)
    u_ring = hop_ring(u_pair)

    zx, zz, u_y, uz = pin(zx, zz, u_y, uz)
    g_far_y = [hop_y(block) for block in g_far]
    middle = inputs + arrived(z_own, zx, zz)
    inverse_two = lax.rsqrt(jnp.mean(middle * middle, axis=-1, keepdims=True) + eps_norm)
    unit_two = middle * inverse_two
    own_two = (unit_two * gains[1]).astype(low_type)
    az, ax = hop_low(own_two), hop_x(own_two)

    ax, az, u_ring, d_pair, uz, *g_far_y = pin(ax, az, u_ring, d_pair, uz, *g_far_y)
    af = hop_x(az)
    u_far = rest_of_ring(u_ring)
    u_far_y = [hop_y(block) for block in u_far]
    d_ring = hop_ring(d_pair)
    gate_full = legs(g_pair, g_y, g_far, g_far_y)

    af, d_pair, uz = pin(af, d_pair, uz)
    near_two = pack(own_two, ax, az, af)
    far_two = hop_core(near_two)
    d_y, uf = hop_y(d_pair), hop_x(uz)

    far_two, *u_far_y = pin(far_two, *u_far_y)
    up_full = legs(u_pair, u_y, u_far, u_far_y)
    turned_two, hidden, first_factor, second_factor = ffn(
        near_two, far_two, gate_full, up_full
    )

    d_ring, d_y, uf, hidden = pin(d_ring, d_y, uf, hidden)
    d_far = rest_of_ring(d_ring)
    d_far_y = [hop_y(block) for block in d_far]
    near_up = pack(up_own, ux, uz, uf)
    far_up = hop_core(near_up)
    turned_up = turn(near_up, far_up)
    down_first = share_first(turned_up, hidden)

    down_first, hidden, *d_far_y = pin(down_first, hidden, *d_far_y)
    down_sent = hop_y(down_first)
    down_full = legs(d_pair, d_y, d_far, d_far_y)
    grad_gate, grad_up = ffn_back(near_up, far_up, down_full, first_factor, second_factor)
    ffn_pairs = [(grad_gate, gate_full), (grad_up, up_full)]
    s_got = hop_core(branch(ffn_pairs, 1))
    gate_first = share_first(turned_two, grad_gate)

    s_got, grad_up, gate_first = pin(s_got, grad_up, gate_first)
    s_own, s_x, s_low, s_corner = branch(ffn_pairs, 0, s_got)
    sc = hop_x(s_corner)

    sc, s_x, grad_up = pin(sc, s_x, grad_up)
    sz, sx = hop_low(onward(s_low, sc)), hop_x(s_x)
    up_first = share_first(turned_two, grad_up)

    sx, sz, down_got, gate_first, up_first, hidden = pin(
        sx, sz, down_sent, gate_first, up_first, hidden
    )
    grad_normed_two = arrived(s_own, sx, sz)
    gain_two = jnp.sum(grad_normed_two * unit_two, axis=0)
    grad_middle = upstream.astype(wide_type) + norm_back(
        grad_normed_two, unit_two, inverse_two, gains[1]
    )
    own_three = grad_middle.astype(low_type)
    bz, bx = hop_low(own_three), hop_x(own_three)
    gate_sent = hop_y(gate_first)
    down_travel = share_rest(
        turned_up, hidden, down_got, share_term(turned_up, hidden, down_got, 0)
    )

    bx, bz = pin(bx, bz)
    bf = hop_x(bz)

    (bf,) = pin(bf)
    near_three = pack(own_three, bx, bz, bf)
    far_three = hop_core(near_three)

    (far_three,) = pin(far_three)
    dq_turned, dkv_own, dkv_y, dkv_a, dkv_b = attend_back(
        layout, kv, output_full, near_three, far_three, out_turned, lse, cos, sin
    )

    dkv_y, dkv_a, dkv_b, gate_got, down_travel, up_first = pin(
        dkv_y, dkv_a, dkv_b, gate_sent, down_travel, up_first
    )
    dkv_a, dkv_b, dkv_y = to_previous(dkv_a, 0), to_previous(dkv_b, 1), hop_y(dkv_y)
    up_sent = hop_y(up_first)
    gate_term = share_term(turned_two, grad_gate, gate_got, 0)

    dkv_y, dkv_a, dkv_b, gate_term, near_three = pin(
        dkv_y, dkv_a, dkv_b, gate_term, near_three
    )
    gate_travel = share_rest(turned_two, grad_gate, gate_got, gate_term)

    dq_turned, near_three = pin.apart(dq_turned, near_three)
    dqkv = finish(
        (1 - l).astype(jnp.int32).reshape(1), dq_turned, dkv_own, dkv_y, dkv_a, dkv_b, cos, sin
    )
    attn_pairs = [(dqkv, qkv_full)]
    r_got = hop_core(branch(attn_pairs, 1))
    turned_three = turn(near_three, far_three)
    output_first = share_first(turned_three, attended)

    r_got, dqkv, output_first = pin(r_got, dqkv, output_first)
    output_sent = hop_y(output_first)
    r_own, r_x, r_low, r_corner = branch([(dqkv, qkv_full)], 0, r_got)
    rc = hop_x(r_corner)
    qkv_first = share_first(turned_one, dqkv)

    rc, r_x, up_got, qkv_first, down_travel = pin(rc, r_x, up_sent, qkv_first, down_travel)
    rz, rx = hop_low(onward(r_low, rc)), hop_x(r_x)
    up_travel = share_rest(
        turned_two, grad_up, up_got, share_term(turned_two, grad_up, up_got, 0)
    )

    down_travel, qkv_first = pin.apart(down_travel, qkv_first)
    down_mine, down_theirs, down_square = share_third(turned_up, hidden, down_got, down_travel)

    rx, rz, gate_travel, output_got, down_theirs, qkv_first = pin(
        rx, rz, gate_travel, output_sent, down_theirs, qkv_first
    )
    qkv_sent = hop_y(qkv_first)
    down_other = hop_low(down_theirs)

    hidden, gate_travel, output_got, rx = pin.apart(hidden, gate_travel, output_got, rx)
    f_got = hop_core(branch([(hidden, down_full)], 1))
    output_term = share_term(turned_three, attended, output_got, 0)
    grad_normed_one = arrived(r_own, rx, rz)
    gain_one = jnp.sum(grad_normed_one * unit_one, axis=0)
    grad_tokens = grad_middle + norm_back(grad_normed_one, unit_one, inverse_one, gains[0])
    gate_mine, gate_theirs, gate_square = share_third(
        turned_two, grad_gate, gate_got, gate_travel
    )
    gate_other = hop_low(gate_theirs)

    f_got, qkv_got, output_term, down_other = pin(f_got, qkv_sent, output_term, down_other)
    output_travel = share_rest(turned_three, attended, output_got, output_term)
    qkv_travel = share_rest(
        turned_one, dqkv, qkv_got, share_term(turned_one, dqkv, qkv_got, 0)
    )

    up_travel, gate_other = pin.apart(up_travel, gate_other)
    up_mine, up_theirs, up_square = share_third(turned_two, grad_up, up_got, up_travel)

    up_theirs, hidden, f_got = pin(up_theirs, hidden, f_got)
    up_other = hop_low(up_theirs)

    hidden, f_got = pin.apart(hidden, f_got)
    f_own, f_x, f_low, f_corner = branch([(hidden, down_full)], 0, f_got)
    fc = hop_x(f_corner)

    fc, f_x, gain_one = pin(fc, f_x, gain_one)
    fz, fx = hop_low(onward(f_low, fc)), hop_x(f_x)

    (output_travel,) = pin.apart(output_travel)
    output_mine, output_theirs, output_square = share_third(
        turned_three, attended, output_got, output_travel
    )
    output_other = hop_low(output_theirs)
    square_row = jnp.full(
        (1, width), (down_square + gate_square + up_square + output_square) / width
    )
    sums = jnp.concatenate([gain_one[None], gain_two[None], square_row], axis=0)

    qkv_travel, sums, up_other = pin(qkv_travel, sums, up_other)
    qkv_mine, qkv_theirs, qkv_square = share_third(turned_one, dqkv, qkv_got, qkv_travel)
    qkv_other = hop_low(qkv_theirs)
    last_row = (jnp.arange(3) == 2).astype(wide_type)[:, None]
    totals = sums + last_row * (qkv_square / width)
    totals = totals + hop_core(totals)

    totals = sum_rest(totals + hop_x(totals))
    totals, qkv_other, output_other, fx, fz = pin(totals, qkv_other, output_other, fx, fz)
    block_out = (middle + arrived(f_own, fx, fz)).astype(low_type)
    totals = totals + hop_low(totals)
    gain_total = totals[:2]
    grad_norm = jnp.sqrt(totals[2, 0] * width + jnp.sum(gain_total * gain_total))
    def joined(mine, other, start, stop):
        return ordered(l, mine[:, start:stop], other[:, start:stop].astype(wide_type), 1)

    edge_one = QROWS + HEAD_SIZE
    hidden_part = down_mine.shape[1]
    grad_query = joined(qkv_mine, qkv_other, 0, QROWS)
    grad_keyval = jnp.stack(
        [
            joined(qkv_mine, qkv_other, QROWS, edge_one).T,
            joined(qkv_mine, qkv_other, edge_one, EDGE).T,
        ]
    )
    grad_output = joined(output_mine, output_other, 0, QROWS)
    grad_gateup = jnp.stack(
        [
            joined(gate_mine, gate_other, 0, hidden_part),
            joined(up_mine, up_other, 0, hidden_part),
        ]
    )
    grad_down = joined(down_mine, down_other, 0, hidden_part)
    rows_owned = query_weight.shape[0]
    grad_gains = lax.dynamic_slice_in_dim(
        gain_total, lax.axis_index("dp") * rows_owned, rows_owned, 1
    )
    clipping_bound = math.sqrt(
        MODEL_WIDTH
        * (2 * QUERY_HEAD_COUNT * HEAD_SIZE + 2 * KEY_VALUE_HEADS * HEAD_SIZE + 3 * HIDDEN_UNITS)
        + 2 * MODEL_WIDTH
    )
    clip = jnp.minimum(1.0, clipping_bound / (grad_norm + 1e-06))
    params = (query_weight, keyval_weight, output_weight, gateup_weight, down_weight, pin.held)
    firsts = (first_query, first_keyval, first_output, first_gateup, first_down, first_gains)
    seconds = (second_query, second_keyval, second_output, second_gateup, second_down, second_gains)
    grads = (grad_query, grad_keyval, grad_output, grad_gateup, grad_down, grad_gains)
    turned = lambda a: jnp.swapaxes(a, 1, 2)
    states = [
        adamw(params[index], grads[index] * clip, firsts[index], seconds[index])
        if index != 1
        else tuple(
            turned(a)
            for a in adamw(
                turned(params[1]), grads[1] * clip, turned(firsts[1]), turned(seconds[1])
            )
        )
        for index in range(6)
    ]
    grads = (grads[0], turned(grads[1]), *grads[2:])
    return (
        block_out,
        grad_tokens,
        grad_norm,
        *grads,
        *[state[0] for state in states],
        *[state[1] for state in states],
        *[state[2] for state in states],
    )


def solution(mesh):
    weights = (
        P("dp", "mp"),
        P(None, "dp", "mp"),
        P("dp", "mp"),
        P(None, "dp", "mp"),
        P("dp", "mp"),
        P(None, "dp"),
    )
    rows = P(("dp", "mp"), None)
    return jax.shard_map(
        on_device,
        mesh=mesh,
        in_specs=(rows, rows, P("dp"), *weights, *weights, *weights),
        out_specs=(rows, rows, P(), *weights, *weights, *weights, *weights),
        check_vma=False,
    )
```
